256 devices in a mesh: phase: 4 (over x), dp: 64 (over z, y, core).
Axes of the slice: x: 4, y: 4, z: 8, core: 2. Of those that a mesh axis runs over, the one named last changes fastest.
Arguments:
- query_states: bfloat16 [4096, 2048], P('dp', 'phase'), may hold values from -25 to 25
- doc_states: bfloat16 [8192, 4096], P('dp', 'phase'), may hold values from -8.7 to 8.7
- query_proj: bfloat16 [2048, 2048], P('phase'), may hold values from -0.75 to 2.75
- doc_proj: bfloat16 [4096, 2048], P('phase'), may hold values from -0.75 to 2.75
- document_requests: int32 [64, 64, 16], P('dp'), may hold values from 0 to 127, as said below
- slot_valid: int32 [64, 1024], P('dp'), may hold values from 0 to 1
- neg_slot: int32 [4096, 7], P('dp'), may hold values from 0 to 1023, as said below
- query_weight: float32 [4096], P('dp'), may hold values from 0.5 to 2
Outputs:
- loss_rows: float32 [4096], P('dp')
- grad_query: bfloat16 [4096, 2048], P('dp', 'phase')
- grad_doc: bfloat16 [8192, 4096], P('dp', 'phase')
The draws below stay inside these ranges and needn't reach their ends.
Inputs may be any that keep to these rules, and one draw needn't show every extreme that they name: `document_requests`: rows may repeat within and across slots. `neg_slot`: slots index the rows received by the query's own dp index.
All inputs are finite; a program needn't handle non-finite values.
Results may differ from the reference program's by a relative error of at most 0.0067.
Values may be sent and summed in bfloat16 or wider, within the bound.
No kernel may reach another device: no remote copies, remote signals or barrier semaphores. Data moves between devices by JAX's collectives and lax.ppermute only.
A program may use at most 128 MiB of HBM per device.

```python
import math
import jax
import jax.numpy as jnp
from jax import lax

DQ = 2048
DD = 4096
EMBED = 2048
QDEV = 64
DDEV = 128
CAP = 16
HARD_NEGATIVES = 7
SLOTS_PER_INDEX = 1024
QUERY_TOTAL = 4096
DOCS = 8192
N_DP = 64


negative_gain = 0.6


query_jitter = 0.3


diagonal_gain = 2.0


def integer_tables(key):
    request_table = jax.random.randint(jax.random.fold_in(key, 11), (N_DP, N_DP, CAP), 0, DDEV, dtype=jnp.int32)
    validity_lookup = jax.random.randint(jax.random.fold_in(key, 12), (N_DP, SLOTS_PER_INDEX), 0, 2, dtype=jnp.int32)
    negative_lookup = jax.random.randint(jax.random.fold_in(key, 13), (QUERY_TOTAL, HARD_NEGATIVES), 0, SLOTS_PER_INDEX, dtype=jnp.int32)
    return (request_table, validity_lookup, negative_lookup)


def unit_noise(key, shape, bound):
    return jax.random.truncated_normal(key, -bound, bound, shape, jnp.float32)


def document_kernel(key):
    return unit_noise(jax.random.fold_in(key, 21), (DOCS, DD), 6.0)


def draw_document_requests(key, part):
    return integer_tables(key)[0]


def draw_slot_valid(key, part):
    return integer_tables(key)[1]


def draw_neg_slot(key, part):
    return integer_tables(key)[2]


def draw_doc_states(key, part):
    states = document_kernel(key)
    return states.astype(jnp.bfloat16)


def draw_query_states(key, part):
    request_table, validity_lookup, negative_lookup = integer_tables(key)
    leading = document_kernel(key)[:, :EMBED]
    query_ids = jnp.arange(QUERY_TOTAL, dtype=jnp.int32)
    owner_ids = query_ids // QDEV
    positive_ids = owner_ids * DDEV + query_ids % QDEV
    mixed = leading[positive_ids]
    for entry in range(HARD_NEGATIVES):
        slot_ids = negative_lookup[:, entry]
        source_ids = slot_ids // CAP
        column_ids = slot_ids % CAP
        local_rows = request_table[source_ids, owner_ids, column_ids]
        mixed = mixed + negative_gain * leading[source_ids * DDEV + local_rows]
    mixed = mixed * math.sqrt(0.9 / (1.0 + HARD_NEGATIVES * negative_gain * negative_gain))
    padded = jnp.concatenate([mixed, jnp.zeros((QUERY_TOTAL, DQ - EMBED), jnp.float32)], axis=1)
    noise = unit_noise(jax.random.fold_in(key, 31), (QUERY_TOTAL, DQ), 6.0)
    states = padded + query_jitter * noise
    return states.astype(jnp.bfloat16)


def draw_query_proj(key, part):
    noise = unit_noise(jax.random.fold_in(key, 41), (DQ, EMBED), 4.0)
    weights = diagonal_gain * jnp.eye(DQ, EMBED, dtype=jnp.float32) + noise / math.sqrt(DQ)
    return weights.astype(jnp.bfloat16)


def draw_doc_proj(key, part):
    noise = unit_noise(jax.random.fold_in(key, 42), (DD, EMBED), 4.0)
    weights = diagonal_gain * jnp.eye(DD, EMBED, dtype=jnp.float32) + noise / math.sqrt(DD)
    return weights.astype(jnp.bfloat16)


def block_levels(stream_key, dims, pieces, least, top_value):
    def one(dim, parts):
        draws = jax.random.uniform(jax.random.fold_in(jax.random.fold_in(stream_key, 6), dim), (parts,), jnp.float32, least / len(pieces), top_value / len(pieces))
        return jnp.repeat(jnp.exp(draws), dims[dim] // parts).reshape((-1,) + (1,) * (len(dims) - dim - 1))

    gain = one(*pieces[0])
    for cut in pieces[1:]:
        gain = gain * one(*cut)
    return gain


def setup_inputs(seed: int = 0) -> dict:
    key_list = jax.random.split(jax.random.key(seed), 9)
    query_states = draw_query_states(jax.random.fold_in(key_list[8], 71), 0)
    doc_states = draw_doc_states(jax.random.fold_in(key_list[8], 71), 0)
    query_proj = draw_query_proj(jax.random.fold_in(key_list[8], 71), 0)
    doc_proj = draw_doc_proj(jax.random.fold_in(key_list[8], 71), 0)
    document_requests = draw_document_requests(jax.random.fold_in(key_list[8], 71), 0)
    slot_valid = draw_slot_valid(jax.random.fold_in(key_list[8], 71), 0)
    neg_slot = draw_neg_slot(jax.random.fold_in(key_list[8], 71), 0)
    query_weight = jnp.clip(jnp.exp(math.log(2.0) - 1.3862944 * jax.random.uniform(key_list[7], (QUERY_TOTAL,), jnp.float32) ** block_levels(key_list[7], (QUERY_TOTAL,), ((0, 64),), -0.2, 0.2)), 0.5, 2.0)
    return {"query_states": query_states, "doc_states": doc_states, "query_proj": query_proj, "doc_proj": doc_proj, "document_requests": document_requests, "slot_valid": slot_valid, "neg_slot": neg_slot, "query_weight": query_weight}


logit_scale = 20.0
epsilon = 1e-06

def unit_rows(raw):
    scale_rows = lax.rsqrt(lax.optimization_barrier(jnp.sum(raw * raw, axis=1, keepdims=True)) + epsilon)
    return (raw * scale_rows, scale_rows)

def softmax_terms(inner_scores, slot_scores, negatives, validity, weights):
    count_slots = slot_scores.shape[1]
    hard_scores = jnp.take_along_axis(slot_scores, negatives, axis=1)
    kept_mask = jnp.take(validity, negatives).astype(jnp.float32)
    inner_exp = jnp.exp(inner_scores)
    hard_exp = jnp.exp(hard_scores) * kept_mask
    row_total = lax.optimization_barrier(jnp.sum(inner_exp, axis=1)) + lax.optimization_barrier(jnp.sum(hard_exp, axis=1))
    row_ids = lax.broadcasted_iota(jnp.int32, inner_scores.shape, 0)
    col_ids = lax.broadcasted_iota(jnp.int32, inner_scores.shape, 1)
    is_positive = (row_ids == col_ids).astype(jnp.float32)
    positive = lax.optimization_barrier(jnp.sum(inner_scores * is_positive, axis=1))
    loss_rows = jnp.log(row_total) - positive
    factor = (logit_scale * weights / row_total)[:, None]
    grad_inner = factor * inner_exp - (logit_scale * weights)[:, None] * is_positive
    hard_grad = factor * hard_exp
    slot_ids = lax.broadcasted_iota(jnp.int32, (1, 1, count_slots), 2)
    slot_onehot = (negatives[:, :, None] == slot_ids).astype(jnp.float32)
    grad_slots = lax.optimization_barrier(jnp.sum(slot_onehot * hard_grad[:, :, None], axis=1))
    return (loss_rows, grad_inner.astype(jnp.bfloat16), grad_slots.astype(jnp.bfloat16))

def reference(query_states, doc_states, query_proj, doc_proj, document_requests, slot_valid, neg_slot, query_weight):
    q_raw = jnp.dot(query_states, query_proj, preferred_element_type=jnp.float32)
    d_raw = jnp.dot(doc_states, doc_proj, preferred_element_type=jnp.float32)
    q_unit, q_scale = unit_rows(q_raw)
    d_unit, d_scale = unit_rows(d_raw)
    q_low = q_unit.astype(jnp.bfloat16)
    d_low = d_unit.astype(jnp.bfloat16)
    width = q_raw.shape[1]
    q_shards = q_low.reshape(N_DP, QDEV, width)
    d_shards = d_low.reshape(N_DP, DDEV, width)
    neg_shards = neg_slot.reshape(N_DP, QDEV, HARD_NEGATIVES)
    weight_shards = query_weight.reshape(N_DP, QDEV)
    source_ids = jnp.arange(N_DP, dtype=jnp.int32)[:, None]

    def per_owner(carry_grad, inputs):
        owner_index, q_local, d_local, negatives, validity, weights = inputs
        requested = jnp.take(document_requests, owner_index, axis=1)
        received = d_shards[source_ids, requested].reshape(N_DP * CAP, width)
        inner_scores = logit_scale * jnp.dot(q_local, d_local.T, preferred_element_type=jnp.float32)
        slot_scores = logit_scale * jnp.dot(q_local, received.T, preferred_element_type=jnp.float32)
        loss_rows, grad_inner, grad_slots = softmax_terms(inner_scores, slot_scores, negatives, validity, weights)
        grad_unit = jnp.dot(grad_inner, d_local, preferred_element_type=jnp.float32) + jnp.dot(grad_slots, received, preferred_element_type=jnp.float32)
        grad_local = jnp.dot(grad_inner.T, q_local, preferred_element_type=jnp.float32)
        grad_received = jnp.dot(grad_slots.T, q_local, preferred_element_type=jnp.float32).reshape(N_DP, CAP, width)
        carry_grad = carry_grad.at[source_ids, requested].add(grad_received)
        return (carry_grad, (loss_rows, grad_unit, grad_local))
    start = jnp.zeros((N_DP, DDEV, width), jnp.float32)
    owners = jnp.arange(N_DP, dtype=jnp.int32)
    hard_total, (loss_rows, grad_unit, grad_local) = lax.scan(per_owner, start, (owners, q_shards, d_shards, neg_shards, slot_valid, weight_shards))
    g_query = grad_unit.reshape(QUERY_TOTAL, width)
    g_docs = grad_local.reshape(DOCS, width) + hard_total.reshape(DOCS, width)
    u_query = (q_scale * (g_query - q_unit * lax.optimization_barrier(jnp.sum(q_unit * g_query, axis=1, keepdims=True)))).astype(jnp.bfloat16)
    u_docs = (d_scale * (g_docs - d_unit * lax.optimization_barrier(jnp.sum(d_unit * g_docs, axis=1, keepdims=True)))).astype(jnp.bfloat16)
    grad_query = jnp.dot(u_query, query_proj.T, preferred_element_type=jnp.float32).astype(jnp.bfloat16)
    grad_doc = jnp.dot(u_docs, doc_proj.T, preferred_element_type=jnp.float32).astype(jnp.bfloat16)
    return (loss_rows.reshape(QUERY_TOTAL), grad_query, grad_doc)
```

```python
import jax
import jax.numpy as jnp
from jax import lax
from jax.experimental import pallas as pl
from jax.experimental.pallas import tpu as pltpu
from jax.sharding import PartitionSpec as P

scale20 = 20.0
epsilon = 1e-06
f32 = jnp.float32
bf16 = jnp.bfloat16
NT = (((1,), (1,)), ((), ()))
TN = (((0,), (0,)), ((), ()))
N_PHASE = 4


def dot(a, b, dims=(((1,), (0,)), ((), ()))):
    return lax.dot_general(a, b, dims, preferred_element_type=f32)


def params():
    return pltpu.CompilerParams(vmem_limit_bytes=48 * 1024 * 1024)


def call(body, outs, *args):
    return pl.pallas_call(
        body,
        out_shape=[jax.ShapeDtypeStruct(s, t) for s, t in outs],
        compiler_params=params(),
    )(*args)


def iota(shape, dim):
    return lax.broadcasted_iota(jnp.int32, shape, dim)


def split_bf16(x):
    hi = x.astype(bf16)
    return hi, (x - hi.astype(f32)).astype(bf16)


def project(x, w, k):
    rows, depth = x.shape
    cols = w.shape[1] // N_PHASE

    def body(k_ref, x_ref, w_ref, own_ref, *send_refs):
        y = dot(x_ref[...], w_ref[...])
        step = pl.program_id(0)

        @pl.when(step == 0)
        def _():
            own_ref[...] = y

        for s in range(1, N_PHASE):

            @pl.when(step == s)
            def _():
                send_refs[s - 1][...] = y.astype(bf16)

    whole = pl.BlockSpec((rows, cols), lambda s, k_ref: (0, 0))
    return pl.pallas_call(
        body,
        grid_spec=pltpu.PrefetchScalarGridSpec(
            num_scalar_prefetch=1,
            grid=(N_PHASE,),
            in_specs=[
                pl.BlockSpec((rows, depth), lambda s, k_ref: (0, 0)),
                pl.BlockSpec((depth, cols), lambda s, k_ref: (0, lax.rem(k_ref[0] + s, N_PHASE))),
            ],
            out_specs=[whole] * N_PHASE,
        ),
        out_shape=[jax.ShapeDtypeStruct((rows, cols), f32)]
        + [jax.ShapeDtypeStruct((rows, cols), bf16)] * (N_PHASE - 1),
        compiler_params=params(),
    )(k, x, w)


def project_back(blocks, w, k):
    rows, cols = blocks[0].shape
    depth = w.shape[0]

    def body(k_ref, *refs):
        block_refs, w_ref, out_ref, acc_ref = refs[:N_PHASE], refs[N_PHASE], refs[N_PHASE + 1], refs[N_PHASE + 2]
        step = pl.program_id(0)

        @pl.when(step == 0)
        def _():
            acc_ref[...] = dot(block_refs[0][...], w_ref[...], NT)

        for s in range(1, N_PHASE):

            @pl.when(step == s)
            def _():
                acc_ref[...] += dot(block_refs[s][...], w_ref[...], NT)

        @pl.when(step == N_PHASE - 1)
        def _():
            out_ref[...] = acc_ref[...].astype(bf16)

    whole = pl.BlockSpec((rows, cols), lambda s, k_ref: (0, 0))
    return pl.pallas_call(
        body,
        grid_spec=pltpu.PrefetchScalarGridSpec(
            num_scalar_prefetch=1,
            grid=(N_PHASE,),
            in_specs=[whole] * N_PHASE
            + [pl.BlockSpec((depth, cols), lambda s, k_ref: (0, lax.rem(k_ref[0] + s, N_PHASE)))],
            out_specs=pl.BlockSpec((rows, depth), lambda s, k_ref: (0, 0)),
            scratch_shapes=[pltpu.VMEM((rows, depth), f32)],
        ),
        out_shape=jax.ShapeDtypeStruct((rows, depth), bf16),
        compiler_params=params(),
    )(k, *blocks, w)


def shift_sends(blocks):
    return [
        lax.ppermute(b, "phase", [(i, (i + s) % N_PHASE) for i in range(N_PHASE)])
        for s, b in enumerate(blocks, start=1)
    ]


def gather_blocks(x):
    return [x] + [
        lax.ppermute(x, "phase", [((i + s) % N_PHASE, i) for i in range(N_PHASE)]) for s in range(1, N_PHASE)
    ]


def sum_refs(refs):
    total = refs[0][...].astype(f32)
    for r in refs[1:]:
        total = total + r[...].astype(f32)
    return total


def sum_queries(own, a, b, c, total_ref, low_ref):
    total = sum_refs((own, a, b, c))
    total_ref[...] = total
    low_ref[...] = total.astype(bf16)


def sum_docs(own, a, b, c, request_ref, total_ref, rows_ref):
    total = sum_refs((own, a, b, c))
    total_ref[...] = total
    slots = rows_ref.shape[0]
    onehot = (iota((total.shape[0], slots), 0) == request_ref[...]).astype(f32).astype(bf16)
    rows_ref[...] = dot(onehot, total.astype(bf16), TN).astype(bf16)


def ones_row_sums(x):
    hi, lo = split_bf16(x)
    ones = jnp.ones((8, x.shape[1]), bf16)
    return dot(ones, hi, NT) + dot(ones, lo, NT)


def inner_partials(q_ref, d_ref, out_ref):
    q = q_ref[...]
    d = d_ref[...]
    q2 = jnp.concatenate([q, q], axis=0)
    docs = d.shape[0]
    out_ref[0:docs, :] = dot(d.astype(bf16), q2.astype(bf16), NT)
    out_ref[docs : docs + 8, :] = ones_row_sums(q2 * q2)
    out_ref[docs + 8 : docs + 16, :] = ones_row_sums(d * d)


def hard_partials(rows_ref, q_ref, neg_ref, out_ref):
    rows = rows_ref[...]
    q = q_ref[...]
    scores = dot(rows, jnp.concatenate([q, q], axis=0), NT)
    wide = rows.astype(f32)
    square = wide * wide
    lanes = scores.shape[1]
    folded = square[:, 0:lanes]
    for s in range(lanes, square.shape[1], lanes):
        folded = folded + square[:, s : s + lanes]
    hi, lo = split_bf16(folded)
    ones = jnp.ones((lanes, lanes), bf16)
    squares = dot(hi, ones) + dot(lo, ones)
    slot = iota(scores.shape, 0)
    for j in range(8):
        hit = slot == neg_ref[j : j + 1, :]
        out_ref[j : j + 1, :] = jnp.sum(jnp.where(hit, scores, 0.0), axis=0, keepdims=True)
        out_ref[8 + j : 9 + j, :] = jnp.sum(jnp.where(hit, squares, 0.0), axis=0, keepdims=True)


def softmax_terms(*refs):
    inner_refs, hard_refs = refs[0:4], refs[4:8]
    small_ref, neg_ref, coef_ref, local_ref, grad_ref, row_ref, col_ref = refs[8:]
    sums = sum_refs(inner_refs)
    picks = sum_refs(hard_refs)
    docs = grad_ref.shape[0]
    q_scale = lax.rsqrt(sums[docs : docs + 1, :] + epsilon)
    d_scale_row = lax.rsqrt(sums[docs + 8 : docs + 9, :] + epsilon)
    row = iota((docs, 128), 0)
    lane = iota((docs, 128), 1)
    d_scale = jnp.sum(jnp.where(row == lane, d_scale_row, 0.0), axis=1, keepdims=True)
    inner = scale20 * (sums[0:docs, :] * q_scale * d_scale)
    hard_scale = lax.rsqrt(picks[8:16, :] + epsilon)
    hard = scale20 * (picks[0:8, :] * q_scale * hard_scale)
    valid = small_ref[0:8, :]
    weight = scale20 * small_ref[8:9, :]
    hard_exp = jnp.exp(hard) * valid
    inner_exp = jnp.exp(inner)
    total = jnp.sum(inner_exp, axis=0, keepdims=True) + jnp.sum(hard_exp, axis=0, keepdims=True)
    own = row == lax.bitwise_and(lane, 63)
    positive = jnp.sum(jnp.where(own, inner, 0.0), axis=0, keepdims=True)
    factor = weight / total
    grad = (factor * inner_exp - jnp.where(own, weight, 0.0)).astype(bf16)
    grad_ref[...] = grad
    grad = grad.astype(f32)
    hard_grad = factor * hard_exp
    hard_dot = hard_grad * hard * (1.0 / scale20)
    products = grad * inner * (1.0 / scale20)
    row_ref[...] = jnp.zeros_like(row_ref)
    row_ref[0:1, :] = jnp.log(total) - positive
    row_ref[1:2, :] = q_scale
    row_ref[2:3, :] = jnp.sum(products, axis=0, keepdims=True) + jnp.sum(hard_dot, axis=0, keepdims=True)
    doc_dot = jnp.sum(jnp.where(lane < 64, products, 0.0), axis=1, keepdims=True)
    col_ref[...] = jnp.where(lane == 0, d_scale, doc_dot)
    sent = jnp.where(iota((8, 128), 1) < 64, hard_grad * q_scale, hard_dot)
    kept = hard_grad * hard_scale
    slots = coef_ref.shape[0]
    slot = iota((slots, 128), 0)
    coef = jnp.zeros((slots, 128), f32)
    local = jnp.zeros((slots, 128), f32)
    for j in range(7):
        hit = slot == neg_ref[j : j + 1, :]
        coef = coef + jnp.where(hit, sent[j : j + 1, :], 0.0)
        local = local + jnp.where(hit, kept[j : j + 1, :], 0.0)
    coef_ref[...] = coef.astype(bf16)
    local_ref[...] = local.astype(bf16)


def local_grads(grad_ref, local_ref, rows_ref, d_ref, q_ref, row_ref, col_ref, u_ref, g_ref):
    queries = q_ref.shape[0]
    d_low = (d_ref[...] * col_ref[:, 0:1]).astype(bf16)
    eye = iota((queries, 128), 0) == iota((queries, 128), 1)
    q_scale = jnp.sum(jnp.where(eye, row_ref[1:2, :], 0.0), axis=1, keepdims=True)
    q_dot = jnp.sum(jnp.where(eye, row_ref[2:3, :], 0.0), axis=1, keepdims=True)
    q_unit = q_ref[...] * q_scale
    q_low = q_unit.astype(bf16)
    grad = grad_ref[...]
    g = dot(grad, d_low, TN) + dot(local_ref[...], rows_ref[...], TN)
    u_ref[...] = (q_scale * (g[0:queries, :] - q_unit * q_dot)).astype(bf16)
    half = jnp.where(iota(grad.shape, 1) < 64, grad.astype(f32), 0.0).astype(bf16)
    g_ref[...] = dot(half, jnp.concatenate([q_low, q_low], axis=0))


def doc_grads(coef, requests, q_all, g_local, d_total, col):
    docs, cols = g_local.shape
    steps = 8
    slots = coef.shape[0] // steps
    queries = q_all.shape[0] // steps

    def body(coef_ref, request_ref, q_ref, g_ref, d_ref, col_ref, u_ref, acc_ref, dot_ref):
        step = pl.program_id(0)

        @pl.when(step == 0)
        def _():
            acc_ref[...] = g_ref[...]
            dot_ref[...] = jnp.zeros_like(dot_ref)

        onehot = (iota((docs, slots), 0) == request_ref[...]).astype(f32).astype(bf16)
        block = coef_ref[...]
        dot_ref[...] += dot(onehot, block)
        wide = block.astype(f32)
        lane = iota((slots, 128), 1)
        twice = jnp.where(lane < 64, wide, pltpu.roll(wide, 64, 1))
        source = lax.shift_right_logical(iota((slots, 128), 0), 4)
        part = lax.shift_right_logical(lane, 6)
        spread = jnp.concatenate(
            [jnp.where(source == part + 2 * s, twice, 0.0).astype(bf16) for s in range(queries // 128)], axis=1
        )
        mixed = dot(onehot, spread).astype(bf16)
        acc_ref[...] += dot(mixed, q_ref[...])

        @pl.when(step == steps - 1)
        def _():
            d_scale = col_ref[:, 0:1]
            far = jnp.where(iota((docs, 128), 1) < 64, 0.0, dot_ref[...])
            total = col_ref[:, 1:2] + jnp.sum(far, axis=1, keepdims=True)
            d_unit = d_ref[...] * d_scale
            u_ref[...] = (d_scale * (acc_ref[...] - d_unit * total)).astype(bf16)

    const = lambda shape: pl.BlockSpec(shape, lambda s: (0, 0))
    return pl.pallas_call(
        body,
        grid=(steps,),
        in_specs=[
            pl.BlockSpec((slots, 128), lambda s: (s, 0)),
            pl.BlockSpec((1, slots), lambda s: (0, s)),
            pl.BlockSpec((queries, cols), lambda s: (s, 0)),
            const((docs, cols)),
            const((docs, cols)),
            const((docs, 128)),
        ],
        out_specs=const((docs, cols)),
        out_shape=jax.ShapeDtypeStruct((docs, cols), bf16),
        scratch_shapes=[pltpu.VMEM((docs, cols), f32), pltpu.VMEM((docs, 128), f32)],
        compiler_params=params(),
    )(coef, requests, q_all, g_local, d_total, col)


def local(
    query_states,
    doc_states,
    query_proj,
    doc_proj,
    document_requests,
    slot_valid,
    neg_slot,
    query_weight,
):
    k = lax.axis_index("phase").astype(jnp.int32).reshape(1)
    queries, docs = query_states.shape[0], doc_states.shape[0]
    cols = query_proj.shape[1] // N_PHASE
    n_dp, cap = document_requests.shape[1:]
    slots = n_dp * cap

    negatives = neg_slot.T
    requests = document_requests.reshape(1, slots)
    neg_rows = jnp.pad(jnp.concatenate([negatives, negatives], axis=1), ((0, 1), (0, 0)), constant_values=-1)

    q_own, *q_send = project(query_states, query_proj, k)
    q_parts = shift_sends(q_send)
    d_own, *d_send = project(doc_states, doc_proj, k)
    d_parts = shift_sends(d_send)

    q_total, q_low = call(sum_queries, [((queries, cols), f32), ((queries, cols), bf16)], q_own, *q_parts)
    q_all = lax.all_gather(q_low, "dp", axis=0, tiled=True)

    d_total, outgoing = call(
        sum_docs, [((docs, cols), f32), ((slots, cols), bf16)], d_own, *d_parts, requests
    )
    received = lax.all_to_all(
        outgoing.reshape(n_dp, cap, cols), "dp", split_axis=0, concat_axis=0, tiled=True
    ).reshape(slots, cols)

    (inner,) = call(inner_partials, [((docs + 16, 128), f32)], q_total, d_total)
    inner_all = gather_blocks(inner)
    valid = jnp.take(slot_valid[0], negatives).astype(f32)
    weight = query_weight[None, :]
    small = jnp.pad(
        jnp.concatenate([valid, jnp.zeros_like(weight), weight], axis=0), ((0, 7), (0, 0))
    )
    small = jnp.concatenate([small, small], axis=1)

    (hard,) = call(hard_partials, [((16, 128), f32)], received, q_low, neg_rows)
    hard_all = gather_blocks(hard)
    coef, kept, grad, rows, columns = call(
        softmax_terms,
        [((slots, 128), bf16), ((slots, 128), bf16), ((docs, 128), bf16), ((8, 128), f32), ((docs, 128), f32)],
        *inner_all,
        *hard_all,
        small,
        neg_rows,
    )
    arrived = lax.all_to_all(
        coef.reshape(n_dp, cap, 128), "dp", split_axis=0, concat_axis=0, tiled=True
    ).reshape(slots, 128)

    u_query, g_local = call(
        local_grads,
        [((queries, cols), bf16), ((docs, cols), f32)],
        grad,
        kept,
        received,
        d_total,
        q_total,
        rows,
        columns,
    )
    grad_query = project_back(gather_blocks(u_query), query_proj, k)

    u_docs = doc_grads(arrived, requests, q_all, g_local, d_total, columns)
    grad_doc = project_back(gather_blocks(u_docs), doc_proj, k)
    return (rows[0, :queries], grad_query, grad_doc)


def solution(mesh):
    in_specs = (
        P("dp", "phase"),
        P("dp", "phase"),
        P("phase", None),
        P("phase", None),
        P("dp", None, None),
        P("dp", None),
        P("dp", None),
        P("dp"),
    )
    out_specs = (P("dp"), P("dp", "phase"), P("dp", "phase"))
    return jax.shard_map(local, mesh=mesh, in_specs=in_specs, out_specs=out_specs, check_vma=False)
```

```python
import jax
import jax.numpy as jnp
from jax import lax
from jax.experimental import pallas as pl
from jax.experimental.pallas import tpu as pltpu
from jax.sharding import PartitionSpec as P

scale20 = 20.0
epsilon = 1e-06
f32 = jnp.float32
bf16 = jnp.bfloat16
NT = (((1,), (1,)), ((), ()))
TN = (((0,), (0,)), ((), ()))
N_PHASE = 4
cost = pl.CostEstimate(flops=10**9, bytes_accessed=10**5, transcendentals=0)


def dot(a, b, dims=(((1,), (0,)), ((), ()))):
    return lax.dot_general(a, b, dims, preferred_element_type=f32)


def params():
    return pltpu.CompilerParams(vmem_limit_bytes=48 * 1024 * 1024)


def call(body, outs, *args):
    return pl.pallas_call(
        body,
        out_shape=[jax.ShapeDtypeStruct(s, t) for s, t in outs],
        compiler_params=params(),
        cost_estimate=cost,
    )(*args)


def iota(shape, dim):
    return lax.broadcasted_iota(jnp.int32, shape, dim)


def split_bf16(x):
    hi = x.astype(bf16)
    return hi, (x - hi.astype(f32)).astype(bf16)


def project(x, w, k):
    rows, depth = x.shape
    cols = w.shape[1] // N_PHASE

    def body(k_ref, x_ref, w_ref, own_ref, *refs):
        send_refs, buf_ref, sem_ref = refs[: N_PHASE - 1], refs[N_PHASE - 1], refs[N_PHASE]

        def copy(s):
            start = pl.multiple_of(lax.rem(k_ref[0] + s, N_PHASE) * cols, cols)
            return pltpu.make_async_copy(w_ref.at[:, pl.ds(start, cols)], buf_ref.at[s], sem_ref.at[s])

        for s in range(N_PHASE):
            copy(s).start()
        for s in range(N_PHASE):
            copy(s).wait()
            y = dot(x_ref[...], buf_ref[s])
            if s == 0:
                own_ref[...] = y
            else:
                send_refs[s - 1][...] = y.astype(bf16)

    vmem = pl.BlockSpec(memory_space=pltpu.VMEM)
    return pl.pallas_call(
        body,
        in_specs=[pl.BlockSpec(memory_space=pltpu.SMEM), vmem, pl.BlockSpec(memory_space=pltpu.HBM)],
        out_specs=[vmem] * N_PHASE,
        out_shape=[jax.ShapeDtypeStruct((rows, cols), f32)]
        + [jax.ShapeDtypeStruct((rows, cols), bf16)] * (N_PHASE - 1),
        scratch_shapes=[pltpu.VMEM((N_PHASE, depth, cols), bf16), pltpu.SemaphoreType.DMA((N_PHASE,))],
        compiler_params=params(),
        cost_estimate=cost,
    )(k, x, w)


def project_back_own(block, w, k):
    rows, cols = block.shape
    depth = w.shape[0]

    def body(k_ref, u_ref, w_ref, acc_ref):
        acc_ref[...] = dot(u_ref[...], w_ref[...], NT)

    return pl.pallas_call(
        body,
        grid_spec=pltpu.PrefetchScalarGridSpec(
            num_scalar_prefetch=1,
            grid=(1,),
            in_specs=[
                pl.BlockSpec((rows, cols), lambda s, k_ref: (0, 0)),
                pl.BlockSpec((depth, cols), lambda s, k_ref: (0, k_ref[0])),
            ],
            out_specs=pl.BlockSpec((rows, depth), lambda s, k_ref: (0, 0)),
        ),
        out_shape=jax.ShapeDtypeStruct((rows, depth), f32),
        compiler_params=params(),
        cost_estimate=cost,
    )(k, block, w)


def project_back_rest(acc, blocks, w, k):
    rows, cols = blocks[0].shape
    depth = w.shape[0]

    def body(k_ref, in_ref, *refs):
        block_refs, w_ref, out_ref, acc_ref = refs[:3], refs[3], refs[4], refs[5]
        step = pl.program_id(0)
        for s in range(N_PHASE - 1):

            @pl.when(step == s)
            def _():
                before = in_ref if s == 0 else acc_ref
                total = before[...] + dot(block_refs[s][...], w_ref[...], NT)
                if s == N_PHASE - 2:
                    out_ref[...] = total.astype(bf16)
                else:
                    acc_ref[...] = total

    const = lambda shape: pl.BlockSpec(shape, lambda s, k_ref: (0, 0))
    return pl.pallas_call(
        body,
        grid_spec=pltpu.PrefetchScalarGridSpec(
            num_scalar_prefetch=1,
            grid=(N_PHASE - 1,),
            in_specs=[const((rows, depth))]
            + [const((rows, cols))] * (N_PHASE - 1)
            + [pl.BlockSpec((depth, cols), lambda s, k_ref: (0, lax.rem(k_ref[0] + s + 1, N_PHASE)))],
            out_specs=const((rows, depth)),
            scratch_shapes=[pltpu.VMEM((rows, depth), f32)],
        ),
        out_shape=jax.ShapeDtypeStruct((rows, depth), bf16),
        compiler_params=params(),
        cost_estimate=cost,
    )(k, acc, *blocks, w)


def project_back(u, w, k):
    return project_back_rest(project_back_own(u, w, k), gather_blocks(u)[1:], w, k)


def shift_sends(blocks):
    return [
        lax.ppermute(b, "phase", [(i, (i + s) % N_PHASE) for i in range(N_PHASE)])
        for s, b in enumerate(blocks, start=1)
    ]


def gather_blocks(x):
    return [x] + [
        lax.ppermute(x, "phase", [((i + s) % N_PHASE, i) for i in range(N_PHASE)]) for s in range(1, N_PHASE)
    ]


def sum_refs(refs):
    total = refs[0][...].astype(f32)
    for r in refs[1:]:
        total = total + r[...].astype(f32)
    return total


def sum_queries(own, a, b, c, total_ref, low_ref):
    total = sum_refs((own, a, b, c))
    total_ref[...] = total
    low_ref[...] = total.astype(bf16)


def sum_docs(own, a, b, c, request_ref, total_ref, rows_ref):
    total = sum_refs((own, a, b, c))
    total_ref[...] = total
    slots = rows_ref.shape[0]
    onehot = (iota((total.shape[0], slots), 0) == request_ref[...]).astype(f32).astype(bf16)
    rows_ref[...] = dot(onehot, total.astype(bf16), TN).astype(bf16)


def ones_row_sums(x):
    hi, lo = split_bf16(x)
    ones = jnp.ones((8, x.shape[1]), bf16)
    return dot(ones, hi, NT) + dot(ones, lo, NT)


def inner_partials(q_ref, d_ref, out_ref):
    q = q_ref[...]
    d = d_ref[...]
    q2 = jnp.concatenate([q, q], axis=0)
    docs = d.shape[0]
    out_ref[0:docs, :] = dot(d.astype(bf16), q2.astype(bf16), NT)
    out_ref[docs : docs + 8, :] = ones_row_sums(q2 * q2)
    out_ref[docs + 8 : docs + 16, :] = ones_row_sums(d * d)


def hard_partials(rows_ref, q_ref, neg_ref, out_ref):
    rows = rows_ref[...]
    q = q_ref[...]
    scores = dot(rows, jnp.concatenate([q, q], axis=0), NT)
    wide = rows.astype(f32)
    square = wide * wide
    lanes = scores.shape[1]
    folded = square[:, 0:lanes]
    for s in range(lanes, square.shape[1], lanes):
        folded = folded + square[:, s : s + lanes]
    hi, lo = split_bf16(folded)
    ones = jnp.ones((lanes, lanes), bf16)
    squares = dot(hi, ones) + dot(lo, ones)
    slot = iota(scores.shape, 0)
    for j in range(8):
        hit = slot == neg_ref[j : j + 1, :]
        out_ref[j : j + 1, :] = jnp.sum(jnp.where(hit, scores, 0.0), axis=0, keepdims=True)
        out_ref[8 + j : 9 + j, :] = jnp.sum(jnp.where(hit, squares, 0.0), axis=0, keepdims=True)


def softmax_terms(*refs):
    inner_refs, hard_refs = refs[0:4], refs[4:8]
    small_ref, neg_ref, rows_ref, d_ref, q_ref, out_ref, u_ref, g_ref, loss_ref = refs[8:]
    sums = sum_refs(inner_refs)
    picks = sum_refs(hard_refs)
    docs, queries = d_ref.shape[0], q_ref.shape[0]
    q_scale = lax.rsqrt(sums[docs : docs + 1, :] + epsilon)
    d_scale_row = lax.rsqrt(sums[docs + 8 : docs + 9, :] + epsilon)
    row = iota((docs, 128), 0)
    lane = iota((docs, 128), 1)
    d_scale = jnp.sum(jnp.where(row == lane, d_scale_row, 0.0), axis=1, keepdims=True)
    inner = scale20 * (sums[0:docs, :] * q_scale * d_scale)
    hard_scale = lax.rsqrt(picks[8:16, :] + epsilon)
    hard = scale20 * (picks[0:8, :] * q_scale * hard_scale)
    valid = small_ref[0:8, :]
    weight = scale20 * small_ref[8:9, :]
    hard_exp = jnp.exp(hard) * valid
    inner_exp = jnp.exp(inner)
    total = jnp.sum(inner_exp, axis=0, keepdims=True) + jnp.sum(hard_exp, axis=0, keepdims=True)
    own = row == lax.bitwise_and(lane, 63)
    positive = jnp.sum(jnp.where(own, inner, 0.0), axis=0, keepdims=True)
    loss_ref[...] = jnp.broadcast_to(jnp.log(total) - positive, loss_ref.shape)
    factor = weight / total
    grad = (factor * inner_exp - jnp.where(own, weight, 0.0)).astype(bf16)
    wide_grad = grad.astype(f32)
    hard_grad = factor * hard_exp
    hard_dot = hard_grad * hard * (1.0 / scale20)
    products = wide_grad * inner * (1.0 / scale20)
    q_dot = jnp.sum(products, axis=0, keepdims=True) + jnp.sum(hard_dot, axis=0, keepdims=True)
    d_dot = jnp.sum(jnp.where(lane < 64, products, 0.0), axis=1, keepdims=True)
    sent = hard_scale * jnp.where(iota((8, 128), 1) < 64, hard_grad, hard_dot * hard_scale)
    slots = out_ref.shape[0]
    slot = iota((slots, 128), 0)
    coef = jnp.zeros((slots, 128), f32)
    for j in range(7):
        coef = coef + jnp.where(slot == neg_ref[j : j + 1, :], sent[j : j + 1, :], 0.0)
    coef = coef.astype(bf16)

    eye = iota((queries, 128), 0) == iota((queries, 128), 1)
    q_scale_col = jnp.sum(jnp.where(eye, q_scale, 0.0), axis=1, keepdims=True)
    q_dot_col = jnp.sum(jnp.where(eye, q_dot, 0.0), axis=1, keepdims=True)
    q_unit = q_ref[...] * q_scale_col
    q_low = jnp.concatenate([q_unit.astype(bf16), jnp.zeros(q_ref.shape, bf16)], axis=0)
    second = (iota((128, 128), 0) >= 64).astype(f32).astype(bf16)
    along = dot(coef, second)
    mixed = dot(coef, q_low)
    for s in range(0, mixed.shape[1], 128):
        part = rows_ref[:, s : s + 128].astype(f32)
        out_ref[:, s : s + 128] = (mixed[:, s : s + 128] - along * part).astype(bf16)

    d_unit = d_ref[...] * d_scale
    g_query = dot(grad, d_unit.astype(bf16), TN) + dot(coef, rows_ref[...], TN)
    u_ref[...] = (q_scale_col * (g_query[0:queries, :] - q_unit * q_dot_col)).astype(bf16)
    g_ref[...] = d_scale * (dot(grad, q_low) - d_unit * d_dot)


def doc_grads(rows_ref, request_ref, g_ref, u_ref):
    docs, slots = g_ref.shape[0], rows_ref.shape[0]
    onehot = (iota((docs, slots), 0) == request_ref[...]).astype(f32).astype(bf16)
    u_ref[...] = (g_ref[...] + dot(onehot, rows_ref[...])).astype(bf16)


def local(
    query_states,
    doc_states,
    query_proj,
    doc_proj,
    document_requests,
    slot_valid,
    neg_slot,
    query_weight,
):
    k = lax.axis_index("phase").astype(jnp.int32).reshape(1)
    queries, docs = query_states.shape[0], doc_states.shape[0]
    cols = query_proj.shape[1] // N_PHASE
    n_dp, cap = document_requests.shape[1:]
    slots = n_dp * cap

    negatives = neg_slot.T
    requests = document_requests.reshape(1, slots)
    neg_rows = jnp.pad(jnp.concatenate([negatives, negatives], axis=1), ((0, 1), (0, 0)), constant_values=-1)

    d_own, *d_send = project(doc_states, doc_proj, k)
    d_parts = shift_sends(d_send)
    d_total, outgoing = call(
        sum_docs, [((docs, cols), f32), ((slots, cols), bf16)], d_own, *d_parts, requests
    )
    outgoing, query_states = lax.optimization_barrier((outgoing, query_states))
    received = lax.all_to_all(
        outgoing.reshape(n_dp, cap, cols), "dp", split_axis=0, concat_axis=0, tiled=True
    ).reshape(slots, cols)

    q_own, *q_send = project(query_states, query_proj, k)
    q_parts = shift_sends(q_send)
    q_total, q_low = call(sum_queries, [((queries, cols), f32), ((queries, cols), bf16)], q_own, *q_parts)
    (inner,) = call(inner_partials, [((docs + 16, 128), f32)], q_total, d_total)
    inner_all = gather_blocks(inner)
    valid = jnp.take(slot_valid[0], negatives).astype(f32)
    weight = query_weight[None, :]
    small = jnp.pad(
        jnp.concatenate([valid, jnp.zeros_like(weight), weight], axis=0), ((0, 7), (0, 0))
    )
    small = jnp.concatenate([small, small], axis=1)
    received, small, neg_rows = lax.optimization_barrier((received, small, neg_rows))

    (hard,) = call(hard_partials, [((16, 128), f32)], received, q_low, neg_rows)
    hard_all = gather_blocks(hard)
    rows, u_query, g_local, loss = call(
        softmax_terms,
        [((slots, cols), bf16), ((queries, cols), bf16), ((docs, cols), f32), ((8, 128), f32)],
        *inner_all,
        *hard_all,
        small,
        neg_rows,
        received,
        d_total,
        q_total,
    )
    arrived = lax.all_to_all(
        rows.reshape(n_dp, cap, cols), "dp", split_axis=0, concat_axis=0, tiled=True
    ).reshape(slots, cols)
    grad_query = project_back(u_query, query_proj, k)

    (u_docs,) = call(doc_grads, [((docs, cols), bf16)], arrived, requests, g_local)
    grad_doc = project_back(u_docs, doc_proj, k)
    return (loss[0, :queries], grad_query, grad_doc)


def solution(mesh):
    in_specs = (
        P("dp", "phase"),
        P("dp", "phase"),
        P("phase", None),
        P("phase", None),
        P("dp", None, None),
        P("dp", None),
        P("dp", None),
        P("dp"),
    )
    out_specs = (P("dp"), P("dp", "phase"), P("dp", "phase"))
    return jax.shard_map(local, mesh=mesh, in_specs=in_specs, out_specs=out_specs, check_vma=False)
```

```python
import jax
import jax.numpy as jnp
from jax import lax
from jax.experimental import pallas as pl
from jax.experimental.pallas import tpu as pltpu
from jax.sharding import PartitionSpec as P

scale20 = 20.0
epsilon = 1e-06
f32 = jnp.float32
bf16 = jnp.bfloat16
NT = (((1,), (1,)), ((), ()))
TN = (((0,), (0,)), ((), ()))
N_PHASE = 4
cost = pl.CostEstimate(flops=10**9, bytes_accessed=10**5, transcendentals=0)


def dot(a, b, dims=(((1,), (0,)), ((), ()))):
    return lax.dot_general(a, b, dims, preferred_element_type=f32)


def params(mib=16):
    return pltpu.CompilerParams(vmem_limit_bytes=mib * 1024 * 1024)


def call(body, outs, *args):
    return pl.pallas_call(
        body,
        out_shape=[jax.ShapeDtypeStruct(s, t) for s, t in outs],
        compiler_params=params(),
        cost_estimate=cost,
    )(*args)


def iota(shape, dim):
    return lax.broadcasted_iota(jnp.int32, shape, dim)


def split_bf16(x):
    hi = x.astype(bf16)
    return hi, (x - hi.astype(f32)).astype(bf16)


def project(x, w, k):
    rows, depth = x.shape
    cols = w.shape[1] // N_PHASE
    order = (2, 1, 3, 0)

    def body(k_ref, x_ref, w_ref, *refs):
        outs, (x_buf, w_buf, own_buf, send_buf, sem_ref) = refs[:N_PHASE], refs[N_PHASE:]

        def load(s):
            start = pl.multiple_of(lax.rem(k_ref[0] + s, N_PHASE) * cols, cols)
            return pltpu.make_async_copy(w_ref.at[:, pl.ds(start, cols)], w_buf.at[s], sem_ref.at[s])

        def store(s):
            source = own_buf if s == 0 else send_buf.at[s - 1]
            return pltpu.make_async_copy(source, outs[s], sem_ref.at[N_PHASE + 1 + s])

        load_x = pltpu.make_async_copy(x_ref, x_buf, sem_ref.at[N_PHASE])
        load_x.start()
        for s in order:
            load(s).start()
        load_x.wait()
        for s in order:
            load(s).wait()
            y = dot(x_buf[...], w_buf[s])
            if s == 0:
                own_buf[...] = y
            else:
                send_buf[s - 1] = y.astype(bf16)
            store(s).start()
        for s in order:
            store(s).wait()

    hbm = pl.BlockSpec(memory_space=pltpu.HBM)
    return pl.pallas_call(
        body,
        in_specs=[pl.BlockSpec(memory_space=pltpu.SMEM), hbm, hbm],
        out_specs=[hbm] * N_PHASE,
        out_shape=[jax.ShapeDtypeStruct((rows, cols), f32)]
        + [jax.ShapeDtypeStruct((rows, cols), bf16)] * (N_PHASE - 1),
        scratch_shapes=[
            pltpu.VMEM((rows, depth), bf16),
            pltpu.VMEM((N_PHASE, depth, cols), bf16),
            pltpu.VMEM((rows, cols), f32),
            pltpu.VMEM((N_PHASE - 1, rows, cols), bf16),
            pltpu.SemaphoreType.DMA((2 * N_PHASE + 1,)),
        ],
        compiler_params=params(63),
        cost_estimate=cost,
    )(k, x, w)


def project_back_own(block, w, k):
    rows, cols = block.shape
    depth = w.shape[0]

    def body(k_ref, u_ref, w_ref, acc_ref):
        acc_ref[...] = dot(u_ref[...], w_ref[...], NT)

    return pl.pallas_call(
        body,
        grid_spec=pltpu.PrefetchScalarGridSpec(
            num_scalar_prefetch=1,
            grid=(1,),
            in_specs=[
                pl.BlockSpec((rows, cols), lambda s, k_ref: (0, 0)),
                pl.BlockSpec((depth, cols), lambda s, k_ref: (0, k_ref[0])),
            ],
            out_specs=pl.BlockSpec((rows, depth), lambda s, k_ref: (0, 0)),
        ),
        out_shape=jax.ShapeDtypeStruct((rows, depth), f32),
        compiler_params=params(),
        cost_estimate=cost,
    )(k, block, w)


def project_back_rest(acc, blocks, w, k):
    rows, cols = blocks[0].shape
    depth = w.shape[0]

    def body(k_ref, in_ref, *refs):
        block_refs, w_ref, out_ref, acc_ref = refs[:3], refs[3], refs[4], refs[5]
        step = pl.program_id(0)
        for s in range(N_PHASE - 1):

            @pl.when(step == s)
            def _():
                before = in_ref if s == 0 else acc_ref
                total = before[...] + dot(block_refs[s][...], w_ref[...], NT)
                if s == N_PHASE - 2:
                    out_ref[...] = total.astype(bf16)
                else:
                    acc_ref[...] = total

    const = lambda shape: pl.BlockSpec(shape, lambda s, k_ref: (0, 0))
    return pl.pallas_call(
        body,
        grid_spec=pltpu.PrefetchScalarGridSpec(
            num_scalar_prefetch=1,
            grid=(N_PHASE - 1,),
            in_specs=[const((rows, depth))]
            + [const((rows, cols))] * (N_PHASE - 1)
            + [pl.BlockSpec((depth, cols), lambda s, k_ref: (0, lax.rem(k_ref[0] + s + 1, N_PHASE)))],
            out_specs=const((rows, depth)),
            scratch_shapes=[pltpu.VMEM((rows, depth), f32)],
        ),
        out_shape=jax.ShapeDtypeStruct((rows, depth), bf16),
        compiler_params=params(),
        cost_estimate=cost,
    )(k, acc, *blocks, w)


def project_back(u, w, k):
    return project_back_rest(project_back_own(u, w, k), gather_blocks(u)[1:], w, k)


def shift_sends(blocks):
    return [
        lax.ppermute(b, "phase", [(i, (i + s) % N_PHASE) for i in range(N_PHASE)])
        for s, b in enumerate(blocks, start=1)
    ]


def gather_blocks(x):
    return [x] + [
        lax.ppermute(x, "phase", [((i + s) % N_PHASE, i) for i in range(N_PHASE)]) for s in range(1, N_PHASE)
    ]


def sum_refs(refs):
    total = refs[0][...].astype(f32)
    for r in refs[1:]:
        total = total + r[...].astype(f32)
    return total


def sum_queries(own, a, b, c, total_ref, low_ref):
    total = sum_refs((own, a, b, c))
    total_ref[...] = total
    low_ref[...] = total.astype(bf16)


def sum_docs(own, a, b, c, request_ref, total_ref, rows_ref):
    total = sum_refs((own, a, b, c))
    total_ref[...] = total
    slots = rows_ref.shape[0]
    onehot = (iota((total.shape[0], slots), 0) == request_ref[...]).astype(f32).astype(bf16)
    rows_ref[...] = dot(onehot, total.astype(bf16), TN).astype(bf16)


def ones_row_sums(x):
    hi, lo = split_bf16(x)
    ones = jnp.ones((8, x.shape[1]), bf16)
    return dot(ones, hi, NT) + dot(ones, lo, NT)


def inner_partials(q_ref, d_ref, out_ref):
    q = q_ref[...]
    d = d_ref[...]
    q2 = jnp.concatenate([q, q], axis=0)
    docs = d.shape[0]
    out_ref[0:docs, :] = dot(d.astype(bf16), q2.astype(bf16), NT)
    out_ref[docs : docs + 8, :] = ones_row_sums(q2 * q2)
    out_ref[docs + 8 : docs + 16, :] = ones_row_sums(d * d)


def hard_partials(rows_ref, q_ref, neg_ref, out_ref):
    rows = rows_ref[...]
    q = q_ref[...]
    scores = dot(rows, jnp.concatenate([q, q], axis=0), NT)
    wide = rows.astype(f32)
    square = wide * wide
    lanes = scores.shape[1]
    folded = square[:, 0:lanes]
    for s in range(lanes, square.shape[1], lanes):
        folded = folded + square[:, s : s + lanes]
    hi, lo = split_bf16(folded)
    ones = jnp.ones((lanes, lanes), bf16)
    squares = dot(hi, ones) + dot(lo, ones)
    slot = iota(scores.shape, 0)
    for j in range(8):
        hit = slot == neg_ref[j : j + 1, :]
        out_ref[j : j + 1, :] = jnp.sum(jnp.where(hit, scores, 0.0), axis=0, keepdims=True)
        out_ref[8 + j : 9 + j, :] = jnp.sum(jnp.where(hit, squares, 0.0), axis=0, keepdims=True)


def softmax_terms(*refs):
    inner_refs, hard_refs = refs[0:4], refs[4:8]
    small_ref, neg_ref, rows_ref, d_ref, q_ref, out_ref, u_ref, g_ref, loss_ref = refs[8:]
    sums = sum_refs(inner_refs)
    picks = sum_refs(hard_refs)
    docs, queries = d_ref.shape[0], q_ref.shape[0]
    q_scale = lax.rsqrt(sums[docs : docs + 1, :] + epsilon)
    d_scale_row = lax.rsqrt(sums[docs + 8 : docs + 9, :] + epsilon)
    row = iota((docs, 128), 0)
    lane = iota((docs, 128), 1)
    d_scale = jnp.sum(jnp.where(row == lane, d_scale_row, 0.0), axis=1, keepdims=True)
    inner = scale20 * (sums[0:docs, :] * q_scale * d_scale)
    hard_scale = lax.rsqrt(picks[8:16, :] + epsilon)
    hard = scale20 * (picks[0:8, :] * q_scale * hard_scale)
    valid = small_ref[0:8, :]
    weight = scale20 * small_ref[8:9, :]
    hard_exp = jnp.exp(hard) * valid
    inner_exp = jnp.exp(inner)
    total = jnp.sum(inner_exp, axis=0, keepdims=True) + jnp.sum(hard_exp, axis=0, keepdims=True)
    own = row == lax.bitwise_and(lane, 63)
    positive = jnp.sum(jnp.where(own, inner, 0.0), axis=0, keepdims=True)
    loss_ref[...] = jnp.broadcast_to(jnp.log(total) - positive, loss_ref.shape)
    factor = weight / total
    grad = (factor * inner_exp - jnp.where(own, weight, 0.0)).astype(bf16)
    wide_grad = grad.astype(f32)
    hard_grad = factor * hard_exp
    hard_dot = hard_grad * hard * (1.0 / scale20)
    products = wide_grad * inner * (1.0 / scale20)
    q_dot = jnp.sum(products, axis=0, keepdims=True) + jnp.sum(hard_dot, axis=0, keepdims=True)
    d_dot = jnp.sum(jnp.where(lane < 64, products, 0.0), axis=1, keepdims=True)
    sent = hard_scale * jnp.where(iota((8, 128), 1) < 64, hard_grad, hard_dot * hard_scale)
    slots = out_ref.shape[0]
    slot = iota((slots, 128), 0)
    coef = jnp.zeros((slots, 128), f32)
    for j in range(7):
        coef = coef + jnp.where(slot == neg_ref[j : j + 1, :], sent[j : j + 1, :], 0.0)
    coef = coef.astype(bf16)

    eye = iota((queries, 128), 0) == iota((queries, 128), 1)
    q_scale_col = jnp.sum(jnp.where(eye, q_scale, 0.0), axis=1, keepdims=True)
    q_dot_col = jnp.sum(jnp.where(eye, q_dot, 0.0), axis=1, keepdims=True)
    q_unit = q_ref[...] * q_scale_col
    q_low = jnp.concatenate([q_unit.astype(bf16), jnp.zeros(q_ref.shape, bf16)], axis=0)
    second = (iota((128, 128), 0) >= 64).astype(f32).astype(bf16)
    along = dot(coef, second)
    mixed = dot(coef, q_low)
    for s in range(0, mixed.shape[1], 128):
        part = rows_ref[:, s : s + 128].astype(f32)
        out_ref[:, s : s + 128] = (mixed[:, s : s + 128] - along * part).astype(bf16)

    d_unit = d_ref[...] * d_scale
    g_query = dot(grad, d_unit.astype(bf16), TN) + dot(coef, rows_ref[...], TN)
    u_ref[...] = (q_scale_col * (g_query[0:queries, :] - q_unit * q_dot_col)).astype(bf16)
    g_ref[...] = d_scale * (dot(grad, q_low) - d_unit * d_dot)


def doc_grads(rows_ref, request_ref, g_ref, u_ref):
    docs, slots = g_ref.shape[0], rows_ref.shape[0]
    onehot = (iota((docs, slots), 0) == request_ref[...]).astype(f32).astype(bf16)
    u_ref[...] = (g_ref[...] + dot(onehot, rows_ref[...])).astype(bf16)


def local(
    query_states,
    doc_states,
    query_proj,
    doc_proj,
    document_requests,
    slot_valid,
    neg_slot,
    query_weight,
):
    k = lax.axis_index("phase").astype(jnp.int32).reshape(1)
    queries, docs = query_states.shape[0], doc_states.shape[0]
    cols = query_proj.shape[1] // N_PHASE
    n_dp, cap = document_requests.shape[1:]
    slots = n_dp * cap

    negatives = neg_slot.T
    requests = document_requests.reshape(1, slots)
    neg_rows = jnp.pad(jnp.concatenate([negatives, negatives], axis=1), ((0, 1), (0, 0)), constant_values=-1)

    d_own, *d_send = project(doc_states, doc_proj, k)
    d_parts = shift_sends(d_send)
    d_total, outgoing = call(
        sum_docs, [((docs, cols), f32), ((slots, cols), bf16)], d_own, *d_parts, requests
    )
    outgoing, query_states = lax.optimization_barrier((outgoing, query_states))
    received = lax.all_to_all(
        outgoing.reshape(n_dp, cap, cols), "dp", split_axis=0, concat_axis=0, tiled=True
    ).reshape(slots, cols)

    q_own, *q_send = project(query_states, query_proj, k)
    q_parts = shift_sends(q_send)
    q_total, q_low = call(sum_queries, [((queries, cols), f32), ((queries, cols), bf16)], q_own, *q_parts)
    (inner,) = call(inner_partials, [((docs + 16, 128), f32)], q_total, d_total)
    inner_all = gather_blocks(inner)
    valid = jnp.take(slot_valid[0], negatives).astype(f32)
    weight = query_weight[None, :]
    small = jnp.pad(
        jnp.concatenate([valid, jnp.zeros_like(weight), weight], axis=0), ((0, 7), (0, 0))
    )
    small = jnp.concatenate([small, small], axis=1)
    received, small, neg_rows = lax.optimization_barrier((received, small, neg_rows))

    (hard,) = call(hard_partials, [((16, 128), f32)], received, q_low, neg_rows)
    hard_all = gather_blocks(hard)
    rows, u_query, g_local, loss = call(
        softmax_terms,
        [((slots, cols), bf16), ((queries, cols), bf16), ((docs, cols), f32), ((8, 128), f32)],
        *inner_all,
        *hard_all,
        small,
        neg_rows,
        received,
        d_total,
        q_total,
    )
    arrived = lax.all_to_all(
        rows.reshape(n_dp, cap, cols), "dp", split_axis=0, concat_axis=0, tiled=True
    ).reshape(slots, cols)
    grad_query = project_back(u_query, query_proj, k)
    arrived, grad_query, loss = lax.optimization_barrier((arrived, grad_query, loss[0, :queries]))

    (u_docs,) = call(doc_grads, [((docs, cols), bf16)], arrived, requests, g_local)
    grad_doc = project_back(u_docs, doc_proj, k)
    return (loss, grad_query, grad_doc)


def solution(mesh):
    in_specs = (
        P("dp", "phase"),
        P("dp", "phase"),
        P("phase", None),
        P("phase", None),
        P("dp", None, None),
        P("dp", None),
        P("dp", None),
        P("dp"),
    )
    out_specs = (P("dp"), P("dp", "phase"), P("dp", "phase"))
    return jax.shard_map(local, mesh=mesh, in_specs=in_specs, out_specs=out_specs, check_vma=False)
```

```python
import jax
import jax.numpy as jnp
from jax import lax
from jax.experimental import pallas as pl
from jax.experimental.pallas import tpu as pltpu
from jax.sharding import PartitionSpec as P

scale20 = 20.0
epsilon = 1e-06
f32 = jnp.float32
bf16 = jnp.bfloat16
NT = (((1,), (1,)), ((), ()))
TN = (((0,), (0,)), ((), ()))
N_PHASE = 4
cost = pl.CostEstimate(flops=10**9, bytes_accessed=10**5, transcendentals=0)


def dot(a, b, dims=(((1,), (0,)), ((), ()))):
    return lax.dot_general(a, b, dims, preferred_element_type=f32)


def params(mib=16):
    return pltpu.CompilerParams(vmem_limit_bytes=mib * 1024 * 1024)


def call(body, outs, *args):
    return pl.pallas_call(
        body,
        out_shape=[jax.ShapeDtypeStruct(s, t) for s, t in outs],
        compiler_params=params(),
        cost_estimate=cost,
    )(*args)


def iota(shape, dim):
    return lax.broadcasted_iota(jnp.int32, shape, dim)


def split_bf16(x):
    hi = x.astype(bf16)
    return hi, (x - hi.astype(f32)).astype(bf16)


def project_sends(x, w, k, mib):
    rows, depth = x.shape
    cols = w.shape[1] // N_PHASE
    order = (2, 1, 3)

    def body(k_ref, x_ref, w_ref, *refs):
        outs, (x_buf, w_buf, out_buf, sem_ref) = refs[:3], refs[3:]

        def load(s):
            start = pl.multiple_of(lax.rem(k_ref[0] + s, N_PHASE) * cols, cols)
            return pltpu.make_async_copy(w_ref.at[:, pl.ds(start, cols)], w_buf.at[s - 1], sem_ref.at[s])

        def store(s):
            return pltpu.make_async_copy(out_buf.at[s - 1], outs[s - 1], sem_ref.at[N_PHASE + s])

        load_x = pltpu.make_async_copy(x_ref, x_buf, sem_ref.at[0])
        load_x.start()
        for s in order:
            load(s).start()
        load_x.wait()
        for s in order:
            load(s).wait()
            out_buf[s - 1] = dot(x_buf[...], w_buf[s - 1]).astype(bf16)
            store(s).start()
        for s in order:
            store(s).wait()

    hbm = pl.BlockSpec(memory_space=pltpu.HBM)
    return pl.pallas_call(
        body,
        in_specs=[pl.BlockSpec(memory_space=pltpu.SMEM), hbm, hbm],
        out_specs=[hbm] * 3,
        out_shape=[jax.ShapeDtypeStruct((rows, cols), bf16)] * 3,
        scratch_shapes=[
            pltpu.VMEM((rows, depth), bf16),
            pltpu.VMEM((3, depth, cols), bf16),
            pltpu.VMEM((3, rows, cols), bf16),
            pltpu.SemaphoreType.DMA((2 * N_PHASE,)),
        ],
        compiler_params=params(mib),
        cost_estimate=cost,
    )(k, x, w)


def project_own(x, w, k):
    rows, depth = x.shape
    cols = w.shape[1] // N_PHASE

    def body(k_ref, x_ref, w_ref, own_ref):
        own_ref[...] = dot(x_ref[...], w_ref[...])

    return pl.pallas_call(
        body,
        grid_spec=pltpu.PrefetchScalarGridSpec(
            num_scalar_prefetch=1,
            grid=(1,),
            in_specs=[
                pl.BlockSpec((rows, depth), lambda s, k_ref: (0, 0)),
                pl.BlockSpec((depth, cols), lambda s, k_ref: (0, k_ref[0])),
            ],
            out_specs=pl.BlockSpec((rows, cols), lambda s, k_ref: (0, 0)),
        ),
        out_shape=jax.ShapeDtypeStruct((rows, cols), f32),
        compiler_params=params(),
        cost_estimate=cost,
    )(k, x, w)


def project(x, w, k, mib=16):
    return project_own(x, w, k), shift_sends(project_sends(x, w, k, mib))


def project_back(u, w, k):
    rows, cols = u.shape
    depth = w.shape[0]

    def columns(w_ref, k_ref, s):
        return w_ref[:, pl.ds(pl.multiple_of(lax.rem(k_ref[0] + s, N_PHASE) * cols, cols), cols)]

    def own(k_ref, u_ref, w_ref, acc_ref):
        acc_ref[...] = dot(u_ref[...], columns(w_ref, k_ref, 0), NT)

    def rest(k_ref, acc_ref, a_ref, b_ref, c_ref, w_ref, out_ref):
        total = acc_ref[...]
        for s, block in enumerate((a_ref, b_ref, c_ref), start=1):
            total = total + dot(block[...], columns(w_ref, k_ref, s), NT)
        out_ref[...] = total.astype(bf16)

    def run(body, dtype, n):
        vmem = pl.BlockSpec(memory_space=pltpu.VMEM)
        return pl.pallas_call(
            body,
            in_specs=[pl.BlockSpec(memory_space=pltpu.SMEM)] + [vmem] * n,
            out_specs=vmem,
            out_shape=jax.ShapeDtypeStruct((rows, depth), dtype),
            compiler_params=params(),
            cost_estimate=cost,
        )

    blocks = gather_blocks(u)
    acc = run(own, f32, 2)(k, blocks[0], w)
    return run(rest, bf16, 5)(k, acc, *blocks[1:], w)


def shift_sends(blocks):
    return [
        lax.ppermute(b, "phase", [(i, (i + s) % N_PHASE) for i in range(N_PHASE)])
        for s, b in enumerate(blocks, start=1)
    ]


def gather_blocks(x):
    return [x] + [
        lax.ppermute(x, "phase", [((i + s) % N_PHASE, i) for i in range(N_PHASE)]) for s in range(1, N_PHASE)
    ]


def sum_refs(refs):
    total = refs[0][...].astype(f32)
    for r in refs[1:]:
        total = total + r[...].astype(f32)
    return total


def sum_queries(own, a, b, c, total_ref, low_ref):
    total = sum_refs((own, a, b, c))
    total_ref[...] = total
    low_ref[...] = total.astype(bf16)


def sum_docs(parts, requests):
    docs, cols = parts[0].shape
    slots = requests.shape[1]
    steps = 4
    block = slots // steps

    def body(a, b, c, d, request_ref, total_ref, rows_ref, low_ref):
        @pl.when(pl.program_id(0) == 0)
        def _():
            total = sum_refs((a, b, c, d))
            total_ref[...] = total
            low_ref[...] = total.astype(bf16)

        onehot = (iota((docs, block), 0) == request_ref[...]).astype(f32).astype(bf16)
        rows_ref[...] = dot(onehot, low_ref[...], TN).astype(bf16)

    whole = pl.BlockSpec((docs, cols), lambda s: (0, 0))
    return pl.pallas_call(
        body,
        grid=(steps,),
        in_specs=[whole] * 4 + [pl.BlockSpec((1, block), lambda s: (0, s))],
        out_specs=[whole, pl.BlockSpec((block, cols), lambda s: (s, 0))],
        out_shape=[jax.ShapeDtypeStruct((docs, cols), f32), jax.ShapeDtypeStruct((slots, cols), bf16)],
        scratch_shapes=[pltpu.VMEM((docs, cols), bf16)],
        compiler_params=params(),
        cost_estimate=cost,
    )(*parts, requests)


def ones_row_sums(x):
    hi, lo = split_bf16(x)
    ones = jnp.ones((8, x.shape[1]), bf16)
    return dot(ones, hi, NT) + dot(ones, lo, NT)


def inner_partials(q_ref, d_ref, out_ref):
    q = q_ref[...]
    d = d_ref[...]
    q2 = jnp.concatenate([q, q], axis=0)
    docs = d.shape[0]
    out_ref[0:docs, :] = dot(d.astype(bf16), q2.astype(bf16), NT)
    out_ref[docs : docs + 8, :] = ones_row_sums(q2 * q2)
    out_ref[docs + 8 : docs + 16, :] = ones_row_sums(d * d)


def hard_partials(rows_ref, q_ref, neg_ref, out_ref):
    rows = rows_ref[...]
    q = q_ref[...]
    scores = dot(rows, jnp.concatenate([q, q], axis=0), NT)
    wide = rows.astype(f32)
    square = wide * wide
    lanes = scores.shape[1]
    folded = square[:, 0:lanes]
    for s in range(lanes, square.shape[1], lanes):
        folded = folded + square[:, s : s + lanes]
    hi, lo = split_bf16(folded)
    ones = jnp.ones((lanes, lanes), bf16)
    squares = dot(hi, ones) + dot(lo, ones)
    slot = iota(scores.shape, 0)
    for j in range(8):
        hit = slot == neg_ref[j : j + 1, :]
        out_ref[j : j + 1, :] = jnp.sum(jnp.where(hit, scores, 0.0), axis=0, keepdims=True)
        out_ref[8 + j : 9 + j, :] = jnp.sum(jnp.where(hit, squares, 0.0), axis=0, keepdims=True)


def softmax_terms(*refs):
    inner_refs, hard_refs = refs[0:4], refs[4:8]
    small_ref, neg_ref, rows_ref, d_ref, q_ref, out_ref, u_ref, g_ref, loss_ref = refs[8:]
    sums = sum_refs(inner_refs)
    picks = sum_refs(hard_refs)
    docs, queries = d_ref.shape[0], q_ref.shape[0]
    q_scale = lax.rsqrt(sums[docs : docs + 1, :] + epsilon)
    d_scale_row = lax.rsqrt(sums[docs + 8 : docs + 9, :] + epsilon)
    row = iota((docs, 128), 0)
    lane = iota((docs, 128), 1)
    d_scale = jnp.sum(jnp.where(row == lane, d_scale_row, 0.0), axis=1, keepdims=True)
    inner = scale20 * (sums[0:docs, :] * q_scale * d_scale)
    hard_scale = lax.rsqrt(picks[8:16, :] + epsilon)
    hard = scale20 * (picks[0:8, :] * q_scale * hard_scale)
    valid = small_ref[0:8, :]
    weight = scale20 * small_ref[8:9, :]
    hard_exp = jnp.exp(hard) * valid
    inner_exp = jnp.exp(inner)
    total = jnp.sum(inner_exp, axis=0, keepdims=True) + jnp.sum(hard_exp, axis=0, keepdims=True)
    own = row == lax.bitwise_and(lane, 63)
    positive = jnp.sum(jnp.where(own, inner, 0.0), axis=0, keepdims=True)
    loss_ref[...] = jnp.broadcast_to(jnp.log(total) - positive, loss_ref.shape)
    factor = weight / total
    grad = (factor * inner_exp - jnp.where(own, weight, 0.0)).astype(bf16)
    wide_grad = grad.astype(f32)
    hard_grad = factor * hard_exp
    hard_dot = hard_grad * hard * (1.0 / scale20)
    products = wide_grad * inner * (1.0 / scale20)
    q_dot = jnp.sum(products, axis=0, keepdims=True) + jnp.sum(hard_dot, axis=0, keepdims=True)
    d_dot = jnp.sum(jnp.where(lane < 64, products, 0.0), axis=1, keepdims=True)
    sent = hard_scale * jnp.where(iota((8, 128), 1) < 64, hard_grad, hard_dot * hard_scale)
    slots = out_ref.shape[0]
    slot = iota((slots, 128), 0)
    coef = jnp.zeros((slots, 128), f32)
    for j in range(7):
        coef = coef + jnp.where(slot == neg_ref[j : j + 1, :], sent[j : j + 1, :], 0.0)
    coef = coef.astype(bf16)

    eye = iota((queries, 128), 0) == iota((queries, 128), 1)
    q_scale_col = jnp.sum(jnp.where(eye, q_scale, 0.0), axis=1, keepdims=True)
    q_dot_col = jnp.sum(jnp.where(eye, q_dot, 0.0), axis=1, keepdims=True)
    q_unit = q_ref[...] * q_scale_col
    q_low = jnp.concatenate([q_unit.astype(bf16), jnp.zeros(q_ref.shape, bf16)], axis=0)
    second = (iota((128, 128), 0) >= 64).astype(f32).astype(bf16)
    along = dot(coef, second)
    mixed = dot(coef, q_low)
    for s in range(0, mixed.shape[1], 128):
        part = rows_ref[:, s : s + 128].astype(f32)
        out_ref[:, s : s + 128] = (mixed[:, s : s + 128] - along * part).astype(bf16)

    d_unit = d_ref[...] * d_scale
    g_query = dot(grad, d_unit.astype(bf16), TN) + dot(coef, rows_ref[...], TN)
    u_ref[...] = (q_scale_col * (g_query[0:queries, :] - q_unit * q_dot_col)).astype(bf16)
    g_ref[...] = d_scale * (dot(grad, q_low) - d_unit * d_dot)


def doc_grads(rows_ref, request_ref, g_ref, u_ref):
    docs, slots = g_ref.shape[0], rows_ref.shape[0]
    onehot = (iota((docs, slots), 0) == request_ref[...]).astype(f32).astype(bf16)
    u_ref[...] = (g_ref[...] + dot(onehot, rows_ref[...])).astype(bf16)


def local(
    query_states,
    doc_states,
    query_proj,
    doc_proj,
    document_requests,
    slot_valid,
    neg_slot,
    query_weight,
):
    k = lax.axis_index("phase").astype(jnp.int32).reshape(1)
    queries, docs = query_states.shape[0], doc_states.shape[0]
    cols = query_proj.shape[1] // N_PHASE
    n_dp, cap = document_requests.shape[1:]
    slots = n_dp * cap

    negatives = neg_slot.T
    requests = document_requests.reshape(1, slots)
    neg_rows = jnp.pad(jnp.concatenate([negatives, negatives], axis=1), ((0, 1), (0, 0)), constant_values=-1)

    d_own, d_parts = project(doc_states, doc_proj, k, 63)
    d_total, outgoing = sum_docs([d_own] + d_parts, requests)
    outgoing, query_states = lax.optimization_barrier((outgoing, query_states))
    received = lax.all_to_all(
        outgoing.reshape(n_dp, cap, cols), "dp", split_axis=0, concat_axis=0, tiled=True
    ).reshape(slots, cols)

    q_own, q_parts = project(query_states, query_proj, k)
    q_total, q_low = call(sum_queries, [((queries, cols), f32), ((queries, cols), bf16)], q_own, *q_parts)
    (inner,) = call(inner_partials, [((docs + 16, 128), f32)], q_total, d_total)
    inner_all = gather_blocks(inner)
    valid = jnp.take(slot_valid[0], negatives).astype(f32)
    weight = query_weight[None, :]
    small = jnp.pad(
        jnp.concatenate([valid, jnp.zeros_like(weight), weight], axis=0), ((0, 7), (0, 0))
    )
    small = jnp.concatenate([small, small], axis=1)
    received, small, neg_rows = lax.optimization_barrier((received, small, neg_rows))

    (hard,) = call(hard_partials, [((16, 128), f32)], received, q_low, neg_rows)
    hard_all = gather_blocks(hard)
    rows, u_query, g_local, loss = call(
        softmax_terms,
        [((slots, cols), bf16), ((queries, cols), bf16), ((docs, cols), f32), ((8, 128), f32)],
        *inner_all,
        *hard_all,
        small,
        neg_rows,
        received,
        d_total,
        q_total,
    )
    arrived = lax.all_to_all(
        rows.reshape(n_dp, cap, cols), "dp", split_axis=0, concat_axis=0, tiled=True
    ).reshape(slots, cols)
    grad_query = project_back(u_query, query_proj, k)
    arrived, grad_query, loss = lax.optimization_barrier((arrived, grad_query, loss[0, :queries]))

    (u_docs,) = call(doc_grads, [((docs, cols), bf16)], arrived, requests, g_local)
    grad_doc = project_back(u_docs, doc_proj, k)
    return (loss, grad_query, grad_doc)


def solution(mesh):
    in_specs = (
        P("dp", "phase"),
        P("dp", "phase"),
        P("phase", None),
        P("phase", None),
        P("dp", None, None),
        P("dp", None),
        P("dp", None),
        P("dp"),
    )
    out_specs = (P("dp"), P("dp", "phase"), P("dp", "phase"))
    return jax.shard_map(local, mesh=mesh, in_specs=in_specs, out_specs=out_specs, check_vma=False)
```

```python
import jax
import jax.numpy as jnp
from jax import lax
from jax.experimental import pallas as pl
from jax.experimental.pallas import tpu as pltpu
from jax.sharding import PartitionSpec as P

scale20 = 20.0
epsilon = 1e-06
f32 = jnp.float32
bf16 = jnp.bfloat16
NT = (((1,), (1,)), ((), ()))
TN = (((0,), (0,)), ((), ()))
N_PHASE = 4
CHUNKS = 4
cost = pl.CostEstimate(flops=10**9, bytes_accessed=10**5, transcendentals=0)


def dot(a, b, dims=(((1,), (0,)), ((), ()))):
    return lax.dot_general(a, b, dims, preferred_element_type=f32)


def params(mib=16):
    return pltpu.CompilerParams(vmem_limit_bytes=mib * 1024 * 1024)


def call(body, outs, *args):
    return pl.pallas_call(
        body,
        out_shape=[jax.ShapeDtypeStruct(s, t) for s, t in outs],
        compiler_params=params(),
        cost_estimate=cost,
    )(*args)


def iota(shape, dim):
    return lax.broadcasted_iota(jnp.int32, shape, dim)


def split_bf16(x):
    hi = x.astype(bf16)
    return hi, (x - hi.astype(f32)).astype(bf16)


def project_sends(x, w, k, mib, order):
    rows, depth = x.shape
    cols = w.shape[1] // N_PHASE
    n = len(order)

    def body(k_ref, x_ref, w_ref, *refs):
        outs, (x_buf, w_buf, out_buf, sem_ref) = refs[:n], refs[n:]

        def load(i):
            start = pl.multiple_of(lax.rem(k_ref[0] + order[i], N_PHASE) * cols, cols)
            return pltpu.make_async_copy(w_ref.at[:, pl.ds(start, cols)], w_buf.at[i], sem_ref.at[i])

        def store(i):
            return pltpu.make_async_copy(out_buf.at[i], outs[i], sem_ref.at[n + i])

        load_x = pltpu.make_async_copy(x_ref, x_buf, sem_ref.at[2 * n])
        load_x.start()
        for i in range(n):
            load(i).start()
        load_x.wait()
        for i in range(n):
            load(i).wait()
            out_buf[i] = dot(x_buf[...], w_buf[i]).astype(bf16)
            store(i).start()
        for i in range(n):
            store(i).wait()

    hbm = pl.BlockSpec(memory_space=pltpu.HBM)
    return pl.pallas_call(
        body,
        in_specs=[pl.BlockSpec(memory_space=pltpu.SMEM), hbm, hbm],
        out_specs=[hbm] * n,
        out_shape=[jax.ShapeDtypeStruct((rows, cols), bf16)] * n,
        scratch_shapes=[
            pltpu.VMEM((rows, depth), bf16),
            pltpu.VMEM((n, depth, cols), bf16),
            pltpu.VMEM((n, rows, cols), bf16),
            pltpu.SemaphoreType.DMA((2 * n + 1,)),
        ],
        compiler_params=params(mib),
        cost_estimate=cost,
    )(k, x, w)


def project_own(x, w, k):
    rows, depth = x.shape
    cols = w.shape[1] // N_PHASE

    def body(k_ref, x_ref, w_ref, own_ref):
        own_ref[...] = dot(x_ref[...], w_ref[...])

    return pl.pallas_call(
        body,
        grid_spec=pltpu.PrefetchScalarGridSpec(
            num_scalar_prefetch=1,
            grid=(1,),
            in_specs=[
                pl.BlockSpec((rows, depth), lambda s, k_ref: (0, 0)),
                pl.BlockSpec((depth, cols), lambda s, k_ref: (0, k_ref[0])),
            ],
            out_specs=pl.BlockSpec((rows, cols), lambda s, k_ref: (0, 0)),
        ),
        out_shape=jax.ShapeDtypeStruct((rows, cols), f32),
        compiler_params=params(),
        cost_estimate=cost,
    )(k, x, w)


def project_back(u, w, k):
    rows, cols = u.shape
    depth = w.shape[0]

    def columns(w_ref, k_ref, s):
        return w_ref[:, pl.ds(pl.multiple_of(lax.rem(k_ref[0] + s, N_PHASE) * cols, cols), cols)]

    def product(*shifts):
        def body(k_ref, *refs):
            block_refs, w_ref, out_ref = refs[-len(shifts) - 2 : -2], refs[-2], refs[-1]
            total = sum(dot(r[...], columns(w_ref, k_ref, s), NT) for s, r in zip(shifts, block_refs))
            if len(refs) > len(shifts) + 2:
                total = refs[0][...] + total
            out_ref[...] = total.astype(out_ref.dtype)

        return body

    def run(body, dtype, *args):
        vmem = pl.BlockSpec(memory_space=pltpu.VMEM)
        return pl.pallas_call(
            body,
            in_specs=[pl.BlockSpec(memory_space=pltpu.SMEM)] + [vmem] * len(args),
            out_specs=vmem,
            out_shape=jax.ShapeDtypeStruct((rows, depth), dtype),
            compiler_params=params(),
            cost_estimate=cost,
        )(k, *args)

    blocks = gather_blocks(u)
    acc = run(product(0), f32, blocks[0], w)
    acc = run(product(3), f32, acc, blocks[3], w)
    return run(product(1, 2), bf16, acc, blocks[1], blocks[2], w)


def send(block, s):
    return lax.ppermute(block, "phase", [(i, (i + s) % N_PHASE) for i in range(N_PHASE)])


def gather_blocks(x):
    return [x] + [
        lax.ppermute(x, "phase", [((i + s) % N_PHASE, i) for i in range(N_PHASE)]) for s in range(1, N_PHASE)
    ]


def sum_refs(refs):
    total = refs[0][...].astype(f32)
    for r in refs[1:]:
        total = total + r[...].astype(f32)
    return total


def sum_queries(own, a, b, c, total_ref, low_ref):
    total = sum_refs((own, a, b, c))
    total_ref[...] = total
    low_ref[...] = total.astype(bf16)


def onehot_rows(request_ref, out_ref):
    docs = out_ref.shape[1]
    slots = out_ref.shape[0]
    onehot = (iota((docs, slots), 0) == request_ref[...]).astype(f32).astype(bf16)
    eye = (iota((docs, docs), 0) == iota((docs, docs), 1)).astype(f32).astype(bf16)
    out_ref[...] = dot(onehot, eye, TN).astype(bf16)


def sum_docs(parts, onehot):
    docs, cols = parts[0].shape
    slots = onehot.shape[0]
    block = slots // CHUNKS

    def body(a, b, c, d, onehot_ref, total_ref, rows_ref, buf_ref, sem_ref):
        total = sum_refs((a, b, c, d))
        total_ref[...] = total
        low = total.astype(bf16)

        def store(i):
            part = pl.ds(i * block, block)
            return pltpu.make_async_copy(buf_ref.at[part], rows_ref.at[part], sem_ref.at[i])

        for i in range(CHUNKS):
            part = slice(i * block, (i + 1) * block)
            buf_ref[part, :] = dot(onehot_ref[part, :], low).astype(bf16)
            store(i).start()
        for i in range(CHUNKS):
            store(i).wait()

    vmem = pl.BlockSpec(memory_space=pltpu.VMEM)
    return pl.pallas_call(
        body,
        in_specs=[vmem] * 5,
        out_specs=[vmem, pl.BlockSpec(memory_space=pltpu.HBM)],
        out_shape=[jax.ShapeDtypeStruct((docs, cols), f32), jax.ShapeDtypeStruct((slots, cols), bf16)],
        scratch_shapes=[pltpu.VMEM((slots, cols), bf16), pltpu.SemaphoreType.DMA((CHUNKS,))],
        compiler_params=params(),
        cost_estimate=cost,
    )(*parts, onehot)


def ones_row_sums(x):
    hi, lo = split_bf16(x)
    ones = jnp.ones((8, x.shape[1]), bf16)
    return dot(ones, hi, NT) + dot(ones, lo, NT)


def inner_partials(q_ref, d_ref, out_ref):
    q = q_ref[...]
    d = d_ref[...]
    q2 = jnp.concatenate([q, q], axis=0)
    docs = d.shape[0]
    out_ref[0:docs, :] = dot(d.astype(bf16), q2.astype(bf16), NT)
    out_ref[docs : docs + 8, :] = ones_row_sums(q2 * q2)
    out_ref[docs + 8 : docs + 16, :] = ones_row_sums(d * d)


def hard_partials(rows_ref, q_ref, neg_ref, out_ref):
    rows = rows_ref[...]
    q = q_ref[...]
    scores = dot(rows, jnp.concatenate([q, q], axis=0), NT)
    wide = rows.astype(f32)
    square = wide * wide
    lanes = scores.shape[1]
    folded = square[:, 0:lanes]
    for s in range(lanes, square.shape[1], lanes):
        folded = folded + square[:, s : s + lanes]
    hi, lo = split_bf16(folded)
    ones = jnp.ones((lanes, lanes), bf16)
    squares = dot(hi, ones) + dot(lo, ones)
    slot = iota(scores.shape, 0)
    for j in range(8):
        hit = slot == neg_ref[j : j + 1, :]
        out_ref[j : j + 1, :] = jnp.sum(jnp.where(hit, scores, 0.0), axis=0, keepdims=True)
        out_ref[8 + j : 9 + j, :] = jnp.sum(jnp.where(hit, squares, 0.0), axis=0, keepdims=True)


def softmax_terms(*refs):
    inner_refs, hard_refs = refs[0:4], refs[4:8]
    small_ref, neg_ref, rows_ref, d_ref, q_ref, out_ref, u_ref, g_ref, loss_ref, buf_ref, sem_ref = refs[8:]
    sums = sum_refs(inner_refs)
    picks = sum_refs(hard_refs)
    docs, queries = d_ref.shape[0], q_ref.shape[0]
    q_scale = lax.rsqrt(sums[docs : docs + 1, :] + epsilon)
    d_scale_row = lax.rsqrt(sums[docs + 8 : docs + 9, :] + epsilon)
    row = iota((docs, 128), 0)
    lane = iota((docs, 128), 1)
    d_scale = jnp.sum(jnp.where(row == lane, d_scale_row, 0.0), axis=1, keepdims=True)
    inner = scale20 * (sums[0:docs, :] * q_scale * d_scale)
    hard_scale = lax.rsqrt(picks[8:16, :] + epsilon)
    hard = scale20 * (picks[0:8, :] * q_scale * hard_scale)
    valid = small_ref[0:8, :]
    weight = scale20 * small_ref[8:9, :]
    hard_exp = jnp.exp(hard) * valid
    inner_exp = jnp.exp(inner)
    total = jnp.sum(inner_exp, axis=0, keepdims=True) + jnp.sum(hard_exp, axis=0, keepdims=True)
    own = row == lax.bitwise_and(lane, 63)
    positive = jnp.sum(jnp.where(own, inner, 0.0), axis=0, keepdims=True)
    loss_ref[...] = jnp.broadcast_to(jnp.log(total) - positive, loss_ref.shape)
    factor = weight / total
    grad = (factor * inner_exp - jnp.where(own, weight, 0.0)).astype(bf16)
    wide_grad = grad.astype(f32)
    hard_grad = factor * hard_exp
    hard_dot = hard_grad * hard * (1.0 / scale20)
    products = wide_grad * inner * (1.0 / scale20)
    q_dot = jnp.sum(products, axis=0, keepdims=True) + jnp.sum(hard_dot, axis=0, keepdims=True)
    d_dot = jnp.sum(jnp.where(lane < 64, products, 0.0), axis=1, keepdims=True)
    sent = hard_scale * jnp.where(iota((8, 128), 1) < 64, hard_grad, hard_dot * hard_scale)
    slots = out_ref.shape[0]
    slot = iota((slots, 128), 0)
    coef = jnp.zeros((slots, 128), f32)
    for j in range(7):
        coef = coef + jnp.where(slot == neg_ref[j : j + 1, :], sent[j : j + 1, :], 0.0)
    coef = coef.astype(bf16)

    eye = iota((queries, 128), 0) == iota((queries, 128), 1)
    q_scale_col = jnp.sum(jnp.where(eye, q_scale, 0.0), axis=1, keepdims=True)
    q_dot_col = jnp.sum(jnp.where(eye, q_dot, 0.0), axis=1, keepdims=True)
    q_unit = q_ref[...] * q_scale_col
    q_low = jnp.concatenate([q_unit.astype(bf16), jnp.zeros(q_ref.shape, bf16)], axis=0)
    second = (iota((128, 128), 0) >= 64).astype(f32).astype(bf16)
    block = slots // CHUNKS

    def store(i):
        part = pl.ds(i * block, block)
        return pltpu.make_async_copy(buf_ref.at[part], out_ref.at[part], sem_ref.at[i])

    for i in range(CHUNKS):
        part = slice(i * block, (i + 1) * block)
        along = dot(coef[part, :], second)
        mixed = dot(coef[part, :], q_low)
        for c in range(0, mixed.shape[1], 128):
            away = along * rows_ref[part, c : c + 128].astype(f32)
            buf_ref[part, c : c + 128] = (mixed[:, c : c + 128] - away).astype(bf16)
        store(i).start()

    d_unit = d_ref[...] * d_scale
    g_query = dot(grad, d_unit.astype(bf16), TN) + dot(coef, rows_ref[...], TN)
    u_ref[...] = (q_scale_col * (g_query[0:queries, :] - q_unit * q_dot_col)).astype(bf16)
    g_ref[...] = d_scale * (dot(grad, q_low) - d_unit * d_dot)
    for i in range(CHUNKS):
        store(i).wait()


def doc_grads(rows_ref, request_ref, g_ref, u_ref):
    docs, slots = g_ref.shape[0], rows_ref.shape[0]
    onehot = (iota((docs, slots), 0) == request_ref[...]).astype(f32).astype(bf16)
    u_ref[...] = (g_ref[...] + dot(onehot, rows_ref[...])).astype(bf16)


def local(
    query_states,
    doc_states,
    query_proj,
    doc_proj,
    document_requests,
    slot_valid,
    neg_slot,
    query_weight,
):
    k = lax.axis_index("phase").astype(jnp.int32).reshape(1)
    queries, docs = query_states.shape[0], doc_states.shape[0]
    cols = query_proj.shape[1] // N_PHASE
    n_dp, cap = document_requests.shape[1:]
    slots = n_dp * cap

    negatives = neg_slot.T
    requests = document_requests.reshape(1, slots)
    neg_rows = jnp.pad(jnp.concatenate([negatives, negatives], axis=1), ((0, 1), (0, 0)), constant_values=-1)

    (d_far,) = project_sends(doc_states, doc_proj, k, 63, (2,))
    d_next, d_last, requests = lax.optimization_barrier((*project_sends(doc_states, doc_proj, k, 63, (1, 3)), requests))
    d_parts = [send(d_far, 2), send(d_next, 1), send(d_last, 3)]
    d_own = project_own(doc_states, doc_proj, k)
    (onehot,) = call(onehot_rows, [((slots, docs), bf16)], requests)
    d_total, outgoing = sum_docs([d_own] + d_parts, onehot)
    outgoing, query_states = lax.optimization_barrier((outgoing, query_states))
    received = lax.all_to_all(
        outgoing.reshape(n_dp, cap, cols), "dp", split_axis=0, concat_axis=0, tiled=True
    ).reshape(slots, cols)

    q_own = project_own(query_states, query_proj, k)
    q_far, q_next, q_last = project_sends(query_states, query_proj, k, 16, (2, 1, 3))
    q_parts = [send(q_far, 2), send(q_next, 1), send(q_last, 3)]
    q_total, q_low = call(sum_queries, [((queries, cols), f32), ((queries, cols), bf16)], q_own, *q_parts)
    (inner,) = call(inner_partials, [((docs + 16, 128), f32)], q_total, d_total)
    inner_all = gather_blocks(inner)
    valid = jnp.take(slot_valid[0], negatives).astype(f32)
    weight = query_weight[None, :]
    small = jnp.pad(
        jnp.concatenate([valid, jnp.zeros_like(weight), weight], axis=0), ((0, 7), (0, 0))
    )
    small = jnp.concatenate([small, small], axis=1)
    received, small, neg_rows = lax.optimization_barrier((received, small, neg_rows))

    (hard,) = call(hard_partials, [((16, 128), f32)], received, q_low, neg_rows)
    hard_all = gather_blocks(hard)
    vmem = pl.BlockSpec(memory_space=pltpu.VMEM)
    rows, u_query, g_local, loss = pl.pallas_call(
        softmax_terms,
        in_specs=[vmem] * 13,
        out_specs=[pl.BlockSpec(memory_space=pltpu.HBM), vmem, vmem, vmem],
        out_shape=[
            jax.ShapeDtypeStruct((slots, cols), bf16),
            jax.ShapeDtypeStruct((queries, cols), bf16),
            jax.ShapeDtypeStruct((docs, cols), f32),
            jax.ShapeDtypeStruct((8, 128), f32),
        ],
        scratch_shapes=[pltpu.VMEM((slots, cols), bf16), pltpu.SemaphoreType.DMA((CHUNKS,))],
        compiler_params=params(),
        cost_estimate=cost,
    )(*inner_all, *hard_all, small, neg_rows, received, d_total, q_total)
    arrived = lax.all_to_all(
        rows.reshape(n_dp, cap, cols), "dp", split_axis=0, concat_axis=0, tiled=True
    ).reshape(slots, cols)
    grad_query = project_back(u_query, query_proj, k)
    arrived, grad_query, loss = lax.optimization_barrier((arrived, grad_query, loss[0, :queries]))

    (u_docs,) = call(doc_grads, [((docs, cols), bf16)], arrived, requests, g_local)
    grad_doc = project_back(u_docs, doc_proj, k)
    return (loss, grad_query, grad_doc)


def solution(mesh):
    in_specs = (
        P("dp", "phase"),
        P("dp", "phase"),
        P("phase", None),
        P("phase", None),
        P("dp", None, None),
        P("dp", None),
        P("dp", None),
        P("dp"),
    )
    out_specs = (P("dp"), P("dp", "phase"), P("dp", "phase"))
    return jax.shard_map(local, mesh=mesh, in_specs=in_specs, out_specs=out_specs, check_vma=False)
```

```python
import jax
import jax.numpy as jnp
from jax import lax
from jax.experimental import pallas as pl
from jax.experimental.pallas import tpu as pltpu
from jax.sharding import PartitionSpec as P

scale20 = 20.0
epsilon = 1e-06
f32 = jnp.float32
bf16 = jnp.bfloat16
NT = (((1,), (1,)), ((), ()))
TN = (((0,), (0,)), ((), ()))
N_PHASE = 4
CHUNKS = 4
cost = pl.CostEstimate(flops=10**9, bytes_accessed=10**5, transcendentals=0)


def dot(a, b, dims=(((1,), (0,)), ((), ()))):
    return lax.dot_general(a, b, dims, preferred_element_type=f32)


def params(mib=16):
    return pltpu.CompilerParams(vmem_limit_bytes=mib * 1024 * 1024)


def call(body, outs, *args):
    return pl.pallas_call(
        body,
        out_shape=[jax.ShapeDtypeStruct(s, t) for s, t in outs],
        compiler_params=params(),
        cost_estimate=cost,
    )(*args)


def iota(shape, dim):
    return lax.broadcasted_iota(jnp.int32, shape, dim)


def split_bf16(x):
    hi = x.astype(bf16)
    return hi, (x - hi.astype(f32)).astype(bf16)


def project_sends(x, w, k, mib, order):
    rows, depth = x.shape
    cols = w.shape[1] // N_PHASE
    n = len(order)

    def body(k_ref, x_ref, w_ref, *refs):
        outs, (x_buf, w_buf, out_buf, sem_ref) = refs[:n], refs[n:]

        def load(i):
            start = pl.multiple_of(lax.rem(k_ref[0] + order[i], N_PHASE) * cols, cols)
            return pltpu.make_async_copy(w_ref.at[:, pl.ds(start, cols)], w_buf.at[i], sem_ref.at[i])

        def store(i):
            return pltpu.make_async_copy(out_buf.at[i], outs[i], sem_ref.at[n + i])

        load_x = pltpu.make_async_copy(x_ref, x_buf, sem_ref.at[2 * n])
        load_x.start()
        for i in range(n):
            load(i).start()
        load_x.wait()
        for i in range(n):
            load(i).wait()
            out_buf[i] = dot(x_buf[...], w_buf[i]).astype(bf16)
            store(i).start()
        for i in range(n):
            store(i).wait()

    hbm = pl.BlockSpec(memory_space=pltpu.HBM)
    return pl.pallas_call(
        body,
        in_specs=[pl.BlockSpec(memory_space=pltpu.SMEM), hbm, hbm],
        out_specs=[hbm] * n,
        out_shape=[jax.ShapeDtypeStruct((rows, cols), bf16)] * n,
        scratch_shapes=[
            pltpu.VMEM((rows, depth), bf16),
            pltpu.VMEM((n, depth, cols), bf16),
            pltpu.VMEM((n, rows, cols), bf16),
            pltpu.SemaphoreType.DMA((2 * n + 1,)),
        ],
        compiler_params=params(mib),
        cost_estimate=cost,
    )(k, x, w)


def project_own(x, w, k):
    rows, depth = x.shape
    cols = w.shape[1] // N_PHASE

    def body(k_ref, x_ref, w_ref, own_ref):
        own_ref[...] = dot(x_ref[...], w_ref[...])

    return pl.pallas_call(
        body,
        grid_spec=pltpu.PrefetchScalarGridSpec(
            num_scalar_prefetch=1,
            grid=(1,),
            in_specs=[
                pl.BlockSpec((rows, depth), lambda s, k_ref: (0, 0)),
                pl.BlockSpec((depth, cols), lambda s, k_ref: (0, k_ref[0])),
            ],
            out_specs=pl.BlockSpec((rows, cols), lambda s, k_ref: (0, 0)),
        ),
        out_shape=jax.ShapeDtypeStruct((rows, cols), f32),
        compiler_params=params(),
        cost_estimate=cost,
    )(k, x, w)


def project_back(u, w, k):
    rows, cols = u.shape
    depth = w.shape[0]

    def columns(w_ref, k_ref, s):
        return w_ref[:, pl.ds(pl.multiple_of(lax.rem(k_ref[0] + s, N_PHASE) * cols, cols), cols)]

    def product(*shifts):
        def body(k_ref, *refs):
            block_refs, w_ref, out_ref = refs[-len(shifts) - 2 : -2], refs[-2], refs[-1]
            total = sum(dot(r[...], columns(w_ref, k_ref, s), NT) for s, r in zip(shifts, block_refs))
            if len(refs) > len(shifts) + 2:
                total = refs[0][...] + total
            out_ref[...] = total.astype(out_ref.dtype)

        return body

    def run(body, dtype, *args):
        vmem = pl.BlockSpec(memory_space=pltpu.VMEM)
        return pl.pallas_call(
            body,
            in_specs=[pl.BlockSpec(memory_space=pltpu.SMEM)] + [vmem] * len(args),
            out_specs=vmem,
            out_shape=jax.ShapeDtypeStruct((rows, depth), dtype),
            compiler_params=params(),
            cost_estimate=cost,
        )(k, *args)

    blocks = gather_blocks(u)
    acc = run(product(0), f32, blocks[0], w)
    acc = run(product(3), f32, acc, blocks[3], w)
    return run(product(1, 2), bf16, acc, blocks[1], blocks[2], w)


def send(block, s):
    return lax.ppermute(block, "phase", [(i, (i + s) % N_PHASE) for i in range(N_PHASE)])


def gather_blocks(x):
    return [x] + [
        lax.ppermute(x, "phase", [((i + s) % N_PHASE, i) for i in range(N_PHASE)]) for s in range(1, N_PHASE)
    ]


def sum_refs(refs):
    total = refs[0][...].astype(f32)
    for r in refs[1:]:
        total = total + r[...].astype(f32)
    return total


def sum_queries(own, a, b, c, total_ref, low_ref):
    total = sum_refs((own, a, b, c))
    total_ref[...] = total
    low_ref[...] = total.astype(bf16)


def onehot_rows(request_ref, out_ref):
    docs = out_ref.shape[1]
    slots = out_ref.shape[0]
    onehot = (iota((docs, slots), 0) == request_ref[...]).astype(f32).astype(bf16)
    eye = (iota((docs, docs), 0) == iota((docs, docs), 1)).astype(f32).astype(bf16)
    out_ref[...] = dot(onehot, eye, TN).astype(bf16)


def sum_docs(parts, onehot):
    docs, cols = parts[0].shape
    slots = onehot.shape[0]
    block = slots // CHUNKS

    def body(a, b, c, d, onehot_ref, total_ref, rows_ref, buf_ref, sem_ref):
        total = sum_refs((a, b, c, d))
        total_ref[...] = total
        low = total.astype(bf16)

        def store(i):
            part = pl.ds(i * block, block)
            return pltpu.make_async_copy(buf_ref.at[part], rows_ref.at[part], sem_ref.at[i])

        for i in range(CHUNKS):
            part = slice(i * block, (i + 1) * block)
            buf_ref[part, :] = dot(onehot_ref[part, :], low).astype(bf16)
            store(i).start()
        for i in range(CHUNKS):
            store(i).wait()

    vmem = pl.BlockSpec(memory_space=pltpu.VMEM)
    return pl.pallas_call(
        body,
        in_specs=[vmem] * 5,
        out_specs=[vmem, pl.BlockSpec(memory_space=pltpu.HBM)],
        out_shape=[jax.ShapeDtypeStruct((docs, cols), f32), jax.ShapeDtypeStruct((slots, cols), bf16)],
        scratch_shapes=[pltpu.VMEM((slots, cols), bf16), pltpu.SemaphoreType.DMA((CHUNKS,))],
        compiler_params=params(),
        cost_estimate=cost,
    )(*parts, onehot)


def ones_row_sums(x):
    hi, lo = split_bf16(x)
    ones = jnp.ones((8, x.shape[1]), bf16)
    return dot(ones, hi, NT) + dot(ones, lo, NT)


def inner_partials(q_ref, d_ref, out_ref):
    q = q_ref[...]
    d = d_ref[...]
    q2 = jnp.concatenate([q, q], axis=0)
    docs = d.shape[0]
    out_ref[0:docs, :] = dot(d.astype(bf16), q2.astype(bf16), NT)
    out_ref[docs : docs + 8, :] = ones_row_sums(q2 * q2)
    out_ref[docs + 8 : docs + 16, :] = ones_row_sums(d * d)


def hard_partials(rows_ref, q_ref, neg_ref, out_ref):
    rows = rows_ref[...]
    q = q_ref[...]
    scores = dot(rows, jnp.concatenate([q, q], axis=0), NT)
    wide = rows.astype(f32)
    square = wide * wide
    lanes = scores.shape[1]
    folded = square[:, 0:lanes]
    for s in range(lanes, square.shape[1], lanes):
        folded = folded + square[:, s : s + lanes]
    hi, lo = split_bf16(folded)
    ones = jnp.ones((lanes, lanes), bf16)
    squares = dot(hi, ones) + dot(lo, ones)
    slot = iota(scores.shape, 0)
    for j in range(8):
        hit = slot == neg_ref[j : j + 1, :]
        out_ref[j : j + 1, :] = jnp.sum(jnp.where(hit, scores, 0.0), axis=0, keepdims=True)
        out_ref[8 + j : 9 + j, :] = jnp.sum(jnp.where(hit, squares, 0.0), axis=0, keepdims=True)


def softmax_terms(*refs):
    inner_refs, hard_refs = refs[0:4], refs[4:8]
    small_ref, neg_ref, rows_ref, d_ref, q_ref, out_ref, u_ref, g_ref, loss_ref, buf_ref, sem_ref = refs[8:]
    sums = sum_refs(inner_refs)
    picks = sum_refs(hard_refs)
    docs, queries = d_ref.shape[0], q_ref.shape[0]
    q_scale = lax.rsqrt(sums[docs : docs + 1, :] + epsilon)
    d_scale_row = lax.rsqrt(sums[docs + 8 : docs + 9, :] + epsilon)
    row = iota((docs, 128), 0)
    lane = iota((docs, 128), 1)
    d_scale = jnp.sum(jnp.where(row == lane, d_scale_row, 0.0), axis=1, keepdims=True)
    inner = scale20 * (sums[0:docs, :] * q_scale * d_scale)
    hard_scale = lax.rsqrt(picks[8:16, :] + epsilon)
    hard = scale20 * (picks[0:8, :] * q_scale * hard_scale)
    valid = small_ref[0:8, :]
    weight = scale20 * small_ref[8:9, :]
    hard_exp = jnp.exp(hard) * valid
    inner_exp = jnp.exp(inner)
    total = jnp.sum(inner_exp, axis=0, keepdims=True) + jnp.sum(hard_exp, axis=0, keepdims=True)
    own = row == lax.bitwise_and(lane, 63)
    positive = jnp.sum(jnp.where(own, inner, 0.0), axis=0, keepdims=True)
    loss_ref[...] = jnp.broadcast_to(jnp.log(total) - positive, loss_ref.shape)
    factor = weight / total
    grad = (factor * inner_exp - jnp.where(own, weight, 0.0)).astype(bf16)
    wide_grad = grad.astype(f32)
    hard_grad = factor * hard_exp
    hard_dot = hard_grad * hard * (1.0 / scale20)
    products = wide_grad * inner * (1.0 / scale20)
    q_dot = jnp.sum(products, axis=0, keepdims=True) + jnp.sum(hard_dot, axis=0, keepdims=True)
    d_dot = jnp.sum(jnp.where(lane < 64, products, 0.0), axis=1, keepdims=True)
    sent = hard_scale * jnp.where(iota((8, 128), 1) < 64, hard_grad, hard_dot * hard_scale)
    slots = out_ref.shape[0]
    slot = iota((slots, 128), 0)
    coef = jnp.zeros((slots, 128), f32)
    for j in range(7):
        coef = coef + jnp.where(slot == neg_ref[j : j + 1, :], sent[j : j + 1, :], 0.0)
    coef = coef.astype(bf16)

    eye = iota((queries, 128), 0) == iota((queries, 128), 1)
    q_scale_col = jnp.sum(jnp.where(eye, q_scale, 0.0), axis=1, keepdims=True)
    q_dot_col = jnp.sum(jnp.where(eye, q_dot, 0.0), axis=1, keepdims=True)
    q_unit = q_ref[...] * q_scale_col
    q_low = jnp.concatenate([q_unit.astype(bf16), jnp.zeros(q_ref.shape, bf16)], axis=0)
    second = (iota((128, 128), 0) >= 64).astype(f32).astype(bf16)
    block = slots // CHUNKS

    def store(i):
        part = pl.ds(i * block, block)
        return pltpu.make_async_copy(buf_ref.at[part], out_ref.at[part], sem_ref.at[i])

    for i in range(CHUNKS):
        part = slice(i * block, (i + 1) * block)
        along = dot(coef[part, :], second)
        mixed = dot(coef[part, :], q_low)
        for c in range(0, mixed.shape[1], 128):
            away = along * rows_ref[part, c : c + 128].astype(f32)
            buf_ref[part, c : c + 128] = (mixed[:, c : c + 128] - away).astype(bf16)
        store(i).start()

    d_unit = d_ref[...] * d_scale
    g_query = dot(grad, d_unit.astype(bf16), TN) + dot(coef, rows_ref[...], TN)
    u_ref[...] = (q_scale_col * (g_query[0:queries, :] - q_unit * q_dot_col)).astype(bf16)
    g_ref[...] = d_scale * (dot(grad, q_low) - d_unit * d_dot)
    for i in range(CHUNKS):
        store(i).wait()


def doc_grads(rows_ref, request_ref, g_ref, u_ref):
    docs, slots = g_ref.shape[0], rows_ref.shape[0]
    onehot = (iota((docs, slots), 0) == request_ref[...]).astype(f32).astype(bf16)
    u_ref[...] = (g_ref[...] + dot(onehot, rows_ref[...])).astype(bf16)


def local(
    query_states,
    doc_states,
    query_proj,
    doc_proj,
    document_requests,
    slot_valid,
    neg_slot,
    query_weight,
):
    k = lax.axis_index("phase").astype(jnp.int32).reshape(1)
    queries, docs = query_states.shape[0], doc_states.shape[0]
    cols = query_proj.shape[1] // N_PHASE
    n_dp, cap = document_requests.shape[1:]
    slots = n_dp * cap

    negatives = neg_slot.T
    held = (n_dp - 1 - negatives // cap) * cap + negatives % cap
    neg_rows = jnp.pad(jnp.concatenate([held, held], axis=1), ((0, 1), (0, 0)), constant_values=-1)
    order = [list(range(n_dp - 1, -1, -1))]

    def exchange(rows):
        blocks = rows.reshape(n_dp, cap, cols)
        swapped = lax.all_to_all(
            blocks, "dp", split_axis=0, concat_axis=0, tiled=True, axis_index_groups=order
        )
        return swapped.reshape(slots, cols)

    d_far, d_next, d_last, document_requests = lax.optimization_barrier(
        (*project_sends(doc_states, doc_proj, k, 63, (2, 1, 3)), document_requests)
    )
    requests = document_requests[0, ::-1].reshape(1, slots)
    d_parts = [send(d_far, 2), send(d_next, 1), send(d_last, 3)]
    d_own = project_own(doc_states, doc_proj, k)
    (onehot,) = call(onehot_rows, [((slots, docs), bf16)], requests)
    d_total, outgoing = sum_docs([d_own] + d_parts, onehot)
    outgoing, query_states = lax.optimization_barrier((outgoing, query_states))
    received = exchange(outgoing)

    q_own = project_own(query_states, query_proj, k)
    q_far, q_next, q_last = project_sends(query_states, query_proj, k, 16, (2, 1, 3))
    q_parts = [send(q_far, 2), send(q_next, 1), send(q_last, 3)]
    q_total, q_low = call(sum_queries, [((queries, cols), f32), ((queries, cols), bf16)], q_own, *q_parts)
    (inner,) = call(inner_partials, [((docs + 16, 128), f32)], q_total, d_total)
    inner_all = gather_blocks(inner)
    valid = jnp.take(slot_valid[0], negatives).astype(f32)
    weight = query_weight[None, :]
    small = jnp.pad(
        jnp.concatenate([valid, jnp.zeros_like(weight), weight], axis=0), ((0, 7), (0, 0))
    )
    small = jnp.concatenate([small, small], axis=1)
    received, small, neg_rows = lax.optimization_barrier((received, small, neg_rows))

    (hard,) = call(hard_partials, [((16, 128), f32)], received, q_low, neg_rows)
    hard_all = gather_blocks(hard)
    vmem = pl.BlockSpec(memory_space=pltpu.VMEM)
    rows, u_query, g_local, loss = pl.pallas_call(
        softmax_terms,
        in_specs=[vmem] * 13,
        out_specs=[pl.BlockSpec(memory_space=pltpu.HBM), vmem, vmem, vmem],
        out_shape=[
            jax.ShapeDtypeStruct((slots, cols), bf16),
            jax.ShapeDtypeStruct((queries, cols), bf16),
            jax.ShapeDtypeStruct((docs, cols), f32),
            jax.ShapeDtypeStruct((8, 128), f32),
        ],
        scratch_shapes=[pltpu.VMEM((slots, cols), bf16), pltpu.SemaphoreType.DMA((CHUNKS,))],
        compiler_params=params(),
        cost_estimate=cost,
    )(*inner_all, *hard_all, small, neg_rows, received, d_total, q_total)
    arrived = exchange(rows)
    grad_query = project_back(u_query, query_proj, k)
    arrived, grad_query, loss = lax.optimization_barrier((arrived, grad_query, loss[0, :queries]))

    (u_docs,) = call(doc_grads, [((docs, cols), bf16)], arrived, requests, g_local)
    grad_doc = project_back(u_docs, doc_proj, k)
    return (loss, grad_query, grad_doc)


def solution(mesh):
    in_specs = (
        P("dp", "phase"),
        P("dp", "phase"),
        P("phase", None),
        P("phase", None),
        P("dp", None, None),
        P("dp", None),
        P("dp", None),
        P("dp"),
    )
    out_specs = (P("dp"), P("dp", "phase"), P("dp", "phase"))
    return jax.shard_map(local, mesh=mesh, in_specs=in_specs, out_specs=out_specs, check_vma=False)
```

```python
import jax
import jax.numpy as jnp
from jax import lax
from jax.experimental import pallas as pl
from jax.experimental.pallas import tpu as pltpu
from jax.sharding import PartitionSpec as P

scale20 = 20.0
epsilon = 1e-06
f32 = jnp.float32
bf16 = jnp.bfloat16
NT = (((1,), (1,)), ((), ()))
TN = (((0,), (0,)), ((), ()))
N_PHASE = 4
CHUNKS = 4
cost = pl.CostEstimate(flops=10**9, bytes_accessed=10**5, transcendentals=0)


def dot(a, b, dims=(((1,), (0,)), ((), ()))):
    return lax.dot_general(a, b, dims, preferred_element_type=f32)


def params(mib=16):
    return pltpu.CompilerParams(vmem_limit_bytes=mib * 1024 * 1024)


def call(body, outs, *args):
    return pl.pallas_call(
        body,
        out_shape=[jax.ShapeDtypeStruct(s, t) for s, t in outs],
        compiler_params=params(),
        cost_estimate=cost,
    )(*args)


def iota(shape, dim):
    return lax.broadcasted_iota(jnp.int32, shape, dim)


def split_bf16(x):
    hi = x.astype(bf16)
    return hi, (x - hi.astype(f32)).astype(bf16)


def project_sends(x, w, k, mib, order):
    rows, depth = x.shape
    cols = w.shape[1] // N_PHASE
    n = len(order)

    def body(k_ref, x_ref, w_ref, *refs):
        outs, (x_buf, w_buf, out_buf, sem_ref) = refs[:n], refs[n:]

        def load(i):
            start = pl.multiple_of(lax.rem(k_ref[0] + order[i], N_PHASE) * cols, cols)
            return pltpu.make_async_copy(w_ref.at[:, pl.ds(start, cols)], w_buf.at[i], sem_ref.at[i])

        def store(i):
            return pltpu.make_async_copy(out_buf.at[i], outs[i], sem_ref.at[n + i])

        load_x = pltpu.make_async_copy(x_ref, x_buf, sem_ref.at[2 * n])
        load_x.start()
        for i in range(n):
            load(i).start()
        load_x.wait()
        for i in range(n):
            load(i).wait()
            out_buf[i] = dot(x_buf[...], w_buf[i]).astype(bf16)
            store(i).start()
        for i in range(n):
            store(i).wait()

    hbm = pl.BlockSpec(memory_space=pltpu.HBM)
    return pl.pallas_call(
        body,
        in_specs=[pl.BlockSpec(memory_space=pltpu.SMEM), hbm, hbm],
        out_specs=[hbm] * n,
        out_shape=[jax.ShapeDtypeStruct((rows, cols), bf16)] * n,
        scratch_shapes=[
            pltpu.VMEM((rows, depth), bf16),
            pltpu.VMEM((n, depth, cols), bf16),
            pltpu.VMEM((n, rows, cols), bf16),
            pltpu.SemaphoreType.DMA((2 * n + 1,)),
        ],
        compiler_params=params(mib),
        cost_estimate=cost,
    )(k, x, w)


def project_own(x, w, k):
    rows, depth = x.shape
    cols = w.shape[1] // N_PHASE

    def body(k_ref, x_ref, w_ref, own_ref):
        own_ref[...] = dot(x_ref[...], w_ref[...])

    return pl.pallas_call(
        body,
        grid_spec=pltpu.PrefetchScalarGridSpec(
            num_scalar_prefetch=1,
            grid=(1,),
            in_specs=[
                pl.BlockSpec((rows, depth), lambda s, k_ref: (0, 0)),
                pl.BlockSpec((depth, cols), lambda s, k_ref: (0, k_ref[0])),
            ],
            out_specs=pl.BlockSpec((rows, cols), lambda s, k_ref: (0, 0)),
        ),
        out_shape=jax.ShapeDtypeStruct((rows, cols), f32),
        compiler_params=params(),
        cost_estimate=cost,
    )(k, x, w)


def project_back(u, w, k):
    rows, cols = u.shape
    depth = w.shape[0]

    def columns(w_ref, k_ref, s):
        return w_ref[:, pl.ds(pl.multiple_of(lax.rem(k_ref[0] + s, N_PHASE) * cols, cols), cols)]

    def product(*shifts):
        def body(k_ref, *refs):
            block_refs, w_ref, out_ref = refs[-len(shifts) - 2 : -2], refs[-2], refs[-1]
            total = sum(dot(r[...], columns(w_ref, k_ref, s), NT) for s, r in zip(shifts, block_refs))
            if len(refs) > len(shifts) + 2:
                total = refs[0][...] + total
            out_ref[...] = total.astype(out_ref.dtype)

        return body

    def run(body, dtype, *args):
        vmem = pl.BlockSpec(memory_space=pltpu.VMEM)
        return pl.pallas_call(
            body,
            in_specs=[pl.BlockSpec(memory_space=pltpu.SMEM)] + [vmem] * len(args),
            out_specs=vmem,
            out_shape=jax.ShapeDtypeStruct((rows, depth), dtype),
            compiler_params=params(),
            cost_estimate=cost,
        )(k, *args)

    blocks = gather_blocks(u)
    acc = run(product(0), f32, blocks[0], w)
    acc = run(product(3), f32, acc, blocks[3], w)
    return run(product(1, 2), bf16, acc, blocks[1], blocks[2], w)


def send(block, s):
    return lax.ppermute(block, "phase", [(i, (i + s) % N_PHASE) for i in range(N_PHASE)])


def gather_blocks(x):
    return [x] + [
        lax.ppermute(x, "phase", [((i + s) % N_PHASE, i) for i in range(N_PHASE)]) for s in range(1, N_PHASE)
    ]


def sum_refs(refs):
    total = refs[0][...].astype(f32)
    for r in refs[1:]:
        total = total + r[...].astype(f32)
    return total


def sum_queries(own, a, b, c, total_ref, low_ref):
    total = sum_refs((own, a, b, c))
    total_ref[...] = total
    low_ref[...] = total.astype(bf16)


def onehot_rows(request_ref, out_ref):
    docs = out_ref.shape[1]
    slots = out_ref.shape[0]
    onehot = (iota((docs, slots), 0) == request_ref[...]).astype(f32).astype(bf16)
    eye = (iota((docs, docs), 0) == iota((docs, docs), 1)).astype(f32).astype(bf16)
    out_ref[...] = dot(onehot, eye, TN).astype(bf16)


def sum_docs(parts, onehot):
    docs, cols = parts[0].shape
    slots = onehot.shape[0]
    block = slots // CHUNKS

    def body(a, b, c, d, onehot_ref, total_ref, rows_ref, buf_ref, sem_ref):
        total = sum_refs((a, b, c, d))
        total_ref[...] = total
        low = total.astype(bf16)

        def store(i):
            part = pl.ds(i * block, block)
            return pltpu.make_async_copy(buf_ref.at[part], rows_ref.at[part], sem_ref.at[i])

        for i in range(CHUNKS):
            part = slice(i * block, (i + 1) * block)
            buf_ref[part, :] = dot(onehot_ref[part, :], low).astype(bf16)
            store(i).start()
        for i in range(CHUNKS):
            store(i).wait()

    vmem = pl.BlockSpec(memory_space=pltpu.VMEM)
    return pl.pallas_call(
        body,
        in_specs=[vmem] * 5,
        out_specs=[vmem, pl.BlockSpec(memory_space=pltpu.HBM)],
        out_shape=[jax.ShapeDtypeStruct((docs, cols), f32), jax.ShapeDtypeStruct((slots, cols), bf16)],
        scratch_shapes=[pltpu.VMEM((slots, cols), bf16), pltpu.SemaphoreType.DMA((CHUNKS,))],
        compiler_params=params(),
        cost_estimate=cost,
    )(*parts, onehot)


def ones_row_sums(x):
    hi, lo = split_bf16(x)
    ones = jnp.ones((8, x.shape[1]), bf16)
    return dot(ones, hi, NT) + dot(ones, lo, NT)


def inner_partials(q_ref, d_ref, out_ref):
    q = q_ref[...]
    d = d_ref[...]
    q2 = jnp.concatenate([q, q], axis=0)
    docs = d.shape[0]
    out_ref[0:docs, :] = dot(d.astype(bf16), q2.astype(bf16), NT)
    out_ref[docs : docs + 8, :] = ones_row_sums(q2 * q2)
    out_ref[docs + 8 : docs + 16, :] = ones_row_sums(d * d)


def hard_partials(rows_ref, q_ref, neg_ref, out_ref):
    rows = rows_ref[...]
    q = q_ref[...]
    wide = rows.astype(f32)
    square = wide * wide
    folded = square[:, 0:128]
    for s in range(128, square.shape[1], 128):
        folded = folded + square[:, s : s + 128]
    hi, lo = split_bf16(folded)
    upper = (iota((128, 128), 1) >= 64).astype(f32).astype(bf16)
    both = dot(rows, jnp.concatenate([q, jnp.zeros_like(q)], axis=0), NT) + dot(hi, upper) + dot(lo, upper)
    slot = iota(both.shape, 0)
    for j in range(8):
        hit = slot == neg_ref[j : j + 1, :]
        out_ref[j : j + 1, :] = jnp.sum(jnp.where(hit, both, 0.0), axis=0, keepdims=True)


def softmax_terms(*refs):
    inner_refs, hard_refs = refs[0:4], refs[4:8]
    small_ref, neg_ref, rows_ref, q_ref, out_ref, coef_ref, grad_ref, row_ref, col_ref, buf_ref, sem_ref = refs[8:]
    sums = sum_refs(inner_refs)
    picks = sum_refs(hard_refs)
    docs, queries = grad_ref.shape[0], q_ref.shape[0]
    swapped = pltpu.roll(picks, 64, 1)
    low_lane = iota(picks.shape, 1) < 64
    scores = jnp.where(low_lane, picks, swapped)
    squares = jnp.where(low_lane, swapped, picks)
    q_scale = lax.rsqrt(sums[docs : docs + 1, :] + epsilon)
    d_scale_row = lax.rsqrt(sums[docs + 8 : docs + 9, :] + epsilon)
    row = iota((docs, 128), 0)
    lane = iota((docs, 128), 1)
    d_scale = jnp.sum(jnp.where(row == lane, d_scale_row, 0.0), axis=1, keepdims=True)
    inner = scale20 * (sums[0:docs, :] * q_scale * d_scale)
    hard_scale = lax.rsqrt(squares + epsilon)
    hard = scale20 * (scores * q_scale * hard_scale)
    valid = small_ref[0:8, :]
    weight = scale20 * small_ref[8:9, :]
    hard_exp = jnp.exp(hard) * valid
    inner_exp = jnp.exp(inner)
    total = jnp.sum(inner_exp, axis=0, keepdims=True) + jnp.sum(hard_exp, axis=0, keepdims=True)
    own = row == lax.bitwise_and(lane, 63)
    positive = jnp.sum(jnp.where(own, inner, 0.0), axis=0, keepdims=True)
    factor = weight / total
    hard_grad = factor * hard_exp
    hard_dot = hard_grad * hard * (1.0 / scale20)
    sent = hard_scale * jnp.where(low_lane, hard_grad, hard_dot * hard_scale)
    slots = out_ref.shape[0]
    slot = iota((slots, 128), 0)
    coef = jnp.zeros((slots, 128), f32)
    for j in range(7):
        coef = coef + jnp.where(slot == neg_ref[j : j + 1, :], sent[j : j + 1, :], 0.0)
    coef = coef.astype(bf16)
    coef_ref[...] = coef

    eye = iota((queries, 128), 0) == iota((queries, 128), 1)
    q_scale_col = jnp.sum(jnp.where(eye, q_scale, 0.0), axis=1, keepdims=True)
    q_low = (q_ref[...] * q_scale_col).astype(bf16)
    q_low = jnp.concatenate([q_low, jnp.zeros_like(q_low)], axis=0)
    second = (iota((128, 128), 0) >= 64).astype(f32).astype(bf16)
    block = slots // CHUNKS

    def store(i):
        part = pl.ds(i * block, block)
        return pltpu.make_async_copy(buf_ref.at[part], out_ref.at[part], sem_ref.at[i])

    for i in range(CHUNKS):
        part = slice(i * block, (i + 1) * block)
        along = dot(coef[part, :], second)
        mixed = dot(coef[part, :], q_low)
        for c in range(0, mixed.shape[1], 128):
            away = along * rows_ref[part, c : c + 128].astype(f32)
            buf_ref[part, c : c + 128] = (mixed[:, c : c + 128] - away).astype(bf16)
        store(i).start()

    grad = (factor * inner_exp - jnp.where(own, weight, 0.0)).astype(bf16)
    grad_ref[...] = grad
    products = grad.astype(f32) * inner * (1.0 / scale20)
    q_dot = jnp.sum(products, axis=0, keepdims=True) + jnp.sum(hard_dot, axis=0, keepdims=True)
    d_dot = jnp.sum(jnp.where(lane < 64, products, 0.0), axis=1, keepdims=True)
    row_ref[...] = jnp.zeros_like(row_ref)
    row_ref[0:1, :] = jnp.log(total) - positive
    row_ref[1:2, :] = q_scale
    row_ref[2:3, :] = q_dot
    col_ref[...] = jnp.where(lane == 0, d_scale, d_dot)
    for i in range(CHUNKS):
        store(i).wait()


def local_grads(coef_ref, grad_ref, row_ref, col_ref, rows_ref, d_ref, q_ref, u_ref, g_ref):
    queries = q_ref.shape[0]
    d_scale = col_ref[:, 0:1]
    d_dot = col_ref[:, 1:2]
    eye = iota((queries, 128), 0) == iota((queries, 128), 1)
    q_scale = jnp.sum(jnp.where(eye, row_ref[1:2, :], 0.0), axis=1, keepdims=True)
    q_dot = jnp.sum(jnp.where(eye, row_ref[2:3, :], 0.0), axis=1, keepdims=True)
    q_unit = q_ref[...] * q_scale
    q_low = q_unit.astype(bf16)
    q_low = jnp.concatenate([q_low, jnp.zeros_like(q_low)], axis=0)
    d_unit = d_ref[...] * d_scale
    grad = grad_ref[...]
    g_query = dot(grad, d_unit.astype(bf16), TN) + dot(coef_ref[...], rows_ref[...], TN)
    u_ref[...] = (q_scale * (g_query[0:queries, :] - q_unit * q_dot)).astype(bf16)
    g_ref[...] = d_scale * (dot(grad, q_low) - d_unit * d_dot)


def doc_grads(rows_ref, request_ref, g_ref, u_ref):
    docs, slots = g_ref.shape[0], rows_ref.shape[0]
    onehot = (iota((docs, slots), 0) == request_ref[...]).astype(f32).astype(bf16)
    u_ref[...] = (g_ref[...] + dot(onehot, rows_ref[...])).astype(bf16)


def local(
    query_states,
    doc_states,
    query_proj,
    doc_proj,
    document_requests,
    slot_valid,
    neg_slot,
    query_weight,
):
    k = lax.axis_index("phase").astype(jnp.int32).reshape(1)
    queries, docs = query_states.shape[0], doc_states.shape[0]
    cols = query_proj.shape[1] // N_PHASE
    n_dp, cap = document_requests.shape[1:]
    slots = n_dp * cap

    negatives = neg_slot.T
    held = (n_dp - 1 - negatives // cap) * cap + negatives % cap
    neg_rows = jnp.pad(jnp.concatenate([held, held], axis=1), ((0, 1), (0, 0)), constant_values=-1)
    order = [list(range(n_dp - 1, -1, -1))]

    def exchange(rows):
        blocks = rows.reshape(n_dp, cap, cols)
        swapped = lax.all_to_all(
            blocks, "dp", split_axis=0, concat_axis=0, tiled=True, axis_index_groups=order
        )
        return swapped.reshape(slots, cols)

    d_far, d_next, d_last, document_requests = lax.optimization_barrier(
        (*project_sends(doc_states, doc_proj, k, 63, (2, 1, 3)), document_requests)
    )
    requests = document_requests[0, ::-1].reshape(1, slots)
    d_parts = [send(d_far, 2), send(d_next, 1), send(d_last, 3)]
    d_own = project_own(doc_states, doc_proj, k)
    (onehot,) = call(onehot_rows, [((slots, docs), bf16)], requests)
    d_total, outgoing = sum_docs([d_own] + d_parts, onehot)
    outgoing, query_states = lax.optimization_barrier((outgoing, query_states))
    received = exchange(outgoing)

    q_own = project_own(query_states, query_proj, k)
    q_far, q_next, q_last = project_sends(query_states, query_proj, k, 16, (2, 1, 3))
    q_parts = [send(q_far, 2), send(q_next, 1), send(q_last, 3)]
    q_total, q_low = call(sum_queries, [((queries, cols), f32), ((queries, cols), bf16)], q_own, *q_parts)
    (inner,) = call(inner_partials, [((docs + 16, 128), f32)], q_total, d_total)
    inner_all = gather_blocks(inner)
    valid = jnp.take(slot_valid[0], negatives).astype(f32)
    weight = query_weight[None, :]
    small = jnp.pad(
        jnp.concatenate([valid, jnp.zeros_like(weight), weight], axis=0), ((0, 7), (0, 0))
    )
    small = jnp.concatenate([small, small], axis=1)
    received, small, neg_rows = lax.optimization_barrier((received, small, neg_rows))

    (hard,) = call(hard_partials, [((8, 128), f32)], received, q_low, neg_rows)
    hard_all = gather_blocks(hard)
    vmem = pl.BlockSpec(memory_space=pltpu.VMEM)
    rows, coef, grad, by_query, by_doc = pl.pallas_call(
        softmax_terms,
        in_specs=[vmem] * 12,
        out_specs=[pl.BlockSpec(memory_space=pltpu.HBM)] + [vmem] * 4,
        out_shape=[
            jax.ShapeDtypeStruct((slots, cols), bf16),
            jax.ShapeDtypeStruct((slots, 128), bf16),
            jax.ShapeDtypeStruct((docs, 128), bf16),
            jax.ShapeDtypeStruct((8, 128), f32),
            jax.ShapeDtypeStruct((docs, 128), f32),
        ],
        scratch_shapes=[pltpu.VMEM((slots, cols), bf16), pltpu.SemaphoreType.DMA((CHUNKS,))],
        compiler_params=params(),
        cost_estimate=cost,
    )(*inner_all, *hard_all, small, neg_rows, received, q_total)
    arrived = exchange(rows)
    u_query, g_local = call(
        local_grads,
        [((queries, cols), bf16), ((docs, cols), f32)],
        coef,
        grad,
        by_query,
        by_doc,
        received,
        d_total,
        q_total,
    )
    grad_query = project_back(u_query, query_proj, k)
    arrived, grad_query, loss = lax.optimization_barrier((arrived, grad_query, by_query[0, :queries]))

    (u_docs,) = call(doc_grads, [((docs, cols), bf16)], arrived, requests, g_local)
    grad_doc = project_back(u_docs, doc_proj, k)
    return (loss, grad_query, grad_doc)


def solution(mesh):
    in_specs = (
        P("dp", "phase"),
        P("dp", "phase"),
        P("phase", None),
        P("phase", None),
        P("dp", None, None),
        P("dp", None),
        P("dp", None),
        P("dp"),
    )
    out_specs = (P("dp"), P("dp", "phase"), P("dp", "phase"))
    return jax.shard_map(local, mesh=mesh, in_specs=in_specs, out_specs=out_specs, check_vma=False)
```

```python
import jax
import jax.numpy as jnp
from jax import lax
from jax.experimental import pallas as pl
from jax.experimental.pallas import tpu as pltpu
from jax.sharding import PartitionSpec as P

scale20 = 20.0
epsilon = 1e-06
f32 = jnp.float32
bf16 = jnp.bfloat16
NT = (((1,), (1,)), ((), ()))
TN = (((0,), (0,)), ((), ()))
N_PHASE = 4
CHUNKS = 4
cost = pl.CostEstimate(flops=10**9, bytes_accessed=10**5, transcendentals=0)


def dot(a, b, dims=(((1,), (0,)), ((), ()))):
    return lax.dot_general(a, b, dims, preferred_element_type=f32)


def params(mib=16):
    return pltpu.CompilerParams(vmem_limit_bytes=mib * 1024 * 1024)


def call(body, outs, *args):
    return pl.pallas_call(
        body,
        out_shape=[jax.ShapeDtypeStruct(s, t) for s, t in outs],
        compiler_params=params(),
        cost_estimate=cost,
    )(*args)


def iota(shape, dim):
    return lax.broadcasted_iota(jnp.int32, shape, dim)


def split_bf16(x):
    hi = x.astype(bf16)
    return hi, (x - hi.astype(f32)).astype(bf16)


def project_sends(x, w, k, mib, order):
    rows, depth = x.shape
    cols = w.shape[1] // N_PHASE
    n = len(order)

    def body(k_ref, x_ref, w_ref, *refs):
        outs, (x_buf, w_buf, out_buf, sem_ref) = refs[:n], refs[n:]

        def load(i):
            start = pl.multiple_of(lax.rem(k_ref[0] + order[i], N_PHASE) * cols, cols)
            return pltpu.make_async_copy(w_ref.at[:, pl.ds(start, cols)], w_buf.at[i], sem_ref.at[i])

        def store(i):
            return pltpu.make_async_copy(out_buf.at[i], outs[i], sem_ref.at[n + i])

        load_x = pltpu.make_async_copy(x_ref, x_buf, sem_ref.at[2 * n])
        load_x.start()
        for i in range(n):
            load(i).start()
        load_x.wait()
        for i in range(n):
            load(i).wait()
            out_buf[i] = dot(x_buf[...], w_buf[i]).astype(bf16)
            store(i).start()
        for i in range(n):
            store(i).wait()

    hbm = pl.BlockSpec(memory_space=pltpu.HBM)
    return pl.pallas_call(
        body,
        in_specs=[pl.BlockSpec(memory_space=pltpu.SMEM), hbm, hbm],
        out_specs=[hbm] * n,
        out_shape=[jax.ShapeDtypeStruct((rows, cols), bf16)] * n,
        scratch_shapes=[
            pltpu.VMEM((rows, depth), bf16),
            pltpu.VMEM((n, depth, cols), bf16),
            pltpu.VMEM((n, rows, cols), bf16),
            pltpu.SemaphoreType.DMA((2 * n + 1,)),
        ],
        compiler_params=params(mib),
        cost_estimate=cost,
    )(k, x, w)


def project_own(x, w, k):
    rows, depth = x.shape
    cols = w.shape[1] // N_PHASE

    def body(k_ref, x_ref, w_ref, own_ref):
        own_ref[...] = dot(x_ref[...], w_ref[...])

    return pl.pallas_call(
        body,
        grid_spec=pltpu.PrefetchScalarGridSpec(
            num_scalar_prefetch=1,
            grid=(1,),
            in_specs=[
                pl.BlockSpec((rows, depth), lambda s, k_ref: (0, 0)),
                pl.BlockSpec((depth, cols), lambda s, k_ref: (0, k_ref[0])),
            ],
            out_specs=pl.BlockSpec((rows, cols), lambda s, k_ref: (0, 0)),
        ),
        out_shape=jax.ShapeDtypeStruct((rows, cols), f32),
        compiler_params=params(),
        cost_estimate=cost,
    )(k, x, w)


def project_back(u, w, k):
    rows, cols = u.shape
    depth = w.shape[0]

    def columns(w_ref, k_ref, s):
        return w_ref[:, pl.ds(pl.multiple_of(lax.rem(k_ref[0] + s, N_PHASE) * cols, cols), cols)]

    vmem = pl.BlockSpec(memory_space=pltpu.VMEM)
    smem = pl.BlockSpec(memory_space=pltpu.SMEM)

    def product(s, acc, block):
        def body(k_ref, *refs):
            acc_refs, block_ref, w_ref, out_ref = refs[:-3], refs[-3], refs[-2], refs[-1]
            part = dot(block_ref[...], columns(w_ref, k_ref, s), NT)
            out_ref[...] = part + acc_refs[0][...] if acc_refs else part

        args = acc + [block, w]
        return pl.pallas_call(
            body,
            in_specs=[smem] + [vmem] * len(args),
            out_specs=vmem,
            out_shape=jax.ShapeDtypeStruct((rows, depth), f32),
            compiler_params=params(),
            cost_estimate=cost,
        )(k, *args)

    def last(k_ref, acc_ref, block_ref, w_ref, out_ref, buf_ref, sem_ref):
        half = depth // 2
        start = pl.multiple_of(lax.rem(k_ref[0] + 2, N_PHASE) * cols, cols)

        def store(i):
            return pltpu.make_async_copy(buf_ref.at[i], out_ref.at[:, pl.ds(i * half, half)], sem_ref.at[i])

        for i in range(2):
            part = slice(i * half, (i + 1) * half)
            total = acc_ref[:, part] + dot(block_ref[...], w_ref[part, pl.ds(start, cols)], NT)
            buf_ref[i] = total.astype(bf16)
            store(i).start()
        for i in range(2):
            store(i).wait()

    blocks = gather_blocks(u)
    acc = product(0, [], blocks[0])
    acc = product(1, [acc], blocks[1])
    acc = product(3, [acc], blocks[3])
    return pl.pallas_call(
        last,
        in_specs=[smem] + [vmem] * 3,
        out_specs=pl.BlockSpec(memory_space=pltpu.HBM),
        out_shape=jax.ShapeDtypeStruct((rows, depth), bf16),
        scratch_shapes=[pltpu.VMEM((2, rows, depth // 2), bf16), pltpu.SemaphoreType.DMA((2,))],
        compiler_params=params(),
        cost_estimate=cost,
    )(k, acc, blocks[2], w)


def send(block, s):
    return lax.ppermute(block, "phase", [(i, (i + s) % N_PHASE) for i in range(N_PHASE)])


def gather_blocks(x):
    return [x] + [
        lax.ppermute(x, "phase", [((i + s) % N_PHASE, i) for i in range(N_PHASE)]) for s in range(1, N_PHASE)
    ]


def sum_refs(refs):
    total = refs[0][...].astype(f32)
    for r in refs[1:]:
        total = total + r[...].astype(f32)
    return total


def sum_queries(own, a, b, c, total_ref, low_ref):
    total = sum_refs((own, a, b, c))
    total_ref[...] = total
    low_ref[...] = total.astype(bf16)


def onehot_rows(request_ref, out_ref):
    docs = out_ref.shape[1]
    slots = out_ref.shape[0]
    onehot = (iota((docs, slots), 0) == request_ref[...]).astype(f32).astype(bf16)
    eye = (iota((docs, docs), 0) == iota((docs, docs), 1)).astype(f32).astype(bf16)
    out_ref[...] = dot(onehot, eye, TN).astype(bf16)


def sum_docs(parts, onehot):
    docs, cols = parts[0].shape
    slots = onehot.shape[0]
    block = slots // CHUNKS

    def body(a, b, c, d, onehot_ref, total_ref, rows_ref, buf_ref, sem_ref):
        total = sum_refs((a, b, c, d))
        total_ref[...] = total
        low = total.astype(bf16)

        def store(i):
            part = pl.ds(i * block, block)
            return pltpu.make_async_copy(buf_ref.at[part], rows_ref.at[part], sem_ref.at[i])

        for i in range(CHUNKS):
            part = slice(i * block, (i + 1) * block)
            buf_ref[part, :] = dot(onehot_ref[part, :], low).astype(bf16)
            store(i).start()
        for i in range(CHUNKS):
            store(i).wait()

    vmem = pl.BlockSpec(memory_space=pltpu.VMEM)
    return pl.pallas_call(
        body,
        in_specs=[vmem] * 5,
        out_specs=[vmem, pl.BlockSpec(memory_space=pltpu.HBM)],
        out_shape=[jax.ShapeDtypeStruct((docs, cols), f32), jax.ShapeDtypeStruct((slots, cols), bf16)],
        scratch_shapes=[pltpu.VMEM((slots, cols), bf16), pltpu.SemaphoreType.DMA((CHUNKS,))],
        compiler_params=params(),
        cost_estimate=cost,
    )(*parts, onehot)


def ones_row_sums(x):
    hi, lo = split_bf16(x)
    ones = jnp.ones((8, x.shape[1]), bf16)
    return dot(ones, hi, NT) + dot(ones, lo, NT)


def inner_partials(q_ref, d_ref, out_ref):
    q = q_ref[...]
    d = d_ref[...]
    q2 = jnp.concatenate([q, q], axis=0)
    docs = d.shape[0]
    out_ref[0:docs, :] = dot(d.astype(bf16), q2.astype(bf16), NT)
    out_ref[docs : docs + 8, :] = ones_row_sums(q2 * q2)
    out_ref[docs + 8 : docs + 16, :] = ones_row_sums(d * d)


def hard_partials(rows_ref, q_ref, neg_ref, out_ref):
    rows = rows_ref[...]
    q = q_ref[...]
    wide = rows.astype(f32)
    square = wide * wide
    folded = square[:, 0:128]
    for s in range(128, square.shape[1], 128):
        folded = folded + square[:, s : s + 128]
    hi, lo = split_bf16(folded)
    upper = (iota((128, 128), 1) >= 64).astype(f32).astype(bf16)
    both = dot(rows, jnp.concatenate([q, jnp.zeros_like(q)], axis=0), NT) + dot(hi, upper) + dot(lo, upper)
    slot = iota(both.shape, 0)
    for j in range(8):
        hit = slot == neg_ref[j : j + 1, :]
        out_ref[j : j + 1, :] = jnp.sum(jnp.where(hit, both, 0.0), axis=0, keepdims=True)


def softmax_terms(*refs):
    inner_refs, hard_refs = refs[0:4], refs[4:8]
    small_ref, neg_ref, rows_ref, q_ref, out_ref, coef_ref, grad_ref, row_ref, col_ref, buf_ref, sem_ref = refs[8:]
    sums = sum_refs(inner_refs)
    picks = sum_refs(hard_refs)
    docs, queries = grad_ref.shape[0], q_ref.shape[0]
    swapped = pltpu.roll(picks, 64, 1)
    low_lane = iota(picks.shape, 1) < 64
    scores = jnp.where(low_lane, picks, swapped)
    squares = jnp.where(low_lane, swapped, picks)
    q_scale = lax.rsqrt(sums[docs : docs + 1, :] + epsilon)
    d_scale_row = lax.rsqrt(sums[docs + 8 : docs + 9, :] + epsilon)
    row = iota((docs, 128), 0)
    lane = iota((docs, 128), 1)
    d_scale = jnp.sum(jnp.where(row == lane, d_scale_row, 0.0), axis=1, keepdims=True)
    inner = scale20 * (sums[0:docs, :] * q_scale * d_scale)
    hard_scale = lax.rsqrt(squares + epsilon)
    hard = scale20 * (scores * q_scale * hard_scale)
    valid = small_ref[0:8, :]
    weight = scale20 * small_ref[8:9, :]
    hard_exp = jnp.exp(hard) * valid
    inner_exp = jnp.exp(inner)
    total = jnp.sum(inner_exp, axis=0, keepdims=True) + jnp.sum(hard_exp, axis=0, keepdims=True)
    own = row == lax.bitwise_and(lane, 63)
    positive = jnp.sum(jnp.where(own, inner, 0.0), axis=0, keepdims=True)
    factor = weight / total
    hard_grad = factor * hard_exp
    hard_dot = hard_grad * hard * (1.0 / scale20)
    sent = hard_scale * jnp.where(low_lane, hard_grad, hard_dot * hard_scale)
    slots = out_ref.shape[0]
    slot = iota((slots, 128), 0)
    coef = jnp.zeros((slots, 128), f32)
    for j in range(7):
        coef = coef + jnp.where(slot == neg_ref[j : j + 1, :], sent[j : j + 1, :], 0.0)
    coef = coef.astype(bf16)
    coef_ref[...] = coef

    eye = iota((queries, 128), 0) == iota((queries, 128), 1)
    q_scale_col = jnp.sum(jnp.where(eye, q_scale, 0.0), axis=1, keepdims=True)
    q_low = (q_ref[...] * q_scale_col).astype(bf16)
    q_low = jnp.concatenate([q_low, jnp.zeros_like(q_low)], axis=0)
    second = (iota((128, 128), 0) >= 64).astype(f32).astype(bf16)
    block = slots // CHUNKS

    def store(i):
        part = pl.ds(i * block, block)
        return pltpu.make_async_copy(buf_ref.at[part], out_ref.at[part], sem_ref.at[i])

    for i in range(CHUNKS):
        part = slice(i * block, (i + 1) * block)
        along = dot(coef[part, :], second)
        mixed = dot(coef[part, :], q_low)
        for c in range(0, mixed.shape[1], 128):
            away = along * rows_ref[part, c : c + 128].astype(f32)
            buf_ref[part, c : c + 128] = (mixed[:, c : c + 128] - away).astype(bf16)
        store(i).start()

    grad = (factor * inner_exp - jnp.where(own, weight, 0.0)).astype(bf16)
    grad_ref[...] = grad
    products = grad.astype(f32) * inner * (1.0 / scale20)
    q_dot = jnp.sum(products, axis=0, keepdims=True) + jnp.sum(hard_dot, axis=0, keepdims=True)
    d_dot = jnp.sum(jnp.where(lane < 64, products, 0.0), axis=1, keepdims=True)
    row_ref[...] = jnp.zeros_like(row_ref)
    row_ref[0:1, :] = jnp.log(total) - positive
    row_ref[1:2, :] = q_scale
    row_ref[2:3, :] = q_dot
    col_ref[...] = jnp.where(lane == 0, d_scale, d_dot)
    for i in range(CHUNKS):
        store(i).wait()


def local_grads(coef_ref, grad_ref, row_ref, col_ref, rows_ref, d_ref, q_ref, u_ref, g_ref):
    queries = q_ref.shape[0]
    d_scale = col_ref[:, 0:1]
    d_dot = col_ref[:, 1:2]
    eye = iota((queries, 128), 0) == iota((queries, 128), 1)
    q_scale = jnp.sum(jnp.where(eye, row_ref[1:2, :], 0.0), axis=1, keepdims=True)
    q_dot = jnp.sum(jnp.where(eye, row_ref[2:3, :], 0.0), axis=1, keepdims=True)
    q_unit = q_ref[...] * q_scale
    q_low = q_unit.astype(bf16)
    q_low = jnp.concatenate([q_low, jnp.zeros_like(q_low)], axis=0)
    d_unit = d_ref[...] * d_scale
    grad = grad_ref[...]
    g_query = dot(grad, d_unit.astype(bf16), TN) + dot(coef_ref[...], rows_ref[...], TN)
    u_ref[...] = (q_scale * (g_query[0:queries, :] - q_unit * q_dot)).astype(bf16)
    g_ref[...] = d_scale * (dot(grad, q_low) - d_unit * d_dot)


def doc_grads(rows_ref, request_ref, g_ref, u_ref):
    docs, slots = g_ref.shape[0], rows_ref.shape[0]
    onehot = (iota((docs, slots), 0) == request_ref[...]).astype(f32).astype(bf16)
    u_ref[...] = (g_ref[...] + dot(onehot, rows_ref[...])).astype(bf16)


def local(
    query_states,
    doc_states,
    query_proj,
    doc_proj,
    document_requests,
    slot_valid,
    neg_slot,
    query_weight,
):
    k = lax.axis_index("phase").astype(jnp.int32).reshape(1)
    queries, docs = query_states.shape[0], doc_states.shape[0]
    cols = query_proj.shape[1] // N_PHASE
    n_dp, cap = document_requests.shape[1:]
    slots = n_dp * cap

    negatives = neg_slot.T
    held = (n_dp - 1 - negatives // cap) * cap + negatives % cap
    neg_rows = jnp.pad(jnp.concatenate([held, held], axis=1), ((0, 1), (0, 0)), constant_values=-1)
    order = [list(range(n_dp - 1, -1, -1))]

    def exchange(rows):
        blocks = rows.reshape(n_dp, cap, cols)
        swapped = lax.all_to_all(
            blocks, "dp", split_axis=0, concat_axis=0, tiled=True, axis_index_groups=order
        )
        return swapped.reshape(slots, cols)

    d_far, d_next, d_last, document_requests = lax.optimization_barrier(
        (*project_sends(doc_states, doc_proj, k, 63, (2, 1, 3)), document_requests)
    )
    requests = document_requests[0, ::-1].reshape(1, slots)
    d_parts = [send(d_far, 2), send(d_next, 1), send(d_last, 3)]
    d_own = project_own(doc_states, doc_proj, k)
    (onehot,) = call(onehot_rows, [((slots, docs), bf16)], requests)
    d_total, outgoing = sum_docs([d_own] + d_parts, onehot)
    outgoing, query_states = lax.optimization_barrier((outgoing, query_states))
    received = exchange(outgoing)

    q_own = project_own(query_states, query_proj, k)
    q_far, q_next, q_last = project_sends(query_states, query_proj, k, 16, (2, 1, 3))
    q_parts = [send(q_far, 2), send(q_next, 1), send(q_last, 3)]
    q_total, q_low = call(sum_queries, [((queries, cols), f32), ((queries, cols), bf16)], q_own, *q_parts)
    (inner,) = call(inner_partials, [((docs + 16, 128), f32)], q_total, d_total)
    inner_all = gather_blocks(inner)
    valid = jnp.take(slot_valid[0], negatives).astype(f32)
    weight = query_weight[None, :]
    small = jnp.pad(
        jnp.concatenate([valid, jnp.zeros_like(weight), weight], axis=0), ((0, 7), (0, 0))
    )
    small = jnp.concatenate([small, small], axis=1)
    received, small, neg_rows = lax.optimization_barrier((received, small, neg_rows))

    (hard,) = call(hard_partials, [((8, 128), f32)], received, q_low, neg_rows)
    hard_all = gather_blocks(hard)
    vmem = pl.BlockSpec(memory_space=pltpu.VMEM)
    rows, coef, grad, by_query, by_doc = pl.pallas_call(
        softmax_terms,
        in_specs=[vmem] * 12,
        out_specs=[pl.BlockSpec(memory_space=pltpu.HBM)] + [vmem] * 4,
        out_shape=[
            jax.ShapeDtypeStruct((slots, cols), bf16),
            jax.ShapeDtypeStruct((slots, 128), bf16),
            jax.ShapeDtypeStruct((docs, 128), bf16),
            jax.ShapeDtypeStruct((8, 128), f32),
            jax.ShapeDtypeStruct((docs, 128), f32),
        ],
        scratch_shapes=[pltpu.VMEM((slots, cols), bf16), pltpu.SemaphoreType.DMA((CHUNKS,))],
        compiler_params=params(),
        cost_estimate=cost,
    )(*inner_all, *hard_all, small, neg_rows, received, q_total)
    arrived = exchange(rows)
    u_query, g_local = call(
        local_grads,
        [((queries, cols), bf16), ((docs, cols), f32)],
        coef,
        grad,
        by_query,
        by_doc,
        received,
        d_total,
        q_total,
    )
    grad_query = project_back(u_query, query_proj, k)
    arrived, grad_query, loss = lax.optimization_barrier((arrived, grad_query, by_query[0, :queries]))

    (u_docs,) = call(doc_grads, [((docs, cols), bf16)], arrived, requests, g_local)
    grad_doc = project_back(u_docs, doc_proj, k)
    return (loss, grad_query, grad_doc)


def solution(mesh):
    in_specs = (
        P("dp", "phase"),
        P("dp", "phase"),
        P("phase", None),
        P("phase", None),
        P("dp", None, None),
        P("dp", None),
        P("dp", None),
        P("dp"),
    )
    out_specs = (P("dp"), P("dp", "phase"), P("dp", "phase"))
    return jax.shard_map(local, mesh=mesh, in_specs=in_specs, out_specs=out_specs, check_vma=False)
```

```python
import jax
import jax.numpy as jnp
from jax import lax
from jax.experimental import pallas as pl
from jax.experimental.pallas import tpu as pltpu
from jax.sharding import PartitionSpec as P

scale20 = 20.0
epsilon = 1e-06
f32 = jnp.float32
bf16 = jnp.bfloat16
NT = (((1,), (1,)), ((), ()))
TN = (((0,), (0,)), ((), ()))
N_PHASE = 4
CHUNKS = 4
DP_ORDER = [45, 29, 43, 61, 34, 33, 31, 40, 26, 62, 22, 2, 11, 28, 54, 4, 10, 35, 52, 46, 30, 7, 14, 27, 63, 55, 41, 42, 58, 18, 60, 32, 15, 5, 16, 20, 56, 8, 13, 25, 37, 17, 48, 51, 57, 38, 1, 12, 49, 24, 6, 23, 36, 50, 21, 19, 9, 39, 59, 3, 0, 53, 47, 44]
DP_PLACE = [60, 46, 11, 59, 15, 33, 50, 21, 37, 56, 16, 12, 47, 38, 22, 32, 34, 41, 29, 55, 35, 54, 10, 51, 49, 39, 8, 23, 13, 1, 20, 6, 31, 5, 4, 17, 52, 40, 45, 57, 7, 26, 27, 2, 63, 0, 19, 62, 42, 48, 53, 43, 18, 61, 14, 25, 36, 44, 28, 58, 30, 3, 9, 24]
cost = pl.CostEstimate(flops=10**9, bytes_accessed=10**5, transcendentals=0)


def dot(a, b, dims=(((1,), (0,)), ((), ()))):
    return lax.dot_general(a, b, dims, preferred_element_type=f32)


def params(mib=16):
    return pltpu.CompilerParams(vmem_limit_bytes=mib * 1024 * 1024)


def call(body, outs, *args):
    return pl.pallas_call(
        body,
        out_shape=[jax.ShapeDtypeStruct(s, t) for s, t in outs],
        compiler_params=params(),
        cost_estimate=cost,
    )(*args)


def iota(shape, dim):
    return lax.broadcasted_iota(jnp.int32, shape, dim)


def split_bf16(x):
    hi = x.astype(bf16)
    return hi, (x - hi.astype(f32)).astype(bf16)


def project_sends(x, w, k, mib, order):
    rows, depth = x.shape
    cols = w.shape[1] // N_PHASE
    n = len(order)

    def body(k_ref, x_ref, w_ref, *refs):
        outs, (x_buf, w_buf, out_buf, sem_ref) = refs[:n], refs[n:]

        def load(i):
            start = pl.multiple_of(lax.rem(k_ref[0] + order[i], N_PHASE) * cols, cols)
            return pltpu.make_async_copy(w_ref.at[:, pl.ds(start, cols)], w_buf.at[i], sem_ref.at[i])

        def store(i):
            return pltpu.make_async_copy(out_buf.at[i], outs[i], sem_ref.at[n + i])

        load_x = pltpu.make_async_copy(x_ref, x_buf, sem_ref.at[2 * n])
        load_x.start()
        for i in range(n):
            load(i).start()
        load_x.wait()
        for i in range(n):
            load(i).wait()
            out_buf[i] = dot(x_buf[...], w_buf[i]).astype(bf16)
            store(i).start()
        for i in range(n):
            store(i).wait()

    hbm = pl.BlockSpec(memory_space=pltpu.HBM)
    return pl.pallas_call(
        body,
        in_specs=[pl.BlockSpec(memory_space=pltpu.SMEM), hbm, hbm],
        out_specs=[hbm] * n,
        out_shape=[jax.ShapeDtypeStruct((rows, cols), bf16)] * n,
        scratch_shapes=[
            pltpu.VMEM((rows, depth), bf16),
            pltpu.VMEM((n, depth, cols), bf16),
            pltpu.VMEM((n, rows, cols), bf16),
            pltpu.SemaphoreType.DMA((2 * n + 1,)),
        ],
        compiler_params=params(mib),
        cost_estimate=cost,
    )(k, x, w)


def project_own(x, w, k):
    rows, depth = x.shape
    cols = w.shape[1] // N_PHASE

    def body(k_ref, x_ref, w_ref, own_ref):
        own_ref[...] = dot(x_ref[...], w_ref[...])

    return pl.pallas_call(
        body,
        grid_spec=pltpu.PrefetchScalarGridSpec(
            num_scalar_prefetch=1,
            grid=(1,),
            in_specs=[
                pl.BlockSpec((rows, depth), lambda s, k_ref: (0, 0)),
                pl.BlockSpec((depth, cols), lambda s, k_ref: (0, k_ref[0])),
            ],
            out_specs=pl.BlockSpec((rows, cols), lambda s, k_ref: (0, 0)),
        ),
        out_shape=jax.ShapeDtypeStruct((rows, cols), f32),
        compiler_params=params(),
        cost_estimate=cost,
    )(k, x, w)


def project_back(u, w, k):
    rows, cols = u.shape
    depth = w.shape[0]

    def columns(w_ref, k_ref, s):
        return w_ref[:, pl.ds(pl.multiple_of(lax.rem(k_ref[0] + s, N_PHASE) * cols, cols), cols)]

    def product(*shifts):
        def body(k_ref, *refs):
            block_refs, w_ref, out_ref = refs[-len(shifts) - 2 : -2], refs[-2], refs[-1]
            total = sum(dot(r[...], columns(w_ref, k_ref, s), NT) for s, r in zip(shifts, block_refs))
            if len(refs) > len(shifts) + 2:
                total = refs[0][...] + total
            out_ref[...] = total.astype(out_ref.dtype)

        return body

    def run(body, dtype, *args):
        vmem = pl.BlockSpec(memory_space=pltpu.VMEM)
        return pl.pallas_call(
            body,
            in_specs=[pl.BlockSpec(memory_space=pltpu.SMEM)] + [vmem] * len(args),
            out_specs=vmem,
            out_shape=jax.ShapeDtypeStruct((rows, depth), dtype),
            compiler_params=params(),
            cost_estimate=cost,
        )(k, *args)

    blocks = gather_blocks(u)
    acc = run(product(0), f32, blocks[0], w)
    acc = run(product(3), f32, acc, blocks[3], w)
    return run(product(1, 2), bf16, acc, blocks[1], blocks[2], w)


def send(block, s):
    return lax.ppermute(block, "phase", [(i, (i + s) % N_PHASE) for i in range(N_PHASE)])


def gather_blocks(x):
    return [x] + [
        lax.ppermute(x, "phase", [((i + s) % N_PHASE, i) for i in range(N_PHASE)]) for s in range(1, N_PHASE)
    ]


def sum_refs(refs):
    total = refs[0][...].astype(f32)
    for r in refs[1:]:
        total = total + r[...].astype(f32)
    return total


def sum_queries(own, a, b, c, total_ref, low_ref):
    total = sum_refs((own, a, b, c))
    total_ref[...] = total
    low_ref[...] = total.astype(bf16)


def onehot_rows(request_ref, out_ref):
    docs = out_ref.shape[1]
    slots = out_ref.shape[0]
    onehot = (iota((docs, slots), 0) == request_ref[...]).astype(f32).astype(bf16)
    eye = (iota((docs, docs), 0) == iota((docs, docs), 1)).astype(f32).astype(bf16)
    out_ref[...] = dot(onehot, eye, TN).astype(bf16)


def sum_docs(parts, onehot):
    docs, cols = parts[0].shape
    slots = onehot.shape[0]
    block = slots // CHUNKS

    def body(a, b, c, d, onehot_ref, total_ref, rows_ref, buf_ref, sem_ref):
        total = sum_refs((a, b, c, d))
        total_ref[...] = total
        low = total.astype(bf16)

        def store(i):
            part = pl.ds(i * block, block)
            return pltpu.make_async_copy(buf_ref.at[part], rows_ref.at[part], sem_ref.at[i])

        for i in range(CHUNKS):
            part = slice(i * block, (i + 1) * block)
            buf_ref[part, :] = dot(onehot_ref[part, :], low).astype(bf16)
            store(i).start()
        for i in range(CHUNKS):
            store(i).wait()

    vmem = pl.BlockSpec(memory_space=pltpu.VMEM)
    return pl.pallas_call(
        body,
        in_specs=[vmem] * 5,
        out_specs=[vmem, pl.BlockSpec(memory_space=pltpu.HBM)],
        out_shape=[jax.ShapeDtypeStruct((docs, cols), f32), jax.ShapeDtypeStruct((slots, cols), bf16)],
        scratch_shapes=[pltpu.VMEM((slots, cols), bf16), pltpu.SemaphoreType.DMA((CHUNKS,))],
        compiler_params=params(),
        cost_estimate=cost,
    )(*parts, onehot)


def ones_row_sums(x):
    hi, lo = split_bf16(x)
    ones = jnp.ones((8, x.shape[1]), bf16)
    return dot(ones, hi, NT) + dot(ones, lo, NT)


def inner_partials(q_ref, d_ref, out_ref):
    q = q_ref[...]
    d = d_ref[...]
    q2 = jnp.concatenate([q, q], axis=0)
    docs = d.shape[0]
    out_ref[0:docs, :] = dot(d.astype(bf16), q2.astype(bf16), NT)
    out_ref[docs : docs + 8, :] = ones_row_sums(q2 * q2)
    out_ref[docs + 8 : docs + 16, :] = ones_row_sums(d * d)


def hard_partials(rows_ref, q_ref, neg_ref, out_ref):
    rows = rows_ref[...]
    q = q_ref[...]
    wide = rows.astype(f32)
    square = wide * wide
    folded = square[:, 0:128]
    for s in range(128, square.shape[1], 128):
        folded = folded + square[:, s : s + 128]
    hi, lo = split_bf16(folded)
    upper = (iota((128, 128), 1) >= 64).astype(f32).astype(bf16)
    both = dot(rows, jnp.concatenate([q, jnp.zeros_like(q)], axis=0), NT) + dot(hi, upper) + dot(lo, upper)
    slot = iota(both.shape, 0)
    for j in range(8):
        hit = slot == neg_ref[j : j + 1, :]
        out_ref[j : j + 1, :] = jnp.sum(jnp.where(hit, both, 0.0), axis=0, keepdims=True)


def softmax_terms(*refs):
    inner_refs, hard_refs = refs[0:4], refs[4:8]
    small_ref, neg_ref, rows_ref, q_ref, out_ref, coef_ref, grad_ref, row_ref, col_ref, buf_ref, sem_ref = refs[8:]
    sums = sum_refs(inner_refs)
    picks = sum_refs(hard_refs)
    docs, queries = grad_ref.shape[0], q_ref.shape[0]
    swapped = pltpu.roll(picks, 64, 1)
    low_lane = iota(picks.shape, 1) < 64
    scores = jnp.where(low_lane, picks, swapped)
    squares = jnp.where(low_lane, swapped, picks)
    q_scale = lax.rsqrt(sums[docs : docs + 1, :] + epsilon)
    d_scale_row = lax.rsqrt(sums[docs + 8 : docs + 9, :] + epsilon)
    row = iota((docs, 128), 0)
    lane = iota((docs, 128), 1)
    d_scale = jnp.sum(jnp.where(row == lane, d_scale_row, 0.0), axis=1, keepdims=True)
    inner = scale20 * (sums[0:docs, :] * q_scale * d_scale)
    hard_scale = lax.rsqrt(squares + epsilon)
    hard = scale20 * (scores * q_scale * hard_scale)
    valid = small_ref[0:8, :]
    weight = scale20 * small_ref[8:9, :]
    hard_exp = jnp.exp(hard) * valid
    inner_exp = jnp.exp(inner)
    total = jnp.sum(inner_exp, axis=0, keepdims=True) + jnp.sum(hard_exp, axis=0, keepdims=True)
    own = row == lax.bitwise_and(lane, 63)
    positive = jnp.sum(jnp.where(own, inner, 0.0), axis=0, keepdims=True)
    factor = weight / total
    hard_grad = factor * hard_exp
    hard_dot = hard_grad * hard * (1.0 / scale20)
    sent = hard_scale * jnp.where(low_lane, hard_grad, hard_dot * hard_scale)
    slots = out_ref.shape[0]
    slot = iota((slots, 128), 0)
    coef = jnp.zeros((slots, 128), f32)
    for j in range(7):
        coef = coef + jnp.where(slot == neg_ref[j : j + 1, :], sent[j : j + 1, :], 0.0)
    coef = coef.astype(bf16)
    coef_ref[...] = coef

    eye = iota((queries, 128), 0) == iota((queries, 128), 1)
    q_scale_col = jnp.sum(jnp.where(eye, q_scale, 0.0), axis=1, keepdims=True)
    q_low = (q_ref[...] * q_scale_col).astype(bf16)
    q_low = jnp.concatenate([q_low, jnp.zeros_like(q_low)], axis=0)
    second = (iota((128, 128), 0) >= 64).astype(f32).astype(bf16)
    block = slots // CHUNKS

    def store(i):
        part = pl.ds(i * block, block)
        return pltpu.make_async_copy(buf_ref.at[part], out_ref.at[part], sem_ref.at[i])

    for i in range(CHUNKS):
        part = slice(i * block, (i + 1) * block)
        along = dot(coef[part, :], second)
        mixed = dot(coef[part, :], q_low)
        for c in range(0, mixed.shape[1], 128):
            away = along * rows_ref[part, c : c + 128].astype(f32)
            buf_ref[part, c : c + 128] = (mixed[:, c : c + 128] - away).astype(bf16)
        store(i).start()

    grad = (factor * inner_exp - jnp.where(own, weight, 0.0)).astype(bf16)
    grad_ref[...] = grad
    products = grad.astype(f32) * inner * (1.0 / scale20)
    q_dot = jnp.sum(products, axis=0, keepdims=True) + jnp.sum(hard_dot, axis=0, keepdims=True)
    d_dot = jnp.sum(jnp.where(lane < 64, products, 0.0), axis=1, keepdims=True)
    row_ref[...] = jnp.zeros_like(row_ref)
    row_ref[0:1, :] = jnp.log(total) - positive
    row_ref[1:2, :] = q_scale
    row_ref[2:3, :] = q_dot
    col_ref[...] = jnp.where(lane == 0, d_scale, d_dot)
    for i in range(CHUNKS):
        store(i).wait()


def local_grads(coef_ref, grad_ref, row_ref, col_ref, rows_ref, d_ref, q_ref, u_ref, g_ref):
    queries = q_ref.shape[0]
    d_scale = col_ref[:, 0:1]
    d_dot = col_ref[:, 1:2]
    eye = iota((queries, 128), 0) == iota((queries, 128), 1)
    q_scale = jnp.sum(jnp.where(eye, row_ref[1:2, :], 0.0), axis=1, keepdims=True)
    q_dot = jnp.sum(jnp.where(eye, row_ref[2:3, :], 0.0), axis=1, keepdims=True)
    q_unit = q_ref[...] * q_scale
    q_low = q_unit.astype(bf16)
    q_low = jnp.concatenate([q_low, jnp.zeros_like(q_low)], axis=0)
    d_unit = d_ref[...] * d_scale
    grad = grad_ref[...]
    g_query = dot(grad, d_unit.astype(bf16), TN) + dot(coef_ref[...], rows_ref[...], TN)
    u_ref[...] = (q_scale * (g_query[0:queries, :] - q_unit * q_dot)).astype(bf16)
    g_ref[...] = d_scale * (dot(grad, q_low) - d_unit * d_dot)


def doc_grads(rows_ref, request_ref, g_ref, u_ref):
    docs, slots = g_ref.shape[0], rows_ref.shape[0]
    onehot = (iota((docs, slots), 0) == request_ref[...]).astype(f32).astype(bf16)
    u_ref[...] = (g_ref[...] + dot(onehot, rows_ref[...])).astype(bf16)


def local(
    query_states,
    doc_states,
    query_proj,
    doc_proj,
    document_requests,
    slot_valid,
    neg_slot,
    query_weight,
):
    k = lax.axis_index("phase").astype(jnp.int32).reshape(1)
    queries, docs = query_states.shape[0], doc_states.shape[0]
    cols = query_proj.shape[1] // N_PHASE
    n_dp, cap = document_requests.shape[1:]
    slots = n_dp * cap

    negatives = neg_slot.T
    held = jnp.asarray(DP_PLACE, jnp.int32)[negatives // cap] * cap + negatives % cap
    neg_rows = jnp.pad(jnp.concatenate([held, held], axis=1), ((0, 1), (0, 0)), constant_values=-1)
    order = [DP_ORDER]

    def exchange(rows):
        blocks = rows.reshape(n_dp, cap, cols)
        swapped = lax.all_to_all(
            blocks, "dp", split_axis=0, concat_axis=0, tiled=True, axis_index_groups=order
        )
        return swapped.reshape(slots, cols)

    d_far, d_next, d_last, document_requests = lax.optimization_barrier(
        (*project_sends(doc_states, doc_proj, k, 63, (2, 1, 3)), document_requests)
    )
    requests = document_requests[0][jnp.asarray(DP_ORDER, jnp.int32)].reshape(1, slots)
    d_parts = [send(d_far, 2), send(d_next, 1), send(d_last, 3)]
    d_own = project_own(doc_states, doc_proj, k)
    (onehot,) = call(onehot_rows, [((slots, docs), bf16)], requests)
    d_total, outgoing = sum_docs([d_own] + d_parts, onehot)
    outgoing, query_states = lax.optimization_barrier((outgoing, query_states))
    received = exchange(outgoing)

    q_own = project_own(query_states, query_proj, k)
    q_far, q_next, q_last = project_sends(query_states, query_proj, k, 16, (2, 1, 3))
    q_parts = [send(q_far, 2), send(q_next, 1), send(q_last, 3)]
    q_total, q_low = call(sum_queries, [((queries, cols), f32), ((queries, cols), bf16)], q_own, *q_parts)
    (inner,) = call(inner_partials, [((docs + 16, 128), f32)], q_total, d_total)
    inner_all = gather_blocks(inner)
    valid = jnp.take(slot_valid[0], negatives).astype(f32)
    weight = query_weight[None, :]
    small = jnp.pad(
        jnp.concatenate([valid, jnp.zeros_like(weight), weight], axis=0), ((0, 7), (0, 0))
    )
    small = jnp.concatenate([small, small], axis=1)
    received, small, neg_rows = lax.optimization_barrier((received, small, neg_rows))

    (hard,) = call(hard_partials, [((8, 128), f32)], received, q_low, neg_rows)
    hard_all = gather_blocks(hard)
    vmem = pl.BlockSpec(memory_space=pltpu.VMEM)
    rows, coef, grad, by_query, by_doc = pl.pallas_call(
        softmax_terms,
        in_specs=[vmem] * 12,
        out_specs=[pl.BlockSpec(memory_space=pltpu.HBM)] + [vmem] * 4,
        out_shape=[
            jax.ShapeDtypeStruct((slots, cols), bf16),
            jax.ShapeDtypeStruct((slots, 128), bf16),
            jax.ShapeDtypeStruct((docs, 128), bf16),
            jax.ShapeDtypeStruct((8, 128), f32),
            jax.ShapeDtypeStruct((docs, 128), f32),
        ],
        scratch_shapes=[pltpu.VMEM((slots, cols), bf16), pltpu.SemaphoreType.DMA((CHUNKS,))],
        compiler_params=params(),
        cost_estimate=cost,
    )(*inner_all, *hard_all, small, neg_rows, received, q_total)
    arrived = exchange(rows)
    u_query, g_local = call(
        local_grads,
        [((queries, cols), bf16), ((docs, cols), f32)],
        coef,
        grad,
        by_query,
        by_doc,
        received,
        d_total,
        q_total,
    )
    grad_query = project_back(u_query, query_proj, k)
    arrived, grad_query, loss = lax.optimization_barrier((arrived, grad_query, by_query[0, :queries]))

    (u_docs,) = call(doc_grads, [((docs, cols), bf16)], arrived, requests, g_local)
    grad_doc = project_back(u_docs, doc_proj, k)
    return (loss, grad_query, grad_doc)


def solution(mesh):
    in_specs = (
        P("dp", "phase"),
        P("dp", "phase"),
        P("phase", None),
        P("phase", None),
        P("dp", None, None),
        P("dp", None),
        P("dp", None),
        P("dp"),
    )
    out_specs = (P("dp"), P("dp", "phase"), P("dp", "phase"))
    return jax.shard_map(local, mesh=mesh, in_specs=in_specs, out_specs=out_specs, check_vma=False)
```

```python
import jax
import jax.numpy as jnp
from jax import lax
from jax.experimental import pallas as pl
from jax.experimental.pallas import tpu as pltpu
from jax.sharding import PartitionSpec as P

scale20 = 20.0
epsilon = 1e-06
f32 = jnp.float32
bf16 = jnp.bfloat16
NT = (((1,), (1,)), ((), ()))
TN = (((0,), (0,)), ((), ()))
N_PHASE = 4
CHUNKS = 4
DP_ORDER = [45, 29, 43, 61, 34, 33, 31, 40, 26, 62, 22, 2, 11, 28, 54, 4, 10, 35, 52, 46, 30, 7, 14, 27, 63, 55, 41, 42, 58, 18, 60, 32, 15, 5, 16, 20, 56, 8, 13, 25, 37, 17, 48, 51, 57, 38, 1, 12, 49, 24, 6, 23, 36, 50, 21, 19, 9, 39, 59, 3, 0, 53, 47, 44]
DP_PLACE = [60, 46, 11, 59, 15, 33, 50, 21, 37, 56, 16, 12, 47, 38, 22, 32, 34, 41, 29, 55, 35, 54, 10, 51, 49, 39, 8, 23, 13, 1, 20, 6, 31, 5, 4, 17, 52, 40, 45, 57, 7, 26, 27, 2, 63, 0, 19, 62, 42, 48, 53, 43, 18, 61, 14, 25, 36, 44, 28, 58, 30, 3, 9, 24]
cost = pl.CostEstimate(flops=10**9, bytes_accessed=10**5, transcendentals=0)


def dot(a, b, dims=(((1,), (0,)), ((), ()))):
    return lax.dot_general(a, b, dims, preferred_element_type=f32)


def params(mib=16):
    return pltpu.CompilerParams(vmem_limit_bytes=mib * 1024 * 1024)


def call(body, outs, *args):
    return pl.pallas_call(
        body,
        out_shape=[jax.ShapeDtypeStruct(s, t) for s, t in outs],
        compiler_params=params(),
        cost_estimate=cost,
    )(*args)


def iota(shape, dim):
    return lax.broadcasted_iota(jnp.int32, shape, dim)


def split_bf16(x):
    hi = x.astype(bf16)
    return hi, (x - hi.astype(f32)).astype(bf16)


def project_sends(x, w, k, mib, order):
    rows, depth = x.shape
    cols = w.shape[1] // N_PHASE
    n = len(order)

    def body(k_ref, x_ref, w_ref, *refs):
        outs, (x_buf, w_buf, out_buf, sem_ref) = refs[:n], refs[n:]

        def load(i):
            start = pl.multiple_of(lax.rem(k_ref[0] + order[i], N_PHASE) * cols, cols)
            return pltpu.make_async_copy(w_ref.at[:, pl.ds(start, cols)], w_buf.at[i], sem_ref.at[i])

        def store(i):
            return pltpu.make_async_copy(out_buf.at[i], outs[i], sem_ref.at[n + i])

        load_x = pltpu.make_async_copy(x_ref, x_buf, sem_ref.at[2 * n])
        load_x.start()
        for i in range(n):
            load(i).start()
        load_x.wait()
        for i in range(n):
            load(i).wait()
            out_buf[i] = dot(x_buf[...], w_buf[i]).astype(bf16)
            store(i).start()
        for i in range(n):
            store(i).wait()

    hbm = pl.BlockSpec(memory_space=pltpu.HBM)
    return pl.pallas_call(
        body,
        in_specs=[pl.BlockSpec(memory_space=pltpu.SMEM), hbm, hbm],
        out_specs=[hbm] * n,
        out_shape=[jax.ShapeDtypeStruct((rows, cols), bf16)] * n,
        scratch_shapes=[
            pltpu.VMEM((rows, depth), bf16),
            pltpu.VMEM((n, depth, cols), bf16),
            pltpu.VMEM((n, rows, cols), bf16),
            pltpu.SemaphoreType.DMA((2 * n + 1,)),
        ],
        compiler_params=params(mib),
        cost_estimate=cost,
    )(k, x, w)


def project_own(x, w, k):
    rows, depth = x.shape
    cols = w.shape[1] // N_PHASE

    def body(k_ref, x_ref, w_ref, own_ref):
        own_ref[...] = dot(x_ref[...], w_ref[...])

    return pl.pallas_call(
        body,
        grid_spec=pltpu.PrefetchScalarGridSpec(
            num_scalar_prefetch=1,
            grid=(1,),
            in_specs=[
                pl.BlockSpec((rows, depth), lambda s, k_ref: (0, 0)),
                pl.BlockSpec((depth, cols), lambda s, k_ref: (0, k_ref[0])),
            ],
            out_specs=pl.BlockSpec((rows, cols), lambda s, k_ref: (0, 0)),
        ),
        out_shape=jax.ShapeDtypeStruct((rows, cols), f32),
        compiler_params=params(),
        cost_estimate=cost,
    )(k, x, w)


def project_back(u, w, k):
    rows, cols = u.shape
    depth = w.shape[0]

    def columns(w_ref, k_ref, s):
        return w_ref[:, pl.ds(pl.multiple_of(lax.rem(k_ref[0] + s, N_PHASE) * cols, cols), cols)]

    def product(*shifts):
        def body(k_ref, *refs):
            block_refs, w_ref, out_ref = refs[-len(shifts) - 2 : -2], refs[-2], refs[-1]
            total = sum(dot(r[...], columns(w_ref, k_ref, s), NT) for s, r in zip(shifts, block_refs))
            if len(refs) > len(shifts) + 2:
                total = refs[0][...] + total
            out_ref[...] = total.astype(out_ref.dtype)

        return body

    def run(body, dtype, *args):
        vmem = pl.BlockSpec(memory_space=pltpu.VMEM)
        return pl.pallas_call(
            body,
            in_specs=[pl.BlockSpec(memory_space=pltpu.SMEM)] + [vmem] * len(args),
            out_specs=vmem,
            out_shape=jax.ShapeDtypeStruct((rows, depth), dtype),
            compiler_params=params(),
            cost_estimate=cost,
        )(k, *args)

    blocks = gather_blocks(u)
    acc = run(product(0), f32, blocks[0], w)
    acc = run(product(3), f32, acc, blocks[3], w)

    def last(k_ref, acc_ref, a_ref, b_ref, w_ref, out_ref, buf_ref, sem_ref):
        half = depth // 2

        def store(i):
            return pltpu.make_async_copy(buf_ref.at[i], out_ref.at[:, pl.ds(i * half, half)], sem_ref.at[i])

        for i in range(2):
            part = slice(i * half, (i + 1) * half)
            total = acc_ref[:, part]
            for s, block in enumerate((a_ref, b_ref), start=1):
                start = pl.multiple_of(lax.rem(k_ref[0] + s, N_PHASE) * cols, cols)
                total = total + dot(block[...], w_ref[part, pl.ds(start, cols)], NT)
            buf_ref[i] = total.astype(bf16)
            store(i).start()
        for i in range(2):
            store(i).wait()

    return pl.pallas_call(
        last,
        in_specs=[pl.BlockSpec(memory_space=pltpu.SMEM)] + [pl.BlockSpec(memory_space=pltpu.VMEM)] * 4,
        out_specs=pl.BlockSpec(memory_space=pltpu.HBM),
        out_shape=jax.ShapeDtypeStruct((rows, depth), bf16),
        scratch_shapes=[pltpu.VMEM((2, rows, depth // 2), bf16), pltpu.SemaphoreType.DMA((2,))],
        compiler_params=params(),
        cost_estimate=cost,
    )(k, acc, blocks[1], blocks[2], w)


def send(block, s):
    return lax.ppermute(block, "phase", [(i, (i + s) % N_PHASE) for i in range(N_PHASE)])


def gather_blocks(x):
    return [x] + [
        lax.ppermute(x, "phase", [((i + s) % N_PHASE, i) for i in range(N_PHASE)]) for s in range(1, N_PHASE)
    ]


def sum_refs(refs):
    total = refs[0][...].astype(f32)
    for r in refs[1:]:
        total = total + r[...].astype(f32)
    return total


def sum_queries(own, a, b, c, total_ref, low_ref):
    total = sum_refs((own, a, b, c))
    total_ref[...] = total
    low_ref[...] = total.astype(bf16)


def onehot_rows(request_ref, out_ref):
    docs = out_ref.shape[1]
    slots = out_ref.shape[0]
    onehot = (iota((docs, slots), 0) == request_ref[...]).astype(f32).astype(bf16)
    eye = (iota((docs, docs), 0) == iota((docs, docs), 1)).astype(f32).astype(bf16)
    out_ref[...] = dot(onehot, eye, TN).astype(bf16)


def sum_docs(parts, onehot):
    docs, cols = parts[0].shape
    slots = onehot.shape[0]
    block = slots // CHUNKS

    def body(a, b, c, d, onehot_ref, total_ref, rows_ref, buf_ref, sem_ref):
        total = sum_refs((a, b, c, d))
        total_ref[...] = total
        low = total.astype(bf16)

        def store(i):
            part = pl.ds(i * block, block)
            return pltpu.make_async_copy(buf_ref.at[part], rows_ref.at[part], sem_ref.at[i])

        for i in range(CHUNKS):
            part = slice(i * block, (i + 1) * block)
            buf_ref[part, :] = dot(onehot_ref[part, :], low).astype(bf16)
            store(i).start()
        for i in range(CHUNKS):
            store(i).wait()

    vmem = pl.BlockSpec(memory_space=pltpu.VMEM)
    return pl.pallas_call(
        body,
        in_specs=[vmem] * 5,
        out_specs=[vmem, pl.BlockSpec(memory_space=pltpu.HBM)],
        out_shape=[jax.ShapeDtypeStruct((docs, cols), f32), jax.ShapeDtypeStruct((slots, cols), bf16)],
        scratch_shapes=[pltpu.VMEM((slots, cols), bf16), pltpu.SemaphoreType.DMA((CHUNKS,))],
        compiler_params=params(),
        cost_estimate=cost,
    )(*parts, onehot)


def ones_row_sums(x):
    hi, lo = split_bf16(x)
    ones = jnp.ones((8, x.shape[1]), bf16)
    return dot(ones, hi, NT) + dot(ones, lo, NT)


def inner_partials(q_ref, d_ref, out_ref):
    q = q_ref[...]
    d = d_ref[...]
    q2 = jnp.concatenate([q, q], axis=0)
    docs = d.shape[0]
    out_ref[0:docs, :] = dot(d.astype(bf16), q2.astype(bf16), NT)
    out_ref[docs : docs + 8, :] = ones_row_sums(q2 * q2)
    out_ref[docs + 8 : docs + 16, :] = ones_row_sums(d * d)


def hard_partials(rows_ref, q_ref, neg_ref, out_ref):
    rows = rows_ref[...]
    q = q_ref[...]
    wide = rows.astype(f32)
    square = wide * wide
    folded = square[:, 0:128]
    for s in range(128, square.shape[1], 128):
        folded = folded + square[:, s : s + 128]
    hi, lo = split_bf16(folded)
    upper = (iota((128, 128), 1) >= 64).astype(f32).astype(bf16)
    both = dot(rows, jnp.concatenate([q, jnp.zeros_like(q)], axis=0), NT) + dot(hi, upper) + dot(lo, upper)
    slot = iota(both.shape, 0)
    for j in range(8):
        hit = slot == neg_ref[j : j + 1, :]
        out_ref[j : j + 1, :] = jnp.sum(jnp.where(hit, both, 0.0), axis=0, keepdims=True)


def softmax_terms(*refs):
    inner_refs, hard_refs = refs[0:4], refs[4:8]
    small_ref, neg_ref, rows_ref, q_ref, out_ref, coef_ref, grad_ref, row_ref, col_ref, buf_ref, sem_ref = refs[8:]
    sums = sum_refs(inner_refs)
    picks = sum_refs(hard_refs)
    docs, queries = grad_ref.shape[0], q_ref.shape[0]
    swapped = pltpu.roll(picks, 64, 1)
    low_lane = iota(picks.shape, 1) < 64
    scores = jnp.where(low_lane, picks, swapped)
    squares = jnp.where(low_lane, swapped, picks)
    q_scale = lax.rsqrt(sums[docs : docs + 1, :] + epsilon)
    d_scale_row = lax.rsqrt(sums[docs + 8 : docs + 9, :] + epsilon)
    row = iota((docs, 128), 0)
    lane = iota((docs, 128), 1)
    d_scale = jnp.sum(jnp.where(row == lane, d_scale_row, 0.0), axis=1, keepdims=True)
    inner = scale20 * (sums[0:docs, :] * q_scale * d_scale)
    hard_scale = lax.rsqrt(squares + epsilon)
    hard = scale20 * (scores * q_scale * hard_scale)
    valid = small_ref[0:8, :]
    weight = scale20 * small_ref[8:9, :]
    hard_exp = jnp.exp(hard) * valid
    inner_exp = jnp.exp(inner)
    total = jnp.sum(inner_exp, axis=0, keepdims=True) + jnp.sum(hard_exp, axis=0, keepdims=True)
    own = row == lax.bitwise_and(lane, 63)
    positive = jnp.sum(jnp.where(own, inner, 0.0), axis=0, keepdims=True)
    factor = weight / total
    hard_grad = factor * hard_exp
    hard_dot = hard_grad * hard * (1.0 / scale20)
    sent = hard_scale * jnp.where(low_lane, hard_grad, hard_dot * hard_scale)
    slots = out_ref.shape[0]
    slot = iota((slots, 128), 0)
    coef = jnp.zeros((slots, 128), f32)
    for j in range(7):
        coef = coef + jnp.where(slot == neg_ref[j : j + 1, :], sent[j : j + 1, :], 0.0)
    coef = coef.astype(bf16)
    coef_ref[...] = coef

    eye = iota((queries, 128), 0) == iota((queries, 128), 1)
    q_scale_col = jnp.sum(jnp.where(eye, q_scale, 0.0), axis=1, keepdims=True)
    q_low = (q_ref[...] * q_scale_col).astype(bf16)
    q_low = jnp.concatenate([q_low, jnp.zeros_like(q_low)], axis=0)
    second = (iota((128, 128), 0) >= 64).astype(f32).astype(bf16)
    block = slots // CHUNKS

    def store(i):
        part = pl.ds(i * block, block)
        return pltpu.make_async_copy(buf_ref.at[part], out_ref.at[part], sem_ref.at[i])

    for i in range(CHUNKS):
        part = slice(i * block, (i + 1) * block)
        along = dot(coef[part, :], second)
        mixed = dot(coef[part, :], q_low)
        for c in range(0, mixed.shape[1], 128):
            away = along * rows_ref[part, c : c + 128].astype(f32)
            buf_ref[part, c : c + 128] = (mixed[:, c : c + 128] - away).astype(bf16)
        store(i).start()

    grad = (factor * inner_exp - jnp.where(own, weight, 0.0)).astype(bf16)
    grad_ref[...] = grad
    products = grad.astype(f32) * inner * (1.0 / scale20)
    q_dot = jnp.sum(products, axis=0, keepdims=True) + jnp.sum(hard_dot, axis=0, keepdims=True)
    d_dot = jnp.sum(jnp.where(lane < 64, products, 0.0), axis=1, keepdims=True)
    row_ref[...] = jnp.zeros_like(row_ref)
    row_ref[0:1, :] = jnp.log(total) - positive
    row_ref[1:2, :] = q_scale
    row_ref[2:3, :] = q_dot
    col_ref[...] = jnp.where(lane == 0, d_scale, d_dot)
    for i in range(CHUNKS):
        store(i).wait()


def local_grads(coef_ref, grad_ref, row_ref, col_ref, rows_ref, d_ref, q_ref, u_ref, g_ref):
    queries = q_ref.shape[0]
    d_scale = col_ref[:, 0:1]
    d_dot = col_ref[:, 1:2]
    eye = iota((queries, 128), 0) == iota((queries, 128), 1)
    q_scale = jnp.sum(jnp.where(eye, row_ref[1:2, :], 0.0), axis=1, keepdims=True)
    q_dot = jnp.sum(jnp.where(eye, row_ref[2:3, :], 0.0), axis=1, keepdims=True)
    q_unit = q_ref[...] * q_scale
    q_low = q_unit.astype(bf16)
    q_low = jnp.concatenate([q_low, jnp.zeros_like(q_low)], axis=0)
    d_unit = d_ref[...] * d_scale
    grad = grad_ref[...]
    g_query = dot(grad, d_unit.astype(bf16), TN) + dot(coef_ref[...], rows_ref[...], TN)
    u_ref[...] = (q_scale * (g_query[0:queries, :] - q_unit * q_dot)).astype(bf16)
    g_ref[...] = d_scale * (dot(grad, q_low) - d_unit * d_dot)


def doc_grads(rows_ref, request_ref, g_ref, u_ref):
    docs, slots = g_ref.shape[0], rows_ref.shape[0]
    onehot = (iota((docs, slots), 0) == request_ref[...]).astype(f32).astype(bf16)
    u_ref[...] = (g_ref[...] + dot(onehot, rows_ref[...])).astype(bf16)


def local(
    query_states,
    doc_states,
    query_proj,
    doc_proj,
    document_requests,
    slot_valid,
    neg_slot,
    query_weight,
):
    k = lax.axis_index("phase").astype(jnp.int32).reshape(1)
    queries, docs = query_states.shape[0], doc_states.shape[0]
    cols = query_proj.shape[1] // N_PHASE
    n_dp, cap = document_requests.shape[1:]
    slots = n_dp * cap

    negatives = neg_slot.T
    held = jnp.asarray(DP_PLACE, jnp.int32)[negatives // cap] * cap + negatives % cap
    neg_rows = jnp.pad(jnp.concatenate([held, held], axis=1), ((0, 1), (0, 0)), constant_values=-1)
    order = [DP_ORDER]

    def exchange(rows):
        blocks = rows.reshape(n_dp, cap, cols)
        swapped = lax.all_to_all(
            blocks, "dp", split_axis=0, concat_axis=0, tiled=True, axis_index_groups=order
        )
        return swapped.reshape(slots, cols)

    d_far, d_next, d_last, document_requests = lax.optimization_barrier(
        (*project_sends(doc_states, doc_proj, k, 63, (2, 1, 3)), document_requests)
    )
    requests = document_requests[0][jnp.asarray(DP_ORDER, jnp.int32)].reshape(1, slots)
    d_parts = [send(d_far, 2), send(d_next, 1), send(d_last, 3)]
    d_own = project_own(doc_states, doc_proj, k)
    (onehot,) = call(onehot_rows, [((slots, docs), bf16)], requests)
    d_total, outgoing = sum_docs([d_own] + d_parts, onehot)
    outgoing, query_states = lax.optimization_barrier((outgoing, query_states))
    received = exchange(outgoing)

    q_own = project_own(query_states, query_proj, k)
    q_far, q_next, q_last = project_sends(query_states, query_proj, k, 16, (2, 1, 3))
    q_parts = [send(q_far, 2), send(q_next, 1), send(q_last, 3)]
    q_total, q_low = call(sum_queries, [((queries, cols), f32), ((queries, cols), bf16)], q_own, *q_parts)
    (inner,) = call(inner_partials, [((docs + 16, 128), f32)], q_total, d_total)
    inner_all = gather_blocks(inner)
    valid = jnp.take(slot_valid[0], negatives).astype(f32)
    weight = query_weight[None, :]
    small = jnp.pad(
        jnp.concatenate([valid, jnp.zeros_like(weight), weight], axis=0), ((0, 7), (0, 0))
    )
    small = jnp.concatenate([small, small], axis=1)
    received, small, neg_rows = lax.optimization_barrier((received, small, neg_rows))

    (hard,) = call(hard_partials, [((8, 128), f32)], received, q_low, neg_rows)
    hard_all = gather_blocks(hard)
    vmem = pl.BlockSpec(memory_space=pltpu.VMEM)
    rows, coef, grad, by_query, by_doc = pl.pallas_call(
        softmax_terms,
        in_specs=[vmem] * 12,
        out_specs=[pl.BlockSpec(memory_space=pltpu.HBM)] + [vmem] * 4,
        out_shape=[
            jax.ShapeDtypeStruct((slots, cols), bf16),
            jax.ShapeDtypeStruct((slots, 128), bf16),
            jax.ShapeDtypeStruct((docs, 128), bf16),
            jax.ShapeDtypeStruct((8, 128), f32),
            jax.ShapeDtypeStruct((docs, 128), f32),
        ],
        scratch_shapes=[pltpu.VMEM((slots, cols), bf16), pltpu.SemaphoreType.DMA((CHUNKS,))],
        compiler_params=params(),
        cost_estimate=cost,
    )(*inner_all, *hard_all, small, neg_rows, received, q_total)
    arrived = exchange(rows)
    u_query, g_local = call(
        local_grads,
        [((queries, cols), bf16), ((docs, cols), f32)],
        coef,
        grad,
        by_query,
        by_doc,
        received,
        d_total,
        q_total,
    )
    grad_query = project_back(u_query, query_proj, k)
    arrived, grad_query, loss = lax.optimization_barrier((arrived, grad_query, by_query[0, :queries]))

    (u_docs,) = call(doc_grads, [((docs, cols), bf16)], arrived, requests, g_local)
    grad_doc = project_back(u_docs, doc_proj, k)
    return (loss, grad_query, grad_doc)


def solution(mesh):
    in_specs = (
        P("dp", "phase"),
        P("dp", "phase"),
        P("phase", None),
        P("phase", None),
        P("dp", None, None),
        P("dp", None),
        P("dp", None),
        P("dp"),
    )
    out_specs = (P("dp"), P("dp", "phase"), P("dp", "phase"))
    return jax.shard_map(local, mesh=mesh, in_specs=in_specs, out_specs=out_specs, check_vma=False)
```

```python
import jax
import jax.numpy as jnp
from jax import lax
from jax.experimental import pallas as pl
from jax.experimental.pallas import tpu as pltpu
from jax.sharding import PartitionSpec as P

scale20 = 20.0
epsilon = 1e-06
f32 = jnp.float32
bf16 = jnp.bfloat16
NT = (((1,), (1,)), ((), ()))
TN = (((0,), (0,)), ((), ()))
N_PHASE = 4
CHUNKS = 8
DP_ORDER = [45, 29, 43, 61, 34, 33, 31, 40, 26, 62, 22, 2, 11, 28, 54, 4, 10, 35, 52, 46, 30, 7, 14, 27, 63, 55, 41, 42, 58, 18, 60, 32, 15, 5, 16, 20, 56, 8, 13, 25, 37, 17, 48, 51, 57, 38, 1, 12, 49, 24, 6, 23, 36, 50, 21, 19, 9, 39, 59, 3, 0, 53, 47, 44]
DP_PLACE = [60, 46, 11, 59, 15, 33, 50, 21, 37, 56, 16, 12, 47, 38, 22, 32, 34, 41, 29, 55, 35, 54, 10, 51, 49, 39, 8, 23, 13, 1, 20, 6, 31, 5, 4, 17, 52, 40, 45, 57, 7, 26, 27, 2, 63, 0, 19, 62, 42, 48, 53, 43, 18, 61, 14, 25, 36, 44, 28, 58, 30, 3, 9, 24]
cost = pl.CostEstimate(flops=10**9, bytes_accessed=10**5, transcendentals=0)


def dot(a, b, dims=(((1,), (0,)), ((), ()))):
    return lax.dot_general(a, b, dims, preferred_element_type=f32)


def params(mib=16):
    return pltpu.CompilerParams(vmem_limit_bytes=mib * 1024 * 1024)


def call(body, outs, *args):
    return pl.pallas_call(
        body,
        out_shape=[jax.ShapeDtypeStruct(s, t) for s, t in outs],
        compiler_params=params(),
        cost_estimate=cost,
    )(*args)


def iota(shape, dim):
    return lax.broadcasted_iota(jnp.int32, shape, dim)


def split_bf16(x):
    hi = x.astype(bf16)
    return hi, (x - hi.astype(f32)).astype(bf16)


def project_sends(x, w, k, mib, order):
    rows, depth = x.shape
    cols = w.shape[1] // N_PHASE
    n = len(order)

    def body(k_ref, x_ref, w_ref, *refs):
        outs, (x_buf, w_buf, out_buf, sem_ref) = refs[:n], refs[n:]

        def load(i):
            start = pl.multiple_of(lax.rem(k_ref[0] + order[i], N_PHASE) * cols, cols)
            return pltpu.make_async_copy(w_ref.at[:, pl.ds(start, cols)], w_buf.at[i], sem_ref.at[i])

        def store(i):
            return pltpu.make_async_copy(out_buf.at[i], outs[i], sem_ref.at[n + i])

        load_x = pltpu.make_async_copy(x_ref, x_buf, sem_ref.at[2 * n])
        load_x.start()
        for i in range(n):
            load(i).start()
        load_x.wait()
        for i in range(n):
            load(i).wait()
            out_buf[i] = dot(x_buf[...], w_buf[i]).astype(bf16)
            store(i).start()
        for i in range(n):
            store(i).wait()

    hbm = pl.BlockSpec(memory_space=pltpu.HBM)
    return pl.pallas_call(
        body,
        in_specs=[pl.BlockSpec(memory_space=pltpu.SMEM), hbm, hbm],
        out_specs=[hbm] * n,
        out_shape=[jax.ShapeDtypeStruct((rows, cols), bf16)] * n,
        scratch_shapes=[
            pltpu.VMEM((rows, depth), bf16),
            pltpu.VMEM((n, depth, cols), bf16),
            pltpu.VMEM((n, rows, cols), bf16),
            pltpu.SemaphoreType.DMA((2 * n + 1,)),
        ],
        compiler_params=params(mib),
        cost_estimate=cost,
    )(k, x, w)


def project_own(x, w, k):
    rows, depth = x.shape
    cols = w.shape[1] // N_PHASE

    def body(k_ref, x_ref, w_ref, own_ref):
        own_ref[...] = dot(x_ref[...], w_ref[...])

    return pl.pallas_call(
        body,
        grid_spec=pltpu.PrefetchScalarGridSpec(
            num_scalar_prefetch=1,
            grid=(1,),
            in_specs=[
                pl.BlockSpec((rows, depth), lambda s, k_ref: (0, 0)),
                pl.BlockSpec((depth, cols), lambda s, k_ref: (0, k_ref[0])),
            ],
            out_specs=pl.BlockSpec((rows, cols), lambda s, k_ref: (0, 0)),
        ),
        out_shape=jax.ShapeDtypeStruct((rows, cols), f32),
        compiler_params=params(),
        cost_estimate=cost,
    )(k, x, w)


def project_back(u, w, k):
    rows, cols = u.shape
    depth = w.shape[0]

    def columns(w_ref, k_ref, s):
        return w_ref[:, pl.ds(pl.multiple_of(lax.rem(k_ref[0] + s, N_PHASE) * cols, cols), cols)]

    def product(*shifts):
        def body(k_ref, *refs):
            block_refs, w_ref, out_ref = refs[-len(shifts) - 2 : -2], refs[-2], refs[-1]
            total = sum(dot(r[...], columns(w_ref, k_ref, s), NT) for s, r in zip(shifts, block_refs))
            if len(refs) > len(shifts) + 2:
                total = refs[0][...] + total
            out_ref[...] = total.astype(out_ref.dtype)

        return body

    def run(body, dtype, *args):
        vmem = pl.BlockSpec(memory_space=pltpu.VMEM)
        return pl.pallas_call(
            body,
            in_specs=[pl.BlockSpec(memory_space=pltpu.SMEM)] + [vmem] * len(args),
            out_specs=vmem,
            out_shape=jax.ShapeDtypeStruct((rows, depth), dtype),
            compiler_params=params(),
            cost_estimate=cost,
        )(k, *args)

    blocks = gather_blocks(u)
    acc = run(product(0), f32, blocks[0], w)
    acc = run(product(3), f32, acc, blocks[3], w)

    def last(k_ref, acc_ref, a_ref, b_ref, w_ref, out_ref, buf_ref, sem_ref):
        half = depth // 2

        def store(i):
            return pltpu.make_async_copy(buf_ref.at[i], out_ref.at[:, pl.ds(i * half, half)], sem_ref.at[i])

        for i in range(2):
            part = slice(i * half, (i + 1) * half)
            total = acc_ref[:, part]
            for s, block in enumerate((a_ref, b_ref), start=1):
                start = pl.multiple_of(lax.rem(k_ref[0] + s, N_PHASE) * cols, cols)
                total = total + dot(block[...], w_ref[part, pl.ds(start, cols)], NT)
            buf_ref[i] = total.astype(bf16)
            store(i).start()
        for i in range(2):
            store(i).wait()

    return pl.pallas_call(
        last,
        in_specs=[pl.BlockSpec(memory_space=pltpu.SMEM)] + [pl.BlockSpec(memory_space=pltpu.VMEM)] * 4,
        out_specs=pl.BlockSpec(memory_space=pltpu.HBM),
        out_shape=jax.ShapeDtypeStruct((rows, depth), bf16),
        scratch_shapes=[pltpu.VMEM((2, rows, depth // 2), bf16), pltpu.SemaphoreType.DMA((2,))],
        compiler_params=params(),
        cost_estimate=cost,
    )(k, acc, blocks[1], blocks[2], w)


def send(block, s):
    return lax.ppermute(block, "phase", [(i, (i + s) % N_PHASE) for i in range(N_PHASE)])


def gather_blocks(x):
    return [x] + [
        lax.ppermute(x, "phase", [((i + s) % N_PHASE, i) for i in range(N_PHASE)]) for s in range(1, N_PHASE)
    ]


def sum_refs(refs):
    total = refs[0][...].astype(f32)
    for r in refs[1:]:
        total = total + r[...].astype(f32)
    return total


def sum_queries(own, a, b, c, total_ref, low_ref):
    total = sum_refs((own, a, b, c))
    total_ref[...] = total
    low_ref[...] = total.astype(bf16)


def onehot_rows(request_ref, out_ref):
    docs = out_ref.shape[1]
    slots = out_ref.shape[0]
    onehot = (iota((docs, slots), 0) == request_ref[...]).astype(f32).astype(bf16)
    eye = (iota((docs, docs), 0) == iota((docs, docs), 1)).astype(f32).astype(bf16)
    out_ref[...] = dot(onehot, eye, TN).astype(bf16)


def sum_docs(parts, onehot):
    docs, cols = parts[0].shape
    slots = onehot.shape[0]
    block = slots // CHUNKS

    def body(a, b, c, d, onehot_ref, total_ref, rows_ref, buf_ref, sem_ref):
        total = sum_refs((a, b, c, d))
        total_ref[...] = total
        low = total.astype(bf16)

        def store(i):
            part = pl.ds(i * block, block)
            return pltpu.make_async_copy(buf_ref.at[part], rows_ref.at[part], sem_ref.at[i])

        for i in range(CHUNKS):
            part = slice(i * block, (i + 1) * block)
            buf_ref[part, :] = dot(onehot_ref[part, :], low).astype(bf16)
            store(i).start()
        for i in range(CHUNKS):
            store(i).wait()

    vmem = pl.BlockSpec(memory_space=pltpu.VMEM)
    return pl.pallas_call(
        body,
        in_specs=[vmem] * 5,
        out_specs=[vmem, pl.BlockSpec(memory_space=pltpu.HBM)],
        out_shape=[jax.ShapeDtypeStruct((docs, cols), f32), jax.ShapeDtypeStruct((slots, cols), bf16)],
        scratch_shapes=[pltpu.VMEM((slots, cols), bf16), pltpu.SemaphoreType.DMA((CHUNKS,))],
        compiler_params=params(),
        cost_estimate=cost,
    )(*parts, onehot)


def ones_row_sums(x):
    hi, lo = split_bf16(x)
    ones = jnp.ones((8, x.shape[1]), bf16)
    return dot(ones, hi, NT) + dot(ones, lo, NT)


def inner_partials(q_ref, d_ref, out_ref):
    q = q_ref[...]
    d = d_ref[...]
    q2 = jnp.concatenate([q, q], axis=0)
    docs = d.shape[0]
    out_ref[0:docs, :] = dot(d.astype(bf16), q2.astype(bf16), NT)
    out_ref[docs : docs + 8, :] = ones_row_sums(q2 * q2)
    out_ref[docs + 8 : docs + 16, :] = ones_row_sums(d * d)


def hard_partials(rows_ref, q_ref, neg_ref, out_ref):
    rows = rows_ref[...]
    q = q_ref[...]
    wide = rows.astype(f32)
    square = wide * wide
    folded = square[:, 0:128]
    for s in range(128, square.shape[1], 128):
        folded = folded + square[:, s : s + 128]
    hi, lo = split_bf16(folded)
    upper = (iota((128, 128), 1) >= 64).astype(f32).astype(bf16)
    both = dot(rows, jnp.concatenate([q, jnp.zeros_like(q)], axis=0), NT) + dot(hi, upper) + dot(lo, upper)
    slot = iota(both.shape, 0)
    for j in range(8):
        hit = slot == neg_ref[j : j + 1, :]
        out_ref[j : j + 1, :] = jnp.sum(jnp.where(hit, both, 0.0), axis=0, keepdims=True)


def softmax_terms(*refs):
    inner_refs, hard_refs = refs[0:4], refs[4:8]
    small_ref, neg_ref, rows_ref, q_ref, out_ref, coef_ref, grad_ref, row_ref, col_ref, buf_ref, sem_ref = refs[8:]
    sums = sum_refs(inner_refs)
    picks = sum_refs(hard_refs)
    docs, queries = grad_ref.shape[0], q_ref.shape[0]
    swapped = pltpu.roll(picks, 64, 1)
    low_lane = iota(picks.shape, 1) < 64
    scores = jnp.where(low_lane, picks, swapped)
    squares = jnp.where(low_lane, swapped, picks)
    q_scale = lax.rsqrt(sums[docs : docs + 1, :] + epsilon)
    d_scale_row = lax.rsqrt(sums[docs + 8 : docs + 9, :] + epsilon)
    row = iota((docs, 128), 0)
    lane = iota((docs, 128), 1)
    d_scale = jnp.sum(jnp.where(row == lane, d_scale_row, 0.0), axis=1, keepdims=True)
    inner = scale20 * (sums[0:docs, :] * q_scale * d_scale)
    hard_scale = lax.rsqrt(squares + epsilon)
    hard = scale20 * (scores * q_scale * hard_scale)
    valid = small_ref[0:8, :]
    weight = scale20 * small_ref[8:9, :]
    hard_exp = jnp.exp(hard) * valid
    inner_exp = jnp.exp(inner)
    total = jnp.sum(inner_exp, axis=0, keepdims=True) + jnp.sum(hard_exp, axis=0, keepdims=True)
    own = row == lax.bitwise_and(lane, 63)
    positive = jnp.sum(jnp.where(own, inner, 0.0), axis=0, keepdims=True)
    factor = weight / total
    hard_grad = factor * hard_exp
    hard_dot = hard_grad * hard * (1.0 / scale20)
    sent = hard_scale * jnp.where(low_lane, hard_grad, hard_dot * hard_scale)
    slots = out_ref.shape[0]
    slot = iota((slots, 128), 0)
    coef = jnp.zeros((slots, 128), f32)
    for j in range(7):
        coef = coef + jnp.where(slot == neg_ref[j : j + 1, :], sent[j : j + 1, :], 0.0)
    coef = coef.astype(bf16)
    coef_ref[...] = coef

    eye = iota((queries, 128), 0) == iota((queries, 128), 1)
    q_scale_col = jnp.sum(jnp.where(eye, q_scale, 0.0), axis=1, keepdims=True)
    q_low = (q_ref[...] * q_scale_col).astype(bf16)
    q_low = jnp.concatenate([q_low, jnp.zeros_like(q_low)], axis=0)
    second = (iota((128, 128), 0) >= 64).astype(f32).astype(bf16)
    block = slots // CHUNKS

    def store(i):
        part = pl.ds(i * block, block)
        return pltpu.make_async_copy(buf_ref.at[part], out_ref.at[part], sem_ref.at[i])

    for i in range(CHUNKS):
        part = slice(i * block, (i + 1) * block)
        along = dot(coef[part, :], second)
        mixed = dot(coef[part, :], q_low)
        for c in range(0, mixed.shape[1], 128):
            away = along * rows_ref[part, c : c + 128].astype(f32)
            buf_ref[part, c : c + 128] = (mixed[:, c : c + 128] - away).astype(bf16)
        store(i).start()

    grad = (factor * inner_exp - jnp.where(own, weight, 0.0)).astype(bf16)
    grad_ref[...] = grad
    products = grad.astype(f32) * inner * (1.0 / scale20)
    q_dot = jnp.sum(products, axis=0, keepdims=True) + jnp.sum(hard_dot, axis=0, keepdims=True)
    d_dot = jnp.sum(jnp.where(lane < 64, products, 0.0), axis=1, keepdims=True)
    row_ref[...] = jnp.zeros_like(row_ref)
    row_ref[0:1, :] = jnp.log(total) - positive
    row_ref[1:2, :] = q_scale
    row_ref[2:3, :] = q_dot
    col_ref[...] = jnp.where(lane == 0, d_scale, d_dot)
    for i in range(CHUNKS):
        store(i).wait()


def local_grads(coef_ref, grad_ref, row_ref, col_ref, rows_ref, d_ref, q_ref, u_ref, g_ref):
    queries = q_ref.shape[0]
    d_scale = col_ref[:, 0:1]
    d_dot = col_ref[:, 1:2]
    eye = iota((queries, 128), 0) == iota((queries, 128), 1)
    q_scale = jnp.sum(jnp.where(eye, row_ref[1:2, :], 0.0), axis=1, keepdims=True)
    q_dot = jnp.sum(jnp.where(eye, row_ref[2:3, :], 0.0), axis=1, keepdims=True)
    q_unit = q_ref[...] * q_scale
    q_low = q_unit.astype(bf16)
    q_low = jnp.concatenate([q_low, jnp.zeros_like(q_low)], axis=0)
    d_unit = d_ref[...] * d_scale
    grad = grad_ref[...]
    g_query = dot(grad, d_unit.astype(bf16), TN) + dot(coef_ref[...], rows_ref[...], TN)
    u_ref[...] = (q_scale * (g_query[0:queries, :] - q_unit * q_dot)).astype(bf16)
    g_ref[...] = d_scale * (dot(grad, q_low) - d_unit * d_dot)


def doc_grads(rows_ref, request_ref, g_ref, u_ref):
    docs, slots = g_ref.shape[0], rows_ref.shape[0]
    onehot = (iota((docs, slots), 0) == request_ref[...]).astype(f32).astype(bf16)
    u_ref[...] = (g_ref[...] + dot(onehot, rows_ref[...])).astype(bf16)


def local(
    query_states,
    doc_states,
    query_proj,
    doc_proj,
    document_requests,
    slot_valid,
    neg_slot,
    query_weight,
):
    k = lax.axis_index("phase").astype(jnp.int32).reshape(1)
    queries, docs = query_states.shape[0], doc_states.shape[0]
    cols = query_proj.shape[1] // N_PHASE
    n_dp, cap = document_requests.shape[1:]
    slots = n_dp * cap

    negatives = neg_slot.T
    held = jnp.asarray(DP_PLACE, jnp.int32)[negatives // cap] * cap + negatives % cap
    neg_rows = jnp.pad(jnp.concatenate([held, held], axis=1), ((0, 1), (0, 0)), constant_values=-1)
    order = [DP_ORDER]

    def exchange(rows):
        blocks = rows.reshape(n_dp, cap, cols)
        swapped = lax.all_to_all(
            blocks, "dp", split_axis=0, concat_axis=0, tiled=True, axis_index_groups=order
        )
        return swapped.reshape(slots, cols)

    d_far, d_next, d_last, document_requests = lax.optimization_barrier(
        (*project_sends(doc_states, doc_proj, k, 63, (2, 1, 3)), document_requests)
    )
    requests = document_requests[0][jnp.asarray(DP_ORDER, jnp.int32)].reshape(1, slots)
    d_parts = [send(d_far, 2), send(d_next, 1), send(d_last, 3)]
    d_own = project_own(doc_states, doc_proj, k)
    (onehot,) = call(onehot_rows, [((slots, docs), bf16)], requests)
    d_total, outgoing = sum_docs([d_own] + d_parts, onehot)
    outgoing, query_states = lax.optimization_barrier((outgoing, query_states))
    received = exchange(outgoing)

    q_own = project_own(query_states, query_proj, k)
    q_far, q_next, q_last = project_sends(query_states, query_proj, k, 16, (2, 1, 3))
    q_parts = [send(q_far, 2), send(q_next, 1), send(q_last, 3)]
    q_total, q_low = call(sum_queries, [((queries, cols), f32), ((queries, cols), bf16)], q_own, *q_parts)
    (inner,) = call(inner_partials, [((docs + 16, 128), f32)], q_total, d_total)
    inner_all = gather_blocks(inner)
    valid = jnp.take(slot_valid[0], negatives).astype(f32)
    weight = query_weight[None, :]
    small = jnp.pad(
        jnp.concatenate([valid, jnp.zeros_like(weight), weight], axis=0), ((0, 7), (0, 0))
    )
    small = jnp.concatenate([small, small], axis=1)
    received, small, neg_rows = lax.optimization_barrier((received, small, neg_rows))

    (hard,) = call(hard_partials, [((8, 128), f32)], received, q_low, neg_rows)
    hard_all = gather_blocks(hard)
    vmem = pl.BlockSpec(memory_space=pltpu.VMEM)
    rows, coef, grad, by_query, by_doc = pl.pallas_call(
        softmax_terms,
        in_specs=[vmem] * 12,
        out_specs=[pl.BlockSpec(memory_space=pltpu.HBM)] + [vmem] * 4,
        out_shape=[
            jax.ShapeDtypeStruct((slots, cols), bf16),
            jax.ShapeDtypeStruct((slots, 128), bf16),
            jax.ShapeDtypeStruct((docs, 128), bf16),
            jax.ShapeDtypeStruct((8, 128), f32),
            jax.ShapeDtypeStruct((docs, 128), f32),
        ],
        scratch_shapes=[pltpu.VMEM((slots, cols), bf16), pltpu.SemaphoreType.DMA((CHUNKS,))],
        compiler_params=params(),
        cost_estimate=cost,
    )(*inner_all, *hard_all, small, neg_rows, received, q_total)
    arrived = exchange(rows)
    u_query, g_local = call(
        local_grads,
        [((queries, cols), bf16), ((docs, cols), f32)],
        coef,
        grad,
        by_query,
        by_doc,
        received,
        d_total,
        q_total,
    )
    grad_query = project_back(u_query, query_proj, k)
    arrived, grad_query, loss = lax.optimization_barrier((arrived, grad_query, by_query[0, :queries]))

    (u_docs,) = call(doc_grads, [((docs, cols), bf16)], arrived, requests, g_local)
    grad_doc = project_back(u_docs, doc_proj, k)
    return (loss, grad_query, grad_doc)


def solution(mesh):
    in_specs = (
        P("dp", "phase"),
        P("dp", "phase"),
        P("phase", None),
        P("phase", None),
        P("dp", None, None),
        P("dp", None),
        P("dp", None),
        P("dp"),
    )
    out_specs = (P("dp"), P("dp", "phase"), P("dp", "phase"))
    return jax.shard_map(local, mesh=mesh, in_specs=in_specs, out_specs=out_specs, check_vma=False)
```
